128 devices in a mesh: dp: 32 (over y, x, core), ctx: 4 (over z).
Axes of the slice: x: 4, y: 4, z: 4, core: 2. Of those that a mesh axis runs over, the one named last changes fastest.
Arguments:
- conv_input: bfloat16 [32, 1024, 2816], P('dp', 'ctx'), may hold values from -6 to 6
- gate_input: bfloat16 [32, 1024, 2560], P('dp', 'ctx'), may hold values from -6 to 6
- step_input: float32 [32, 40, 1024], P('dp', None, 'ctx'), may hold values from -2.2 to 11.2
- step_bias: float32 [40], replicated, may hold values from -7 to -5
- log_rates: float32 [40], replicated, may hold values from -3 to 3.6
- skip_gain: float32 [40], replicated, may hold values from 0.5 to 1.5
- conv_weight: float32 [4, 2816], replicated, may hold values from -3 to 3
- conv_bias: float32 [2816], replicated, may hold values from -3 to 3
- norm_gain: float32 [2560], replicated, may hold values from 0.5 to 1.5
- doc_ids: int32 [32, 1024], P('dp', 'ctx'), may hold values from 0 to 2, never falling along the last dimension, each value on 1 to 512 neighbouring positions
- cotangent: bfloat16 [32, 1024, 1280], P('dp', 'ctx'), may hold values from -0.03125 to 0.03125
Outputs:
- normed_out: bfloat16 [32, 1024, 2560], P('dp', 'ctx')
- weight_grad: float32 [2560, 1280], P(('dp', 'ctx'))
The draws below stay inside these ranges and needn't reach their ends.
Inputs may be any that keep to these rules, and one draw needn't show every extreme that they name: `doc_ids`: document numbers never fall along a sequence; each sequence holds 3 documents of 1 to 512 positions, one of exactly 512.
All inputs are finite; a program needn't handle non-finite values.
Results may differ from the reference program's by a relative error of at most 0.013.
Values may be sent and summed in bfloat16 or wider, within the bound.
No kernel may reach another device: no remote copies, remote signals or barrier semaphores. Data moves between devices by JAX's collectives and lax.ppermute only.
A program may use at most 64 MiB of HBM per device.

```python
import math
import jax
import jax.numpy as jnp
import numpy as np
from jax import lax

D = 1280
H = 40
P_SIZE = 64
N = 128
KCONV = 4
BLOCK = 256
TOK_DEV = 256
INNER = 2560
C_ALL = 2816
TRACK_SPAN = 1024
TOKENS = 32768
N_DP = 32


def draw_step_input(key, part):
    key = jax.random.fold_in(key, 23)
    rough_seed, shift_seed, spike_seed = jax.random.split(key, 3)
    rough_draws = jnp.clip(0.5 * jax.random.normal(rough_seed, (N_DP, H, TRACK_SPAN), jnp.float32), -1.5, 1.5)
    opening_shifts = jax.random.uniform(shift_seed, (N_DP, H, TRACK_SPAN // TOK_DEV), jnp.float32, -0.7, 0.7)
    opening_shifts = jnp.repeat(opening_shifts, TOK_DEV, axis=2)
    spike_clusters = (jax.random.uniform(spike_seed, (N_DP, 1, TRACK_SPAN), jnp.float32) < 3.0 / TRACK_SPAN).astype(jnp.float32)
    return (rough_draws + opening_shifts + 9.0 * spike_clusters).astype(jnp.float32)


def draw_log_rates(key, part):
    key = jax.random.fold_in(key, 11)
    key_pick, key_fast, key_slow = jax.random.split(key, 3)
    share = 0.5
    slow_pick = jax.random.uniform(key_pick, (H,), jnp.float32) < share
    fast_vals = jax.random.uniform(key_fast, (H,), jnp.float32, 2.8, 3.6)
    slow_vals = jax.random.uniform(key_slow, (H,), jnp.float32, -3.0, -2.3)
    return jnp.where(slow_pick, slow_vals, fast_vals).astype(jnp.float32)


def shard_levels(key, dims, cuts, least, high):
    factor_of, own = 1.0, jax.random.fold_in(key, 6)
    for dim, shards_of in cuts:
        steps = jnp.exp(jax.random.uniform(jax.random.fold_in(own, dim), (shards_of,), jnp.float32, least / len(cuts), high / len(cuts)))
        factor_of = factor_of * jnp.repeat(steps, dims[dim] // shards_of).reshape([-1 if axis == dim else 1 for axis in range(len(dims))])
    return factor_of


def length_profile(amount, total, bound, slope):
    loads = [(1 << 20) // math.isqrt(rank ** slope) + 1 for rank in range(2, amount + 1)]
    rest, given = total - bound - (amount - 1), [1] * (amount - 1)
    while rest > 0:
        free = [i for i in range(amount - 1) if given[i] < bound]
        mass, left = sum([loads[i] for i in free]), rest
        for i in free:
            extra = min(bound - given[i], max(1, left * loads[i] // mass), rest)
            given[i] = given[i] + extra
            rest = rest - extra
    return np.array([bound] + given)


def uneven(rng, number_of, total, bound, slope):
    if number_of == 2:
        one = jax.random.randint(rng, (), max(1, total - bound), min(bound, total - 1) + 1)
        return jnp.stack([one, total - one])
    lengths = jnp.asarray(length_profile(number_of, total, bound, slope), jnp.int32)
    pairs = (number_of - 1) // 2
    donor, taker = lengths[1:1 + 2 * pairs:2], lengths[2:2 + 2 * pairs:2]
    margin = jnp.minimum(donor - 1, bound - taker)
    passed = jax.random.randint(jax.random.fold_in(rng, 1), (pairs,), 0, 1 << 20) % (margin + 1)
    lengths = lengths.at[1:1 + 2 * pairs:2].set(donor - passed).at[2:2 + 2 * pairs:2].set(taker + passed)
    return lengths[jax.random.permutation(jax.random.fold_in(rng, 2), number_of)]


def bell_draw(key, dims, deviation, most, shards=(), kind=jnp.bfloat16):
    entries = deviation * jax.random.normal(key, dims, jnp.float32)
    if shards:
        entries = entries * shard_levels(key, dims, shards, -0.22, 0.18)
    return jnp.clip(entries, -most, most).astype(kind)


def setup_inputs(seed: int = 0) -> dict:
    keys = jax.random.split(jax.random.key(seed), 12)
    conv_input = bell_draw(keys[0], (N_DP, TRACK_SPAN, C_ALL), 1.0, 6.0, ((0, 32), (1, 4)))
    gate_input = bell_draw(keys[1], (N_DP, TRACK_SPAN, INNER), 1.0, 6.0, ((0, 32), (1, 4)))
    step_input = draw_step_input(jax.random.fold_in(keys[11], 71), 0)
    step_bias = jnp.clip(jax.random.uniform(keys[3], (H,), jnp.float32, -7.0, -5.0), -7.0, -5.0)
    log_rates = draw_log_rates(jax.random.fold_in(keys[11], 71), 0)
    skip_gain = jnp.clip(jax.random.uniform(keys[5], (H,), jnp.float32, 0.5, 1.5), 0.5, 1.5)
    conv_weight = bell_draw(keys[6], (KCONV, C_ALL), KCONV ** -0.5, 3.0, (), jnp.float32)
    conv_bias = bell_draw(keys[7], (C_ALL,), 0.5, 3.0, (), jnp.float32)
    norm_gain = jnp.clip(1.0 + 0.1 * jax.random.normal(keys[8], (INNER,), jnp.float32), 0.5, 1.5)
    doc_ids = jax.vmap(lambda own: jnp.searchsorted(jnp.cumsum(uneven(own, 3, TRACK_SPAN, TRACK_SPAN // 2, 0)), jnp.arange(TRACK_SPAN), side="right"))(jax.random.split(keys[9], N_DP)).reshape((N_DP, TRACK_SPAN)).astype(jnp.int32)
    cotangent = bell_draw(keys[10], (N_DP, TRACK_SPAN, D), TOKENS ** -0.5, 0.03125, ((0, 32), (1, 4)))
    return {"conv_input": conv_input, "gate_input": gate_input, "step_input": step_input, "step_bias": step_bias, "log_rates": log_rates, "skip_gain": skip_gain, "conv_weight": conv_weight, "conv_bias": conv_bias, "norm_gain": norm_gain, "doc_ids": doc_ids, "cotangent": cotangent}


def rounded(values):
    return lax.optimization_barrier(values.astype(jnp.bfloat16))

def filter_rows(conv_rows, prev_rows, doc_values, prev_docs, conv_weight, conv_bias):
    tap_count = conv_weight.shape[0]
    joined = jnp.concatenate([prev_rows, conv_rows], 0)
    joined_docs = jnp.concatenate([prev_docs, doc_values], 0)
    length = conv_rows.shape[0]
    summed = jnp.zeros(conv_rows.shape, jnp.float32) + conv_bias[None, :]
    for offset in range(tap_count):
        window = joined[offset:offset + length].astype(jnp.float32)
        same_doc = (joined_docs[offset:offset + length] == doc_values).astype(jnp.float32)
        summed = summed + conv_weight[offset][None, :] * window * same_doc[:, None]
    return summed

def run_blocks(head_values, input_map, output_map, log_decay, step_sizes, doc_list, block_len):
    count_blocks = head_values.shape[0] // block_len
    heads = head_values.shape[1]
    head_size = head_values.shape[2]
    state_size = input_map.shape[1]
    items = (head_values.reshape(count_blocks, block_len, heads, head_size), input_map.reshape(count_blocks, block_len, state_size), output_map.reshape(count_blocks, block_len, state_size), log_decay.reshape(heads, count_blocks, block_len).transpose(1, 0, 2), step_sizes.reshape(heads, count_blocks, block_len).transpose(1, 0, 2), doc_list.reshape(count_blocks, block_len))
    positions = jnp.arange(block_len)
    causal = positions[:, None] >= positions[None, :]

    def one_block(carry, block_items):
        state, last_tag = carry
        vals_block, in_block, out_block, decay_block, step_block, doc_block = block_items
        cumul = jnp.cumsum(decay_block, axis=1)
        same_doc = jnp.logical_and(doc_block[:, None] == doc_block[None, :], causal)[None]
        spread = cumul[:, :, None] - cumul[:, None, :]
        decay_mat = jnp.where(same_doc, jnp.exp(jnp.where(same_doc, spread, 0.0)), 0.0)
        scores = jnp.dot(out_block, in_block.T, preferred_element_type=jnp.float32)
        weights = rounded(scores[None] * decay_mat * step_block[:, None, :])
        inside = jnp.einsum('hts,shp->thp', weights.astype(jnp.float32), vals_block.astype(jnp.float32))
        keep_in = (doc_block == last_tag).astype(jnp.float32)
        reading = jnp.einsum('tn,hpn->thp', out_block.astype(jnp.float32), state, precision=lax.Precision.HIGHEST)
        inter = reading * (jnp.exp(cumul).T * keep_in[:, None])[:, :, None]
        last_doc = doc_block[-1]
        tail_doc = (doc_block == last_doc).astype(jnp.float32)
        factor = step_block * jnp.exp(cumul[:, -1:] - cumul) * tail_doc[None, :]
        scaled = rounded(vals_block.astype(jnp.float32) * factor.T[:, :, None])
        local_state = jnp.einsum('shp,sn->hpn', scaled.astype(jnp.float32), in_block.astype(jnp.float32))
        carry_on = (last_doc == last_tag).astype(jnp.float32)
        new_state = jnp.exp(cumul[:, -1])[:, None, None] * carry_on * state + local_state
        return ((new_state, last_doc), inside + inter)
    start = (jnp.zeros((heads, head_size, state_size), jnp.float32), jnp.array(-1, dtype=jnp.int32))
    (state, last_tag), outputs = lax.scan(one_block, start, items)
    return (outputs.reshape(count_blocks * block_len, heads, head_size), state, last_tag)

def reference(conv_input, gate_input, step_input, step_bias, log_rates, skip_gain, conv_weight, conv_bias, norm_gain, doc_ids, cotangent):
    edge_count = KCONV - 1

    def one_sequence(grad_sum, items):
        conv_rows, gate_rows, step_rows, doc_list, cot_rows = items
        doc_values = doc_list.astype(jnp.float32)
        filtered = filter_rows(conv_rows, jnp.zeros((edge_count, conv_rows.shape[1]), conv_rows.dtype), doc_values, jnp.full((edge_count,), -1.0, jnp.float32), conv_weight, conv_bias)
        activated = rounded(jax.nn.silu(filtered))
        head_values = activated[:, :INNER].reshape(TRACK_SPAN, H, P_SIZE)
        input_map = activated[:, INNER:INNER + N]
        output_map = activated[:, INNER + N:]
        step_sizes = jax.nn.softplus(step_rows + step_bias[:, None])
        log_decay = -jnp.exp(log_rates)[:, None] * step_sizes
        outputs, final_state, final_tag = run_blocks(head_values, input_map, output_map, log_decay, step_sizes, doc_list, BLOCK)
        mixed = outputs + skip_gain[None, :, None] * head_values.astype(jnp.float32)
        mixer_out = rounded(mixed.reshape(TRACK_SPAN, INNER))
        gated = mixer_out.astype(jnp.float32) * jax.nn.silu(gate_rows.astype(jnp.float32))
        normed = (gated * lax.rsqrt(lax.optimization_barrier(jnp.mean(gated * gated, axis=1, keepdims=True)) + 1e-05) * norm_gain[None, :]).astype(jnp.bfloat16)
        grad_sum = grad_sum + jnp.dot(normed.T, cot_rows, preferred_element_type=jnp.float32)
        return (grad_sum, normed)
    weight_grad, normed_out = lax.scan(one_sequence, jnp.zeros((INNER, D), jnp.float32), (conv_input, gate_input, step_input, doc_ids, cotangent))
    return (normed_out, weight_grad)
```

```python
import jax
import jax.numpy as jnp
from jax import lax
from jax.experimental import pallas as pl
from jax.experimental.pallas import tpu as pltpu
from jax.sharding import Mesh
from jax.sharding import PartitionSpec as P

T = 256
H = 40
HD = 64
N = 128
INNER = 2560
C_ALL = 2816
D = 1280
LANES = 128
XCHUNKS = INNER // LANES
MSG = N + 16
F32 = jnp.float32
BF16 = jnp.bfloat16
HIGH = lax.Precision.HIGHEST
VMEM = pltpu.VMEM


def silu(v):
    return 0.5 * v * (1.0 + jnp.tanh(0.5 * v))


def dot(a, b, dims=((1,), (0,)), precision=None):
    return lax.dot_general(a, b, (dims, ((), ())), preferred_element_type=F32, precision=precision)


def split_rows(v):
    hi = v.astype(BF16).astype(F32)
    rest = v - hi
    mid = rest.astype(BF16).astype(F32)
    low = rest - mid
    return jnp.concatenate([hi, mid, low, jnp.zeros((8, v.shape[1]), F32)], 0)


def head_pick(chunk, width):
    rows = lax.broadcasted_iota(jnp.int32, (LANES, width), 0)
    rows = jnp.where(rows >= 2 * H, rows - 2 * H, jnp.where(rows >= H, rows - H, rows))
    real = lax.broadcasted_iota(jnp.int32, (LANES, width), 0) < 3 * H
    lanes = lax.broadcasted_iota(jnp.int32, (LANES, width), 1)
    head = 2 * chunk + jnp.where(lanes >= width // 2, 1, 0)
    return jnp.where(jnp.logical_and(real, rows == head), 1.0, 0.0).astype(BF16)


def front_kernel(conv, halo, step_in, bias, rates, w, cb, doc_row, docb, act, msg, cum_o, step_o, win, dwin, masks, xs, fac):
    step = jax.nn.softplus(step_in[...] + bias[...])
    decay = -jnp.exp(rates[...]) * step
    tri = (
        lax.broadcasted_iota(jnp.int32, (T, T), 0) <= lax.broadcasted_iota(jnp.int32, (T, T), 1)
    ).astype(F32)
    cum = dot(decay, tri, precision=HIGH)
    cum_o[...] = cum
    step_o[...] = step
    docs = doc_row[...]
    tail = (docs == docs[:, T - 1 : T]).astype(F32)
    total = cum[:, T - 1 : T]
    factor = step * jnp.exp(total - cum) * tail
    whole = jnp.broadcast_to(jnp.exp(total), (H, LANES))
    fac[...] = split_rows(jnp.concatenate([factor, whole], 1)).T.astype(BF16)
    dwin[0:8, :] = halo[:, C_ALL:].astype(F32)
    dwin[8:, :] = docb[...].astype(F32)
    own = dwin[8:, :]
    for k in range(3):
        masks[k] = (dwin[5 + k : 5 + k + T, :] == own).astype(F32)
    tag = docb[T - 16 :, :].astype(F32)[15:16, :]

    def conv_chunk(j):
        at = pl.ds(pl.multiple_of(j * LANES, LANES), LANES)
        win[0:8, :] = halo[:, at].astype(F32)
        win[8:, :] = conv[:, at].astype(F32)
        taps = w[:, at]
        total = cb[:, at] + taps[3:4] * win[8:, :]
        for k in range(3):
            total = total + (taps[k : k + 1] * win[5 + k : 5 + k + T, :]) * masks[k]
        out = silu(total).astype(BF16)
        act[:, at] = out
        return at, out

    def value_chunk(j, carry):
        at, out = conv_chunk(j)
        wide = dot(fac[0 : T + 16, :], head_pick(j, LANES))
        xs[:, at] = (out.astype(F32) * wide[0:T]).astype(BF16)
        row = lax.broadcasted_iota(jnp.int32, (16, LANES), 0)
        end = wide[T : T + 16]
        hi = end.astype(BF16).astype(F32)
        info = jnp.where(row == 0, hi, jnp.where(row == 1, end - hi, jnp.where(row == 2, tag, 0.0)))
        msg[N:, at] = info.astype(BF16)
        return carry

    def map_chunk(j, carry):
        conv_chunk(j)
        return carry

    lax.fori_loop(XCHUNKS, XCHUNKS + 2, map_chunk, 0)
    lax.fori_loop(0, XCHUNKS, value_chunk, 0)
    b_t = act[:, INNER : INNER + N].astype(F32).T.astype(BF16)
    for k in range(5):
        at = slice(512 * k, 512 * k + 512)
        msg[0:N, at] = dot(b_t, xs[:, at]).astype(BF16)


def middle_kernel(act, cum, step, doc_row, docb, halo, gate, skip, local, reach, sgate, scores, fac, efac):
    c_map = act[:, INNER + N :]
    b_map = act[:, INNER : INNER + N]
    doc_col = docb[...].astype(F32)
    for s in range(2):
        at = slice(s * LANES, s * LANES + LANES)
        g = dot(c_map, b_map[at], ((1,), (1,)))
        order = lax.broadcasted_iota(jnp.int32, (T, LANES), 0) >= (
            lax.broadcasted_iota(jnp.int32, (T, LANES), 1) + s * LANES
        )
        same = jnp.logical_and(order, doc_col == doc_row[:, at].astype(F32))
        scores[:, at] = jnp.where(same, g, 0.0)
    all_cum = cum[...]
    fac[...] = split_rows(all_cum).T.astype(BF16)
    prev_tag = halo[:, C_ALL : C_ALL + LANES].astype(F32)[7:8, :]
    prev_tag = jnp.concatenate([prev_tag, prev_tag], 1)
    matched = (doc_row[...].astype(F32) == prev_tag).astype(F32)
    efac[...] = split_rows(jnp.exp(all_cum) * matched).T.astype(BF16)
    half = T // 2

    def pair(j, carry):
        at = pl.ds(pl.multiple_of(j * LANES, LANES), LANES)
        vals = act[:, at]
        lanes = lax.broadcasted_iota(jnp.int32, (T, LANES), 1)
        cols = dot(fac[...], head_pick(j, 2 * LANES))
        top = jnp.zeros((half, LANES), F32)
        low = jnp.zeros((half, LANES), F32)
        for k in range(2):
            mine = jnp.where((lanes >= HD) == (k == 1), vals.astype(F32), 0.0).astype(BF16)
            col = cols[:, k * LANES : (k + 1) * LANES]
            row = cum[pl.ds(2 * j + k, 1), :]
            size = step[pl.ds(2 * j + k, 1), :]

            def weights(t, s):
                ts = slice(t * half, t * half + half)
                ss = slice(s * LANES, s * LANES + LANES)
                spread = jnp.minimum(col[ts] - row[:, ss], 0.0)
                return (scores[ts, ss] * jnp.exp(spread) * size[:, ss]).astype(BF16)

            top = top + dot(weights(0, 0), mine[0:half])
            low = low + dot(jnp.concatenate([weights(1, 0), weights(1, 1)], 1), mine)
        gain = skip[:, at]
        local[0:half, at] = top + gain * vals[0:half].astype(F32)
        local[half:, at] = low + gain * vals[half:].astype(F32)
        reach[:, at] = dot(efac[...], head_pick(j, LANES))
        sgate[:, at] = silu(gate[:, at].astype(F32))
        return carry

    lax.fori_loop(0, XCHUNKS, pair, 0)


def back_kernel(local, reach, sgate, act, one, two, gain, normed, parts, gated, squares):
    c_map = act[:, INNER + N :]
    squares[...] = jnp.zeros_like(squares)

    def first(j, carry):
        at = pl.ds(pl.multiple_of(j * LANES, LANES), LANES)
        info = one[N:, at].astype(F32)
        other = two[N:, at].astype(F32)
        linked = (info[2:3] == other[2:3]).astype(F32)
        weight = (info[0:1] + info[1:2]) * linked
        state = one[0:N, at].astype(F32) + weight * two[0:N, at].astype(F32)
        reading = dot(c_map, state.astype(BF16))
        mixed = local[:, at] + reading * reach[:, at]
        value = mixed.astype(BF16).astype(F32) * sgate[:, at]
        gated[:, at] = value
        squares[...] += value * value
        return carry

    lax.fori_loop(0, XCHUNKS, first, 0)
    mean = jnp.sum(squares[...], axis=1, keepdims=True) * (1.0 / INNER)
    squares[...] = jnp.broadcast_to(lax.rsqrt(mean + 1e-05), squares.shape)
    for p in range(4):

        def second(j, carry):
            src = pl.ds(pl.multiple_of((5 * p + j) * LANES, LANES), LANES)
            dst = pl.ds(pl.multiple_of(j * LANES, LANES), LANES)
            value = (gated[:, src] * squares[...] * gain[:, src]).astype(BF16)
            normed[:, src] = value
            parts[p, :, dst] = value
            return carry

        lax.fori_loop(0, 5, second, 0)


def pack_kernel(own, other, out, flat):
    for x in range(4):
        for z in range(4):
            rows = slice(20 * z, 20 * z + 20)
            for k in range(10):
                at = slice(k * LANES, k * LANES + LANES)
                flat[4 * x + z, 20 * k : 20 * k + 20, :] = own[x, rows, at] + other[x, rows, at].astype(F32)
    for i in range(16):
        out[i] = flat[i].astype(BF16)


def sum_kernel(pieces, out, flat):
    total = pieces[0].astype(F32)
    for i in range(1, 16):
        total = total + pieces[i].astype(F32)
    flat[...] = total
    for k in range(10):
        out[:, k * LANES : k * LANES + LANES] = flat[20 * k : 20 * k + 20, :]


def call(kernel, name, out, scratch, limit, flops=0, moved=0, special=0):
    return pl.pallas_call(
        kernel,
        name=name,
        out_shape=out,
        scratch_shapes=scratch,
        compiler_params=pltpu.CompilerParams(vmem_limit_bytes=limit << 20),
        cost_estimate=pl.CostEstimate(flops=flops, bytes_accessed=moved, transcendentals=special),
    )


def shape(dims, kind=F32):
    return jax.ShapeDtypeStruct(dims, kind)


def shifted(value, by):
    return lax.ppermute(value, "z", [(i, i + by) for i in range(4 - by)])


def per_device(conv_input, gate_input, step_input, step_bias, log_rates, skip_gain, conv_weight, conv_bias, norm_gain, doc_ids, cotangent):
    conv = conv_input[0]
    docb = jnp.broadcast_to(doc_ids[0].astype(BF16)[:, None], (T, LANES))
    halo = shifted(jnp.concatenate([conv[T - 8 :], docb[T - 8 :]], 1), 1)
    cots = lax.all_gather(cotangent[0], "y")
    act, msg, cum, step = call(
        front_kernel,
        "front",
        (shape((T, C_ALL), BF16), shape((MSG, INNER), BF16), shape((H, T)), shape((H, T))),
        [
            VMEM((T + 8, LANES), F32),
            VMEM((T + 8, LANES), F32),
            VMEM((3, T, LANES), F32),
            VMEM((T, INNER), BF16),
            VMEM((T + LANES, LANES), BF16),
        ],
        16,
        flops=10**9,
        moved=4 * 10**6,
        special=10**6,
    )(
        conv,
        halo,
        step_input[0],
        step_bias[:, None],
        log_rates[:, None],
        conv_weight,
        conv_bias[None],
        doc_ids,
        docb,
    )
    one = shifted(msg, 1)
    two = shifted(msg, 2)
    local, reach, sgate = call(
        middle_kernel,
        "middle",
        (shape((T, INNER)), shape((T, INNER)), shape((T, INNER))),
        [VMEM((T, T), F32), VMEM((T, LANES), BF16), VMEM((T, LANES), BF16)],
        24,
        flops=2 * 10**9,
        moved=12 * 10**6,
        special=4 * 10**6,
    )(act, cum, step, doc_ids, docb, halo, gate_input[0], jnp.repeat(skip_gain, HD)[None])
    normed, parts = call(
        back_kernel,
        "back",
        (shape((T, INNER), BF16), shape((4, T, INNER // 4), BF16)),
        [VMEM((T, INNER), F32), VMEM((T, LANES), F32)],
        24,
        flops=10**9,
        moved=12 * 10**6,
    )(local, reach, sgate, act, one, two, norm_gain[None])
    rows = lax.all_to_all(parts, "y", 0, 0)
    part = jnp.einsum("ytr,ytd->rd", rows, cots, preferred_element_type=F32)
    part = part.reshape(4, 2, 80, D)
    core = lax.axis_index("c")
    own = jnp.where(core == 0, part[:, 0], part[:, 1])
    send = jnp.where(core == 0, part[:, 1], part[:, 0]).astype(BF16)
    other = lax.ppermute(send, "c", [(0, 1), (1, 0)])
    packed = call(
        pack_kernel, "pack", shape((16, 200, LANES), BF16), [VMEM((16, 200, LANES), F32)], 12, moved=4 * 10**6
    )(own, other)
    pieces = lax.all_to_all(packed, ("x", "z"), 0, 0)
    grad = call(sum_kernel, "total", shape((20, D)), [VMEM((200, LANES), F32)], 8, moved=10**6)(pieces)
    return (normed[None], grad)


def solution(mesh):
    fine = Mesh(mesh.devices.reshape(4, 4, 2, 4), ("y", "x", "c", "z"))
    dp = ("y", "x", "c")
    in_specs = (
        P(dp, "z", None),
        P(dp, "z", None),
        P(dp, None, "z"),
        P(),
        P(),
        P(),
        P(),
        P(),
        P(),
        P(dp, "z"),
        P(dp, "z", None),
    )
    out_specs = (P(dp, "z", None), P(dp + ("z",), None))
    return jax.shard_map(per_device, mesh=fine, in_specs=in_specs, out_specs=out_specs, check_vma=False)
```

```python
import jax
import jax.numpy as jnp
from jax import lax
from jax.experimental import pallas as pl
from jax.experimental.pallas import tpu as pltpu
from jax.sharding import Mesh
from jax.sharding import PartitionSpec as P

T = 256
H = 40
HD = 64
N = 128
INNER = 2560
C_ALL = 2816
D = 1280
LANES = 128
XCHUNKS = INNER // LANES
MSG = N + 16
F32 = jnp.float32
BF16 = jnp.bfloat16
HIGH = lax.Precision.HIGHEST
VMEM = pltpu.VMEM


def silu(v):
    return 0.5 * v * (1.0 + jnp.tanh(0.5 * v))


def dot(a, b, dims=((1,), (0,)), precision=None):
    return lax.dot_general(a, b, (dims, ((), ())), preferred_element_type=F32, precision=precision)


def split_rows(v):
    hi = v.astype(BF16).astype(F32)
    rest = v - hi
    mid = rest.astype(BF16).astype(F32)
    low = rest - mid
    return jnp.concatenate([hi, mid, low, jnp.zeros((8, v.shape[1]), F32)], 0)


def head_pick(chunk, width):
    rows = lax.broadcasted_iota(jnp.int32, (LANES, width), 0)
    rows = jnp.where(rows >= 2 * H, rows - 2 * H, jnp.where(rows >= H, rows - H, rows))
    real = lax.broadcasted_iota(jnp.int32, (LANES, width), 0) < 3 * H
    lanes = lax.broadcasted_iota(jnp.int32, (LANES, width), 1)
    head = 2 * chunk + jnp.where(lanes >= width // 2, 1, 0)
    return jnp.where(jnp.logical_and(real, rows == head), 1.0, 0.0).astype(BF16)


def column(row, width):
    n = row.shape[1]
    diag = lax.broadcasted_iota(jnp.int32, (n, n), 0) == lax.broadcasted_iota(jnp.int32, (n, n), 1)
    diag = jnp.where(diag, jnp.broadcast_to(row, (n, n)), 0.0).astype(BF16)
    return dot(diag, jnp.ones((n, width), BF16))


def upright(row):
    n = row.shape[1]
    diag = lax.broadcasted_iota(jnp.int32, (n, n), 0) == lax.broadcasted_iota(jnp.int32, (n, n), 1)
    return jnp.sum(jnp.where(diag, jnp.broadcast_to(row, (n, n)), 0.0), axis=1, keepdims=True)


def edge_kernel(rows, docs, out):
    out[:, 0:C_ALL] = rows[8:16, :]
    out[:, C_ALL:] = column(docs[...].astype(F32), LANES)[T - 8 :].astype(BF16)


def front_kernel(conv, step_in, bias, rates, w, cb, docs, act, state, info, top, cum_o, step_o, win, dwin, masks, xs, fac):
    step = jax.nn.softplus(step_in[...] + upright(bias[...]))
    decay = -jnp.exp(upright(rates[...])) * step
    tri = (
        lax.broadcasted_iota(jnp.int32, (T, T), 0) <= lax.broadcasted_iota(jnp.int32, (T, T), 1)
    ).astype(F32)
    cum = dot(decay, tri, precision=HIGH)
    cum_o[...] = cum
    step_o[...] = step
    doc_row = docs[...].astype(F32)
    tail = (doc_row == doc_row[:, T - 1 : T]).astype(F32)
    total = cum[:, T - 1 : T]
    factor = step * jnp.exp(total - cum) * tail
    whole = jnp.broadcast_to(jnp.exp(total), (H, LANES))
    fac[...] = split_rows(jnp.concatenate([factor, whole], 1)).T.astype(BF16)
    docb = column(doc_row, LANES)
    dwin[0:8, :] = jnp.zeros((8, LANES), F32)
    dwin[8:, :] = docb
    for k in range(3):
        masks[k] = (dwin[5 + k : 5 + k + T, :] == docb).astype(F32)
    tag = docb[T - 8 :][7:8]
    win[:, 0:8, :] = jnp.zeros((2, 8, LANES), F32)
    xs[0:16, :] = jnp.zeros((16, INNER), BF16)

    def conv_chunk(j, slot):
        at = pl.ds(pl.multiple_of(j * LANES, LANES), LANES)
        win[slot, 8:, :] = conv[:, at].astype(F32)
        taps = w[:, at]
        total = cb[:, at] + taps[3:4] * win[slot, 8:, :]
        for k in range(3):
            total = total + (taps[k : k + 1] * win[slot, 5 + k : 5 + k + T, :]) * masks[k]
        out = silu(total).astype(BF16)
        act[:, at] = out
        return at, out

    def value_chunk(j, slot):
        at, out = conv_chunk(j, slot)
        wide = dot(fac[0 : T + 16, :], head_pick(j, LANES))
        xs[16:, at] = (out[16:].astype(F32) * wide[16:T]).astype(BF16)
        top[:, at] = wide[0:16]
        row = lax.broadcasted_iota(jnp.int32, (16, LANES), 0)
        end = wide[T : T + 16]
        hi = end.astype(BF16).astype(F32)
        rows = jnp.where(row == 0, hi, jnp.where(row == 1, end - hi, jnp.where(row == 2, tag, 0.0)))
        info[:, at] = rows.astype(BF16)

    def value_pair(i, carry):
        for slot in range(2):
            value_chunk(2 * i + slot, slot)
        return carry

    for slot in range(2):
        conv_chunk(XCHUNKS + slot, slot)
    lax.fori_loop(0, XCHUNKS // 2, value_pair, 0)
    b_t = act[:, INNER : INNER + N].astype(F32).T.astype(BF16)
    for k in range(5):
        at = slice(512 * k, 512 * k + 512)
        state[:, at] = dot(b_t, xs[:, at])


def fix_kernel(halo, rows, w, cb, docs, old, state, info, top, act, msg):
    own = column(docs[...].astype(F32), LANES)[0:16]
    joined = jnp.concatenate([halo[:, C_ALL:].astype(F32), own], 0)
    masks = [(joined[5 + k : 21 + k] == own).astype(F32) for k in range(3)]

    def chunk(j):
        at = slice(j * LANES, j * LANES + LANES)
        win = jnp.concatenate([halo[:, at].astype(F32), rows[:, at].astype(F32)], 0)
        total = cb[:, at] + w[3:4, at] * win[8:24]
        for k in range(3):
            total = total + (w[k : k + 1, at] * win[5 + k : 21 + k]) * masks[k]
        out = silu(total).astype(BF16)
        act[:, at] = out
        return at, out

    _, b_rows = chunk(XCHUNKS)
    chunk(XCHUNKS + 1)
    b_t = jnp.concatenate([b_rows.astype(F32), jnp.zeros((LANES - 16, LANES), F32)], 0).T.astype(BF16)
    for j in range(XCHUNKS):
        at, out = chunk(j)
        scaled = (out.astype(F32) * top[:, at]).astype(BF16)
        scaled = jnp.concatenate([scaled, jnp.zeros((LANES - 16, LANES), BF16)], 0)
        msg[0:N, at] = (state[:, at] + dot(b_t, scaled)).astype(BF16)
        msg[N:, at] = info[:, at]


def middle_kernel(act, cum, step, docs, halo, gate, skip, local, reach, sgate, scores, fac, efac):
    doc_row = docs[...].astype(F32)
    c_map = act[:, INNER + N :]
    b_map = act[:, INNER : INNER + N]
    doc_col = column(doc_row, LANES)
    for s in range(2):
        at = slice(s * LANES, s * LANES + LANES)
        g = dot(c_map, b_map[at], ((1,), (1,)))
        order = lax.broadcasted_iota(jnp.int32, (T, LANES), 0) >= (
            lax.broadcasted_iota(jnp.int32, (T, LANES), 1) + s * LANES
        )
        same = jnp.logical_and(order, doc_col == doc_row[:, at])
        scores[:, at] = jnp.where(same, g, 0.0)
    all_cum = cum[...]
    fac[...] = split_rows(all_cum).T.astype(BF16)
    prev_tag = halo[:, C_ALL : C_ALL + LANES].astype(F32)[7:8, :]
    prev_tag = jnp.concatenate([prev_tag, prev_tag], 1)
    matched = (doc_row == prev_tag).astype(F32)
    efac[...] = split_rows(jnp.exp(all_cum) * matched).T.astype(BF16)
    half = T // 2

    def pair(j, carry):
        at = pl.ds(pl.multiple_of(j * LANES, LANES), LANES)
        vals = act[:, at]
        lanes = lax.broadcasted_iota(jnp.int32, (T, LANES), 1)
        cols = dot(fac[...], head_pick(j, 2 * LANES))
        top = jnp.zeros((half, LANES), F32)
        low = jnp.zeros((half, LANES), F32)
        for k in range(2):
            mine = jnp.where((lanes >= HD) == (k == 1), vals.astype(F32), 0.0).astype(BF16)
            col = cols[:, k * LANES : (k + 1) * LANES]
            row = cum[pl.ds(2 * j + k, 1), :]
            size = step[pl.ds(2 * j + k, 1), :]

            def weights(t, s):
                ts = slice(t * half, t * half + half)
                ss = slice(s * LANES, s * LANES + LANES)
                spread = jnp.minimum(col[ts] - row[:, ss], 0.0)
                return (scores[ts, ss] * jnp.exp(spread) * size[:, ss]).astype(BF16)

            top = top + dot(weights(0, 0), mine[0:half])
            low = low + dot(jnp.concatenate([weights(1, 0), weights(1, 1)], 1), mine)
        gain = skip[:, at]
        local[0:half, at] = top + gain * vals[0:half].astype(F32)
        local[half:, at] = low + gain * vals[half:].astype(F32)
        reach[:, at] = dot(efac[...], head_pick(j, LANES))
        sgate[:, at] = silu(gate[:, at].astype(F32))
        return carry

    lax.fori_loop(0, XCHUNKS, pair, 0)


def back_kernel(local, reach, sgate, act, one, two, gain, place, normed, mine, give, gated, squares, turned):
    c_map = act[:, INNER + N :]
    squares[...] = jnp.zeros_like(squares)

    def first(j):
        at = pl.ds(pl.multiple_of(j * LANES, LANES), LANES)
        info = one[N:, at].astype(F32)
        other = two[N:, at].astype(F32)
        linked = (info[2:3] == other[2:3]).astype(F32)
        weight = (info[0:1] + info[1:2]) * linked
        state = one[0:N, at].astype(F32) + weight * two[0:N, at].astype(F32)
        reading = dot(c_map, state.astype(BF16))
        mixed = local[:, at] + reading * reach[:, at]
        value = mixed.astype(BF16).astype(F32) * sgate[:, at]
        gated[:, at] = value
        return value * value

    def first_pair(i, carry):
        squares[...] += first(2 * i) + first(2 * i + 1)
        return carry

    lax.fori_loop(0, XCHUNKS // 2, first_pair, 0)
    mean = jnp.sum(squares[...], axis=1, keepdims=True) * (1.0 / INNER)
    squares[...] = jnp.broadcast_to(lax.rsqrt(mean + 1e-05), squares.shape)
    eye = (
        lax.broadcasted_iota(jnp.int32, (LANES, LANES), 0) == lax.broadcasted_iota(jnp.int32, (LANES, LANES), 1)
    ).astype(BF16)

    def second(i, carry):
        for k in range(2):
            at = pl.ds(pl.multiple_of((2 * i + k) * LANES, LANES), LANES)
            value = (gated[:, at] * squares[...] * gain[:, at]).astype(BF16)
            normed[:, at] = value
            turned[at, :] = dot(eye, value, ((1,), (1,))).astype(BF16)
        return carry

    lax.fori_loop(0, XCHUNKS // 2, second, 0)
    y, x, c = place[0], place[1], place[2]

    def deal(i, carry):
        far_y, far_x = lax.rem(i // 4 - y + 4, 4), lax.rem(lax.rem(i, 4) - x + 4, 4)
        blocks = [turned[pl.ds(pl.multiple_of(160 * i + 80 * k, 16), 80), :] for k in range(2)]

        @pl.when(c == 0)
        def _():
            mine[far_y, far_x] = blocks[0]
            give[far_x, far_y] = blocks[1]

        @pl.when(c == 1)
        def _():
            give[far_y, far_x] = blocks[0]
            mine[far_x, far_y] = blocks[1]

        return carry

    lax.fori_loop(0, 16, deal, 0)


def grad_kernel(mine, got, r1, r2, r3, c0, c1, c2, c3, keep, s1, s2, s3):
    left = [mine[0].reshape(320, T), got[0].reshape(320, T)]
    right = [c0[0], c0[1]]
    for r, c in ((r1, c1), (r2, c2), (r3, c3)):
        for k in range(2):
            left.append(r[k].reshape(320, T))
            right.append(c[k])
    for n in range(5):
        at = slice(256 * n, 256 * n + 256)
        total = dot(left[0], right[0][:, at])
        for k in range(1, 8):
            total = total + dot(left[k], right[k][:, at])
        keep[:, at] = total[0:80]
        for k, out in enumerate((s1, s2, s3)):
            out[:, at] = total[80 * k + 80 : 80 * k + 160].astype(BF16)


def join_kernel(keep, r1, r2, r3, out, total, flat):
    total[...] = keep[...] + r1[...].astype(F32) + r2[...].astype(F32) + r3[...].astype(F32)
    for z in range(4):
        for k in range(10):
            flat[z, 20 * k : 20 * k + 20, :] = total[20 * z : 20 * z + 20, k * LANES : k * LANES + LANES]
        out[z] = flat[z].astype(BF16)


def sum_kernel(pieces, out, flat):
    total = pieces[0].astype(F32)
    for i in range(1, 4):
        total = total + pieces[i].astype(F32)
    flat[...] = total
    for k in range(10):
        out[:, k * LANES : k * LANES + LANES] = flat[20 * k : 20 * k + 20, :]


def call(kernel, name, out, scratch, limit, flops=0, moved=0, special=0, **kw):
    return pl.pallas_call(
        kernel,
        name=name,
        out_shape=out,
        scratch_shapes=scratch,
        compiler_params=pltpu.CompilerParams(vmem_limit_bytes=limit << 20),
        cost_estimate=pl.CostEstimate(flops=flops, bytes_accessed=moved, transcendentals=special),
        **kw,
    )


def shape(dims, kind=F32):
    return jax.ShapeDtypeStruct(dims, kind)


def shifted(value, by):
    return lax.ppermute(value, "z", [(i, i + by) for i in range(4 - by)])


def around(value, by, first_axis):
    pairs = []
    for y in range(4):
        for x in range(4):
            for c in range(2):
                along_y = (c == 0) == (first_axis == "y")
                to_y, to_x = ((y + by) % 4, x) if along_y else (y, (x + by) % 4)
                pairs.append(((y * 4 + x) * 2 + c, (to_y * 4 + to_x) * 2 + c))
    return lax.ppermute(value, ("y", "x", "c"), pairs)


def swapped(value):
    return lax.ppermute(value, "c", [(0, 1), (1, 0)])


def whole(dims):
    return pl.BlockSpec(dims, lambda i: (0,) * len(dims))


def per_device(conv_input, gate_input, step_input, step_bias, log_rates, skip_gain, conv_weight, conv_bias, norm_gain, doc_ids, cotangent):
    conv = conv_input[0]
    halo = call(
        edge_kernel,
        "edge",
        shape((8, C_ALL + LANES), BF16),
        [],
        8,
        moved=10**5,
        grid=(1,),
        in_specs=[pl.BlockSpec((16, C_ALL), lambda i: (T // 16 - 1, 0)), whole((1, T))],
        out_specs=whole((8, C_ALL + LANES)),
    )(conv, doc_ids)
    halo = shifted(halo, 1)
    cots = jnp.stack([cotangent[0], swapped(cotangent[0])])
    place = jnp.stack([lax.axis_index(a) for a in ("y", "x", "c")]).astype(jnp.int32)
    act, state, info, top, cum, step = call(
        front_kernel,
        "front",
        (
            shape((T, C_ALL), BF16),
            shape((N, INNER)),
            shape((16, INNER), BF16),
            shape((16, INNER)),
            shape((H, T)),
            shape((H, T)),
        ),
        [
            VMEM((2, T + 8, LANES), F32),
            VMEM((T + 8, LANES), F32),
            VMEM((3, T, LANES), F32),
            VMEM((T, INNER), BF16),
            VMEM((T + LANES, LANES), BF16),
        ],
        16,
        flops=10**9,
        moved=4 * 10**6,
        special=10**6,
    )(conv, step_input[0], step_bias[None], log_rates[None], conv_weight, conv_bias[None], doc_ids)
    act, msg = call(
        fix_kernel,
        "fix",
        (shape((T, C_ALL), BF16), shape((MSG, INNER), BF16)),
        [],
        8,
        moved=2 * 10**6,
        grid=(1,),
        in_specs=[
            whole((8, C_ALL + LANES)),
            whole((16, C_ALL)),
            whole((4, C_ALL)),
            whole((1, C_ALL)),
            whole((1, T)),
            whole((16, C_ALL)),
            whole((N, INNER)),
            whole((16, INNER)),
            whole((16, INNER)),
        ],
        out_specs=(whole((16, C_ALL)), whole((MSG, INNER))),
        input_output_aliases={5: 0},
    )(halo, conv, conv_weight, conv_bias[None], doc_ids, act, state, info, top)
    one = shifted(msg, 1)
    two = shifted(msg, 2)
    c1, c2, c3 = [around(cots, k, "y") for k in (1, 2, 3)]
    local, reach, sgate = call(
        middle_kernel,
        "middle",
        (shape((T, INNER)), shape((T, INNER)), shape((T, INNER))),
        [VMEM((T, T), F32), VMEM((T, LANES), BF16), VMEM((T, LANES), BF16)],
        24,
        flops=2 * 10**9,
        moved=12 * 10**6,
        special=4 * 10**6,
    )(act, cum, step, doc_ids, halo, gate_input[0], jnp.repeat(skip_gain, HD)[None])
    block = (4, 4, 80, T)
    vmem = pl.BlockSpec(memory_space=VMEM)
    normed, mine, give = call(
        back_kernel,
        "back",
        (shape((T, INNER), BF16), shape(block, BF16), shape(block, BF16)),
        [VMEM((T, INNER), F32), VMEM((T, LANES), F32), VMEM((INNER, T), BF16)],
        24,
        flops=10**9,
        moved=12 * 10**6,
        in_specs=[vmem] * 7 + [pl.BlockSpec(memory_space=pltpu.SMEM)],
    )(local, reach, sgate, act, one, two, norm_gain[None], place)
    got = swapped(give)
    r1, r2, r3 = [around(jnp.stack([mine[k], got[k]]), k, "y") for k in (1, 2, 3)]
    keep, s1, s2, s3 = call(
        grad_kernel,
        "grad",
        (shape((80, D)),) + (shape((80, D), BF16),) * 3,
        [],
        24,
        flops=2 * 10**9,
        moved=8 * 10**6,
    )(mine, got, r1, r2, r3, cots, c1, c2, c3)
    t1, t2, t3 = [around(v, k, "x") for k, v in ((1, s1), (2, s2), (3, s3))]
    packed = call(
        join_kernel,
        "join",
        shape((4, 200, LANES), BF16),
        [VMEM((80, D), F32), VMEM((4, 200, LANES), F32)],
        8,
        moved=10**6,
    )(keep, t1, t2, t3)
    pieces = lax.all_to_all(packed, "z", 0, 0)
    grad = call(sum_kernel, "total", shape((20, D)), [VMEM((200, LANES), F32)], 8, moved=10**6)(pieces)
    return (normed[None], grad)


def solution(mesh):
    fine = Mesh(mesh.devices.reshape(4, 4, 2, 4), ("y", "x", "c", "z"))
    dp = ("y", "x", "c")
    in_specs = (
        P(dp, "z", None),
        P(dp, "z", None),
        P(dp, None, "z"),
        P(),
        P(),
        P(),
        P(),
        P(),
        P(),
        P(dp, "z"),
        P(dp, "z", None),
    )
    out_specs = (P(dp, "z", None), P(dp + ("z",), None))
    return jax.shard_map(per_device, mesh=fine, in_specs=in_specs, out_specs=out_specs, check_vma=False)
```

```python
import jax
import jax.numpy as jnp
from jax import lax
from jax.experimental import pallas as pl
from jax.experimental.pallas import tpu as pltpu
from jax.sharding import Mesh
from jax.sharding import PartitionSpec as P

T = 256
H = 40
HD = 64
N = 128
INNER = 2560
C_ALL = 2816
D = 1280
LANES = 128
XCHUNKS = INNER // LANES
EARLY = 4
MSG = N + 16
F32 = jnp.float32
BF16 = jnp.bfloat16
HIGH = lax.Precision.HIGHEST
VMEM = pltpu.VMEM


def silu(v):
    return 0.5 * v * (1.0 + jnp.tanh(0.5 * v))


def dot(a, b, dims=((1,), (0,)), precision=None):
    return lax.dot_general(a, b, (dims, ((), ())), preferred_element_type=F32, precision=precision)


def split_rows(v):
    hi = v.astype(BF16).astype(F32)
    rest = v - hi
    mid = rest.astype(BF16).astype(F32)
    low = rest - mid
    return jnp.concatenate([hi, mid, low, jnp.zeros((8, v.shape[1]), F32)], 0)


def head_pick(chunk, width):
    rows = lax.broadcasted_iota(jnp.int32, (LANES, width), 0)
    rows = jnp.where(rows >= 2 * H, rows - 2 * H, jnp.where(rows >= H, rows - H, rows))
    real = lax.broadcasted_iota(jnp.int32, (LANES, width), 0) < 3 * H
    lanes = lax.broadcasted_iota(jnp.int32, (LANES, width), 1)
    head = 2 * chunk + jnp.where(lanes >= width // 2, 1, 0)
    return jnp.where(jnp.logical_and(real, rows == head), 1.0, 0.0).astype(BF16)


def column(row, width):
    n = row.shape[1]
    diag = lax.broadcasted_iota(jnp.int32, (n, n), 0) == lax.broadcasted_iota(jnp.int32, (n, n), 1)
    diag = jnp.where(diag, jnp.broadcast_to(row, (n, n)), 0.0).astype(BF16)
    return dot(diag, jnp.ones((n, width), BF16))


def upright(row):
    n = row.shape[1]
    diag = lax.broadcasted_iota(jnp.int32, (n, n), 0) == lax.broadcasted_iota(jnp.int32, (n, n), 1)
    return jnp.sum(jnp.where(diag, jnp.broadcast_to(row, (n, n)), 0.0), axis=1, keepdims=True)


def steps(step_in, bias, rates):
    step = jax.nn.softplus(step_in[...] + upright(bias[...]))
    decay = -jnp.exp(upright(rates[...])) * step
    tri = (
        lax.broadcasted_iota(jnp.int32, (T, T), 0) <= lax.broadcasted_iota(jnp.int32, (T, T), 1)
    ).astype(F32)
    return step, dot(decay, tri, precision=HIGH)


def edge_kernel(conv, docs, out, rows, ids, sems):
    copies = [
        pltpu.make_async_copy(conv.at[pl.ds(T - 16, 16), :], rows, sems.at[0]),
        pltpu.make_async_copy(docs, ids, sems.at[1]),
    ]
    for copy in copies:
        copy.start()
    for copy in copies:
        copy.wait()
    out[:, 0:C_ALL] = rows[8:16, :]
    last = ids[:, LANES:].astype(F32)
    pick = lax.broadcasted_iota(jnp.int32, (8, LANES), 0) + LANES - 8 == lax.broadcasted_iota(jnp.int32, (8, LANES), 1)
    docb = jnp.sum(jnp.where(pick, jnp.broadcast_to(last, (8, LANES)), 0.0), axis=1, keepdims=True)
    out[:, C_ALL:] = jnp.broadcast_to(docb, (8, LANES)).astype(BF16)


def tie_kernel(value, *rest):
    del value, rest


def front_kernel(conv, step_far, bias, rates, w, cb, docs, act, state, info, top, win, dwin, masks, xs, fac, step_in, sem):
    fetch = pltpu.make_async_copy(step_far, step_in, sem)
    fetch.start()
    doc_row = docs[...].astype(F32)
    docb = column(doc_row, LANES)
    dwin[0:8, :] = jnp.zeros((8, LANES), F32)
    dwin[8:, :] = docb
    for k in range(3):
        masks[k] = (dwin[5 + k : 5 + k + T, :] == docb).astype(F32)
    tag = docb[T - 8 :][7:8]
    win[:, 0:8, :] = jnp.zeros((2, 8, LANES), F32)
    xs[0:16, :] = jnp.zeros((16, INNER), BF16)

    def conv_chunk(j, slot):
        at = pl.ds(pl.multiple_of(j * LANES, LANES), LANES)
        win[slot, 8:, :] = conv[:, at].astype(F32)
        taps = w[:, at]
        total = cb[:, at] + taps[3:4] * win[slot, 8:, :]
        for k in range(3):
            total = total + (taps[k : k + 1] * win[slot, 5 + k : 5 + k + T, :]) * masks[k]
        out = silu(total).astype(BF16)
        act[:, at] = out
        return at, out

    for slot in range(2):
        conv_chunk(XCHUNKS + slot, slot)
    fetch.wait()
    step, cum = steps(step_in, bias, rates)
    tail = (doc_row == doc_row[:, T - 1 : T]).astype(F32)
    total = cum[:, T - 1 : T]
    factor = step * jnp.exp(total - cum) * tail
    whole = jnp.broadcast_to(jnp.exp(total), (H, LANES))
    fac[...] = split_rows(jnp.concatenate([factor, whole], 1)).T.astype(BF16)

    def value_chunk(j, slot):
        at, out = conv_chunk(j, slot)
        wide = dot(fac[0 : T + 16, :], head_pick(j, LANES))
        xs[16:, at] = (out[16:].astype(F32) * wide[16:T]).astype(BF16)
        top[:, at] = wide[0:16]
        row = lax.broadcasted_iota(jnp.int32, (16, LANES), 0)
        end = wide[T : T + 16]
        hi = end.astype(BF16).astype(F32)
        rows = jnp.where(row == 0, hi, jnp.where(row == 1, end - hi, jnp.where(row == 2, tag, 0.0)))
        info[:, at] = rows.astype(BF16)

    def value_pair(i, carry):
        for slot in range(2):
            value_chunk(2 * i + slot, slot)
        return carry

    lax.fori_loop(0, XCHUNKS // 2, value_pair, 0)
    b_t = act[:, INNER : INNER + N].astype(F32).T.astype(BF16)
    for k in range(5):
        at = slice(512 * k, 512 * k + 512)
        state[:, at] = dot(b_t, xs[:, at])


def fix_kernel(halo, rows, w, cb, docs, old, state, info, top, act, msg):
    own = column(docs[...].astype(F32), LANES)[0:16]
    joined = jnp.concatenate([halo[:, C_ALL:].astype(F32), own], 0)
    masks = [(joined[5 + k : 21 + k] == own).astype(F32) for k in range(3)]

    def chunk(j):
        at = slice(j * LANES, j * LANES + LANES)
        win = jnp.concatenate([halo[:, at].astype(F32), rows[:, at].astype(F32)], 0)
        total = cb[:, at] + w[3:4, at] * win[8:24]
        for k in range(3):
            total = total + (w[k : k + 1, at] * win[5 + k : 21 + k]) * masks[k]
        out = silu(total).astype(BF16)
        act[:, at] = out
        return at, out

    _, b_rows = chunk(XCHUNKS)
    chunk(XCHUNKS + 1)
    b_t = jnp.concatenate([b_rows.astype(F32), jnp.zeros((LANES - 16, LANES), F32)], 0).T.astype(BF16)
    for j in range(XCHUNKS):
        at, out = chunk(j)
        scaled = (out.astype(F32) * top[:, at]).astype(BF16)
        scaled = jnp.concatenate([scaled, jnp.zeros((LANES - 16, LANES), BF16)], 0)
        msg[0:N, at] = (state[:, at] + dot(b_t, scaled)).astype(BF16)
        msg[N:, at] = info[:, at]


def pair_chunk(j, act, cum, step, scores, fac, skip):
    half = T // 2
    at = pl.ds(pl.multiple_of(j * LANES, LANES), LANES)
    vals = act[:, at]
    lanes = lax.broadcasted_iota(jnp.int32, (T, LANES), 1)
    cols = dot(fac[...], head_pick(j, 2 * LANES))
    top = skip[:, at] * vals[0:half].astype(F32)
    low = skip[:, at] * vals[half:].astype(F32)
    for k in range(2):
        mine = jnp.where((lanes >= HD) == (k == 1), vals.astype(F32), 0.0).astype(BF16)
        col = cols[:, k * LANES : (k + 1) * LANES]
        row = cum[pl.ds(2 * j + k, 1), :]
        size = step[pl.ds(2 * j + k, 1), :]

        def weights(t, s):
            ts = slice(t * half, t * half + half)
            ss = slice(s * LANES, s * LANES + LANES)
            spread = jnp.minimum(col[ts] - row[:, ss], 0.0)
            return (scores[ts, ss] * jnp.exp(spread) * size[:, ss]).astype(BF16)

        top = top + dot(weights(0, 0), mine[0:half])
        low = low + dot(jnp.concatenate([weights(1, 0), weights(1, 1)], 1), mine)
    return jnp.concatenate([top, low], 0)


def early_kernel(act, step_in, bias, rates, docs, halo, skip, local, reach, cum, step, scores, fac, efac):
    step[...], cum[...] = steps(step_in, bias, rates)
    doc_row = docs[...].astype(F32)
    prev_tag = halo[:, C_ALL : C_ALL + LANES].astype(F32)[7:8, :]
    prev_tag = jnp.concatenate([prev_tag, prev_tag], 1)
    matched = (doc_row == prev_tag).astype(F32)
    fac[...] = split_rows(cum[...]).T.astype(BF16)
    efac[...] = split_rows(jnp.exp(cum[...]) * matched).T.astype(BF16)
    c_map = act[:, INNER + N :]
    b_map = act[:, INNER : INNER + N]
    doc_col = column(doc_row, LANES)
    for s in range(2):
        at = slice(s * LANES, s * LANES + LANES)
        g = dot(c_map, b_map[at], ((1,), (1,)))
        order = lax.broadcasted_iota(jnp.int32, (T, LANES), 0) >= (
            lax.broadcasted_iota(jnp.int32, (T, LANES), 1) + s * LANES
        )
        same = jnp.logical_and(order, doc_col == doc_row[:, at])
        scores[:, at] = jnp.where(same, g, 0.0)

    def chunk(j, carry):
        at = pl.ds(pl.multiple_of(j * LANES, LANES), LANES)
        reach[:, at] = dot(efac[...], head_pick(j, LANES))
        return carry

    lax.fori_loop(0, XCHUNKS, chunk, 0)

    def pair(j, carry):
        at = pl.ds(pl.multiple_of(j * LANES, LANES), LANES)
        local[:, at] = pair_chunk(j, act, cum, step, scores, fac, skip)
        return carry

    lax.fori_loop(0, EARLY, pair, 0)


def late_kernel(act, cum, step, scores, fac, gate, skip, local, sgate):
    def pair(j, carry):
        at = pl.ds(pl.multiple_of(j * LANES, LANES), LANES)
        local[:, at] = pair_chunk(j + EARLY, act, cum, step, scores, fac, skip)
        return carry

    lax.fori_loop(0, XCHUNKS - EARLY, pair, 0)

    def gates(j, carry):
        at = pl.ds(pl.multiple_of(j * 2 * LANES, 2 * LANES), 2 * LANES)
        sgate[:, at] = silu(gate[:, at].astype(F32))
        return carry

    lax.fori_loop(0, XCHUNKS // 2, gates, 0)


def back_kernel(early, late, reach, sgate, act, one, two, gain, place, normed, mine, give, gated, squares, turned, flat, sem):
    c_map = act[:, INNER + N :]
    wide = 2 * LANES

    def first(j, local, shift):
        at = pl.ds(pl.multiple_of(j * wide, wide), wide)
        info = one[N:, at].astype(F32)
        other = two[N:, at].astype(F32)
        linked = (info[2:3] == other[2:3]).astype(F32)
        weight = (info[0:1] + info[1:2]) * linked
        state = one[0:N, at].astype(F32) + weight * two[0:N, at].astype(F32)
        reading = dot(c_map, state.astype(BF16))
        here = pl.ds(pl.multiple_of((j - shift) * wide, wide), wide)
        mixed = local[:, here] + reading * reach[:, at]
        value = mixed.astype(BF16).astype(F32) * sgate[:, at]
        gated[:, at] = value
        value = value * value
        return value[:, 0:LANES] + value[:, LANES:]

    def first_pair(i, carry):
        squares[...] += first(2 * i, late, EARLY // 2) + first(2 * i + 1, late, EARLY // 2)
        return carry

    squares[...] = first(0, early, 0) + first(1, early, 0)
    lax.fori_loop(1, 5, first_pair, 0)
    mean = jnp.sum(squares[...], axis=1, keepdims=True) * (1.0 / INNER)
    squares[...] = jnp.broadcast_to(lax.rsqrt(mean + 1e-05), squares.shape)
    eye = (
        lax.broadcasted_iota(jnp.int32, (LANES, LANES), 0) == lax.broadcasted_iota(jnp.int32, (LANES, LANES), 1)
    ).astype(BF16)

    def second(i, carry):
        for k in range(4):
            at = pl.ds(pl.multiple_of((4 * i + k) * LANES, LANES), LANES)
            value = (gated[:, at] * squares[...] * gain[:, at]).astype(BF16)
            flat[:, at] = value
            turned[at, :] = dot(eye, value, ((1,), (1,))).astype(BF16)
        return carry

    lax.fori_loop(0, 5, second, 0)
    out = pltpu.make_async_copy(flat, normed, sem)
    out.start()
    y, x, c = place[0], place[1], place[2]
    far_y = [lax.rem(i - y + 4, 4) for i in range(4)]
    far_x = [lax.rem(i - x + 4, 4) for i in range(4)]

    def deal(zero, other):
        for i in range(4):
            for j in range(4):
                row = 80 * (2 * (4 * i + j))
                zero[far_y[i], far_x[j]] = turned[row : row + 80, :]
                other[far_x[j], far_y[i]] = turned[row + 80 : row + 160, :]

    @pl.when(c == 0)
    def _():
        deal(mine, give)

    @pl.when(c == 1)
    def _():
        deal(give, mine)

    out.wait()


def grad_kernel(mine, got, r1, r2, r3, c0, c1, c2, c3, keep, s1, s2, s3):
    left = [mine[0].reshape(320, T), got[0].reshape(320, T)]
    right = [c0[0], c0[1]]
    for r, c in ((r1, c1), (r2, c2), (r3, c3)):
        for k in range(2):
            left.append(r[k].reshape(320, T))
            right.append(c[k])
    for n in range(5):
        at = slice(256 * n, 256 * n + 256)
        total = dot(left[0], right[0][:, at])
        for k in range(1, 8):
            total = total + dot(left[k], right[k][:, at])
        keep[:, at] = total[0:80]
        for k, out in enumerate((s1, s2, s3)):
            out[:, at] = total[80 * k + 80 : 80 * k + 160].astype(BF16)


def join_kernel(keep, r1, r2, r3, place, own, s1, s2, s3, total, flat):
    total[...] = keep[...] + r1[...].astype(F32) + r2[...].astype(F32) + r3[...].astype(F32)
    for z in range(4):
        for k in range(10):
            flat[z, 20 * k : 20 * k + 20, :] = total[20 * z : 20 * z + 20, k * LANES : k * LANES + LANES]
    z = place[3]
    own[...] = flat[z]
    for k, out in enumerate((s1, s2, s3)):
        out[...] = flat[lax.rem(z + k + 1, 4)].astype(BF16)


def sum_kernel(own, r1, r2, r3, out, flat):
    flat[...] = own[...] + r1[...].astype(F32) + r2[...].astype(F32) + r3[...].astype(F32)
    for k in range(10):
        out[:, k * LANES : k * LANES + LANES] = flat[20 * k : 20 * k + 20, :]


def call(kernel, name, out, scratch, limit, flops=0, moved=0, special=0, **kw):
    return pl.pallas_call(
        kernel,
        name=name,
        out_shape=out,
        scratch_shapes=scratch,
        compiler_params=pltpu.CompilerParams(vmem_limit_bytes=limit << 20),
        cost_estimate=pl.CostEstimate(flops=flops, bytes_accessed=moved, transcendentals=special),
        **kw,
    )


def shape(dims, kind=F32):
    return jax.ShapeDtypeStruct(dims, kind)


def shifted(value, by):
    return lax.ppermute(value, "z", [(i, i + by) for i in range(4 - by)])


def around(value, by, first_axis):
    pairs = []
    for y in range(4):
        for x in range(4):
            for c in range(2):
                along_y = (c == 0) == (first_axis == "y")
                to_y, to_x = ((y + by) % 4, x) if along_y else (y, (x + by) % 4)
                pairs.append(((y * 4 + x) * 2 + c, (to_y * 4 + to_x) * 2 + c))
    return lax.ppermute(value, ("y", "x", "c"), pairs)


def swapped(value):
    return lax.ppermute(value, "c", [(0, 1), (1, 0)])


def tied(value, *others):
    anywhere = pl.BlockSpec(memory_space=pl.ANY)
    return call(
        tie_kernel,
        "tie",
        shape(value.shape, value.dtype),
        [],
        4,
        in_specs=[anywhere] * (1 + len(others)),
        out_specs=anywhere,
        input_output_aliases={0: 0},
    )(value, *others)


def whole(dims):
    return pl.BlockSpec(dims, lambda i: (0,) * len(dims))


def per_device(conv_input, gate_input, step_input, step_bias, log_rates, skip_gain, conv_weight, conv_bias, norm_gain, doc_ids, cotangent):
    conv = conv_input[0]
    vmem = pl.BlockSpec(memory_space=VMEM)
    halo = call(
        edge_kernel,
        "edge",
        shape((8, C_ALL + LANES), BF16),
        [VMEM((16, C_ALL), BF16), VMEM((1, T), jnp.int32), pltpu.SemaphoreType.DMA((2,))],
        62,
        moved=10**5,
        in_specs=[pl.BlockSpec(memory_space=pltpu.HBM)] * 2,
    )(conv, doc_ids)
    halo = shifted(halo, 1)
    cot_other = swapped(cotangent[0])
    place = jnp.stack([lax.axis_index(a) for a in ("y", "x", "c", "z")]).astype(jnp.int32)
    act, state, info, top = call(
        front_kernel,
        "front",
        (
            shape((T, C_ALL), BF16),
            shape((N, INNER)),
            shape((16, INNER), BF16),
            shape((16, INNER)),
        ),
        [
            VMEM((2, T + 8, LANES), F32),
            VMEM((T + 8, LANES), F32),
            VMEM((3, T, LANES), F32),
            VMEM((T, INNER), BF16),
            VMEM((T + LANES, LANES), BF16),
            VMEM((H, T), F32),
            pltpu.SemaphoreType.DMA,
        ],
        16,
        flops=10**9,
        moved=4 * 10**6,
        special=10**6,
        in_specs=[vmem, pl.BlockSpec(memory_space=pltpu.HBM)] + [vmem] * 5,
    )(conv, step_input[0], step_bias[None], log_rates[None], conv_weight, conv_bias[None], doc_ids)
    act, msg = call(
        fix_kernel,
        "fix",
        (shape((T, C_ALL), BF16), shape((MSG, INNER), BF16)),
        [],
        8,
        moved=2 * 10**6,
        grid=(1,),
        in_specs=[
            whole((8, C_ALL + LANES)),
            whole((16, C_ALL)),
            whole((4, C_ALL)),
            whole((1, C_ALL)),
            whole((1, T)),
            whole((16, C_ALL)),
            whole((N, INNER)),
            whole((16, INNER)),
            whole((16, INNER)),
        ],
        out_specs=(whole((16, C_ALL)), whole((MSG, INNER))),
        input_output_aliases={5: 0},
    )(halo, conv, conv_weight, conv_bias[None], doc_ids, act, state, info, top)
    one = shifted(msg, 1)
    two = shifted(msg, 2)
    skip = jnp.repeat(skip_gain, HD)[None]
    early, reach, cum, step, scores, fac = call(
        early_kernel,
        "early",
        (
            shape((T, EARLY * LANES)),
            shape((T, INNER)),
            shape((H, T)),
            shape((H, T)),
            shape((T, T)),
            shape((T, LANES), BF16),
        ),
        [VMEM((T, LANES), BF16)],
        16,
    )(act, step_input[0], step_bias[None], log_rates[None], doc_ids, halo, skip)
    cots = jnp.stack([cotangent[0], tied(cot_other, fac)])
    c1, c2, c3 = [around(cots, k, "y") for k in (1, 2, 3)]
    late, sgate = call(
        late_kernel, "late", (shape((T, INNER - EARLY * LANES)), shape((T, INNER))), [], 24
    )(act, cum, step, scores, fac, gate_input[0], skip)
    block = (4, 4, 80, T)
    normed, mine, give = call(
        back_kernel,
        "back",
        (shape((T, INNER), BF16), shape(block, BF16), shape(block, BF16)),
        [
            VMEM((T, INNER), F32),
            VMEM((T, LANES), F32),
            VMEM((INNER, T), BF16),
            VMEM((T, INNER), BF16),
            pltpu.SemaphoreType.DMA,
        ],
        24,
        in_specs=[vmem] * 8 + [pl.BlockSpec(memory_space=pltpu.SMEM)],
        out_specs=(pl.BlockSpec(memory_space=pltpu.HBM), vmem, vmem),
    )(early, late, reach, sgate, act, one, two, norm_gain[None], place)
    got = tied(swapped(give), c1, c2, c3)
    r1, r2, r3 = [around(jnp.stack([mine[k], got[k]]), k, "y") for k in (1, 2, 3)]
    keep, s1, s2, s3 = call(
        grad_kernel,
        "grad",
        (shape((80, D)),) + (shape((80, D), BF16),) * 3,
        [],
        24,
        flops=2 * 10**9,
        moved=8 * 10**6,
    )(mine, got, r1, r2, r3, cots, c1, c2, c3)
    t1, t2, t3 = [around(v, k, "x") for k, v in ((1, s1), (2, s2), (3, s3))]
    small = (200, LANES)
    own, s1, s2, s3 = call(
        join_kernel,
        "join",
        (shape(small),) + (shape(small, BF16),) * 3,
        [VMEM((80, D), F32), VMEM((4,) + small, F32)],
        8,
        moved=10**6,
        in_specs=[vmem] * 4 + [pl.BlockSpec(memory_space=pltpu.SMEM)],
    )(keep, t1, t2, t3, place)
    u1, u2, u3 = [lax.ppermute(v, "z", [(i, (i + k) % 4) for i in range(4)]) for k, v in ((1, s1), (2, s2), (3, s3))]
    grad = call(sum_kernel, "total", shape((20, D)), [VMEM(small, F32)], 8, moved=10**6)(own, u1, u2, u3)
    return (normed[None], grad)


def solution(mesh):
    fine = Mesh(mesh.devices.reshape(4, 4, 2, 4), ("y", "x", "c", "z"))
    dp = ("y", "x", "c")
    in_specs = (
        P(dp, "z", None),
        P(dp, "z", None),
        P(dp, None, "z"),
        P(),
        P(),
        P(),
        P(),
        P(),
        P(),
        P(dp, "z"),
        P(dp, "z", None),
    )
    out_specs = (P(dp, "z", None), P(dp + ("z",), None))
    return jax.shard_map(per_device, mesh=fine, in_specs=in_specs, out_specs=out_specs, check_vma=False)
```

```python
import jax
import jax.numpy as jnp
from jax import lax
from jax.experimental import pallas as pl
from jax.experimental.pallas import tpu as pltpu
from jax.sharding import Mesh
from jax.sharding import PartitionSpec as P

T = 256
H = 40
HD = 64
N = 128
INNER = 2560
C_ALL = 2816
D = 1280
LANES = 128
XCHUNKS = INNER // LANES
EARLY = 4
MSG = N + 16
F32 = jnp.float32
BF16 = jnp.bfloat16
HIGH = lax.Precision.HIGHEST
VMEM = pltpu.VMEM


def silu(v):
    return 0.5 * v * (1.0 + jnp.tanh(0.5 * v))


def dot(a, b, dims=((1,), (0,)), precision=None):
    return lax.dot_general(a, b, (dims, ((), ())), preferred_element_type=F32, precision=precision)


def split_rows(v):
    hi = v.astype(BF16).astype(F32)
    rest = v - hi
    mid = rest.astype(BF16).astype(F32)
    low = rest - mid
    return jnp.concatenate([hi, mid, low, jnp.zeros((8, v.shape[1]), F32)], 0)


def head_pick(chunk, width):
    rows = lax.broadcasted_iota(jnp.int32, (LANES, width), 0)
    rows = jnp.where(rows >= 2 * H, rows - 2 * H, jnp.where(rows >= H, rows - H, rows))
    real = lax.broadcasted_iota(jnp.int32, (LANES, width), 0) < 3 * H
    lanes = lax.broadcasted_iota(jnp.int32, (LANES, width), 1)
    head = 2 * chunk + jnp.where(lanes >= width // 2, 1, 0)
    return jnp.where(jnp.logical_and(real, rows == head), 1.0, 0.0).astype(BF16)


def column(row, width):
    n = row.shape[1]
    diag = lax.broadcasted_iota(jnp.int32, (n, n), 0) == lax.broadcasted_iota(jnp.int32, (n, n), 1)
    diag = jnp.where(diag, jnp.broadcast_to(row, (n, n)), 0.0).astype(BF16)
    return dot(diag, jnp.ones((n, width), BF16))


def upright(row):
    n = row.shape[1]
    diag = lax.broadcasted_iota(jnp.int32, (n, n), 0) == lax.broadcasted_iota(jnp.int32, (n, n), 1)
    return jnp.sum(jnp.where(diag, jnp.broadcast_to(row, (n, n)), 0.0), axis=1, keepdims=True)


def steps(step_in, bias, rates):
    step = jax.nn.softplus(step_in[...] + upright(bias[...]))
    decay = -jnp.exp(upright(rates[...])) * step
    tri = (
        lax.broadcasted_iota(jnp.int32, (T, T), 0) <= lax.broadcasted_iota(jnp.int32, (T, T), 1)
    ).astype(F32)
    return step, dot(decay, tri, precision=HIGH)


def edge_kernel(conv, docs, out, rows, ids, sems):
    copies = [
        pltpu.make_async_copy(conv.at[pl.ds(T - 16, 16), :], rows, sems.at[0]),
        pltpu.make_async_copy(docs, ids, sems.at[1]),
    ]
    for copy in copies:
        copy.start()
    for copy in copies:
        copy.wait()
    out[:, 0:C_ALL] = rows[8:16, :]
    last = ids[:, LANES:].astype(F32)
    pick = lax.broadcasted_iota(jnp.int32, (8, LANES), 0) + LANES - 8 == lax.broadcasted_iota(jnp.int32, (8, LANES), 1)
    docb = jnp.sum(jnp.where(pick, jnp.broadcast_to(last, (8, LANES)), 0.0), axis=1, keepdims=True)
    out[:, C_ALL:] = jnp.broadcast_to(docb, (8, LANES)).astype(BF16)


def front_kernel(conv, step_in, bias, rates, w, cb, docs, act, state, info, top, win, dwin, masks, xs, fac):
    doc_row = docs[...].astype(F32)
    docb = column(doc_row, LANES)
    dwin[0:8, :] = jnp.zeros((8, LANES), F32)
    dwin[8:, :] = docb
    for k in range(3):
        masks[k] = (dwin[5 + k : 5 + k + T, :] == docb).astype(F32)
    tag = docb[T - 8 :][7:8]
    win[:, 0:8, :] = jnp.zeros((2, 8, LANES), F32)
    xs[0:16, :] = jnp.zeros((16, INNER), BF16)

    def conv_chunk(j, slot):
        at = pl.ds(pl.multiple_of(j * LANES, LANES), LANES)
        win[slot, 8:, :] = conv[:, at].astype(F32)
        taps = w[:, at]
        total = cb[at].reshape(1, LANES) + taps[3:4] * win[slot, 8:, :]
        for k in range(3):
            total = total + (taps[k : k + 1] * win[slot, 5 + k : 5 + k + T, :]) * masks[k]
        out = silu(total).astype(BF16)
        act[:, at] = out
        return at, out

    for slot in range(2):
        conv_chunk(XCHUNKS + slot, slot)
    step, cum = steps(step_in, bias, rates)
    tail = (doc_row == doc_row[:, T - 1 : T]).astype(F32)
    total = cum[:, T - 1 : T]
    factor = step * jnp.exp(total - cum) * tail
    whole = jnp.broadcast_to(jnp.exp(total), (H, LANES))
    fac[...] = split_rows(jnp.concatenate([factor, whole], 1)).T.astype(BF16)

    def value_chunk(j, slot):
        at, out = conv_chunk(j, slot)
        wide = dot(fac[0 : T + 16, :], head_pick(j, LANES))
        xs[16:, at] = (out[16:].astype(F32) * wide[16:T]).astype(BF16)
        top[:, at] = wide[0:16]
        row = lax.broadcasted_iota(jnp.int32, (16, LANES), 0)
        end = wide[T : T + 16]
        hi = end.astype(BF16).astype(F32)
        rows = jnp.where(row == 0, hi, jnp.where(row == 1, end - hi, jnp.where(row == 2, tag, 0.0)))
        info[:, at] = rows.astype(BF16)

    def value_pair(i, carry):
        for slot in range(2):
            value_chunk(2 * i + slot, slot)
        return carry

    lax.fori_loop(0, XCHUNKS // 2, value_pair, 0)
    b_t = act[:, INNER : INNER + N].astype(F32).T.astype(BF16)
    for k in range(5):
        at = slice(512 * k, 512 * k + 512)
        state[:, at] = dot(b_t, xs[:, at])


def fix_kernel(halo, rows, w, cb, docs, old, state, info, top, act, msg):
    own = column(docs[...].astype(F32), LANES)[0:16]
    joined = jnp.concatenate([halo[:, C_ALL:].astype(F32), own], 0)
    masks = [(joined[5 + k : 21 + k] == own).astype(F32) for k in range(3)]

    def chunk(j):
        at = slice(j * LANES, j * LANES + LANES)
        win = jnp.concatenate([halo[:, at].astype(F32), rows[:, at].astype(F32)], 0)
        total = cb[at].reshape(1, LANES) + w[3:4, at] * win[8:24]
        for k in range(3):
            total = total + (w[k : k + 1, at] * win[5 + k : 21 + k]) * masks[k]
        out = silu(total).astype(BF16)
        act[:, at] = out
        return at, out

    _, b_rows = chunk(XCHUNKS)
    chunk(XCHUNKS + 1)
    b_t = jnp.concatenate([b_rows.astype(F32), jnp.zeros((LANES - 16, LANES), F32)], 0).T.astype(BF16)
    for j in range(XCHUNKS):
        at, out = chunk(j)
        scaled = (out.astype(F32) * top[:, at]).astype(BF16)
        scaled = jnp.concatenate([scaled, jnp.zeros((LANES - 16, LANES), BF16)], 0)
        value = (state[:, at] + dot(b_t, scaled)).astype(BF16)
        msg[0:N, at] = value
        msg[N:, at] = info[:, at]


def pair_chunk(j, act, cum, step, scores, fac, sfac):
    half = T // 2
    at = pl.ds(pl.multiple_of(j * LANES, LANES), LANES)
    vals = act[:, at]
    lanes = lax.broadcasted_iota(jnp.int32, (T, LANES), 1)
    cols = dot(fac[...], head_pick(j, 2 * LANES))
    skip = dot(sfac[...], head_pick(j, LANES))[0:1]
    top = skip * vals[0:half].astype(F32)
    low = skip * vals[half:].astype(F32)
    for k in range(2):
        mine = jnp.where((lanes >= HD) == (k == 1), vals.astype(F32), 0.0).astype(BF16)
        col = cols[:, k * LANES : (k + 1) * LANES]
        row = cum[pl.ds(2 * j + k, 1), :]
        size = step[pl.ds(2 * j + k, 1), :]

        def weights(t, s):
            ts = slice(t * half, t * half + half)
            ss = slice(s * LANES, s * LANES + LANES)
            spread = jnp.minimum(col[ts] - row[:, ss], 0.0)
            return (scores[ts, ss] * jnp.exp(spread) * size[:, ss]).astype(BF16)

        top = top + dot(weights(0, 0), mine[0:half])
        low = low + dot(jnp.concatenate([weights(1, 0), weights(1, 1)], 1), mine)
    return jnp.concatenate([top, low], 0)


def early_kernel(act, step_in, bias, rates, docs, halo, skip, cot, other, local, reach, cum, step, scores, fac, cots, sfac, efac):
    cots[0] = cot[...]
    cots[1] = other[...]
    sfac[...] = split_rows(jnp.broadcast_to(upright(skip[...]), (H, LANES))).T[0:16].astype(BF16)
    step[...], cum[...] = steps(step_in, bias, rates)
    doc_row = docs[...].astype(F32)
    prev_tag = halo[:, C_ALL : C_ALL + LANES].astype(F32)[7:8, :]
    prev_tag = jnp.concatenate([prev_tag, prev_tag], 1)
    matched = (doc_row == prev_tag).astype(F32)
    fac[...] = split_rows(cum[...]).T.astype(BF16)
    efac[...] = split_rows(jnp.exp(cum[...]) * matched).T.astype(BF16)
    c_map = act[:, INNER + N :]
    b_map = act[:, INNER : INNER + N]
    doc_col = column(doc_row, LANES)
    for s in range(2):
        at = slice(s * LANES, s * LANES + LANES)
        g = dot(c_map, b_map[at], ((1,), (1,)))
        order = lax.broadcasted_iota(jnp.int32, (T, LANES), 0) >= (
            lax.broadcasted_iota(jnp.int32, (T, LANES), 1) + s * LANES
        )
        same = jnp.logical_and(order, doc_col == doc_row[:, at])
        scores[:, at] = jnp.where(same, g, 0.0)

    def chunk(j, carry):
        at = pl.ds(pl.multiple_of(j * LANES, LANES), LANES)
        reach[:, at] = dot(efac[...], head_pick(j, LANES))
        return carry

    lax.fori_loop(0, XCHUNKS, chunk, 0)

    def pair(j, carry):
        at = pl.ds(pl.multiple_of(j * LANES, LANES), LANES)
        local[:, at] = pair_chunk(j, act, cum, step, scores, fac, sfac)
        return carry

    lax.fori_loop(0, EARLY, pair, 0)


def late_kernel(act, cum, step, scores, fac, gate, sfac, local, sgate):
    def pair(j, carry):
        at = pl.ds(pl.multiple_of(j * LANES, LANES), LANES)
        local[:, at] = pair_chunk(j + EARLY, act, cum, step, scores, fac, sfac)
        return carry

    lax.fori_loop(0, XCHUNKS - EARLY, pair, 0)

    def gates(j, carry):
        at = pl.ds(pl.multiple_of(j * 2 * LANES, 2 * LANES), 2 * LANES)
        sgate[:, at] = silu(gate[:, at].astype(F32))
        return carry

    lax.fori_loop(0, XCHUNKS // 2, gates, 0)


def back_kernel(early, late, reach, sgate, act, one, two, gain, normed, mine, give, gated, squares, turned, flat, sem):
    c_map = act[:, INNER + N :]
    wide = 2 * LANES

    def first(j, local, shift):
        at = pl.ds(pl.multiple_of(j * wide, wide), wide)
        info = one[N:, at].astype(F32)
        other = two[N:, at].astype(F32)
        linked = (info[2:3] == other[2:3]).astype(F32)
        weight = (info[0:1] + info[1:2]) * linked
        state = one[0:N, at].astype(F32) + weight * two[0:N, at].astype(F32)
        reading = dot(c_map, state.astype(BF16))
        here = pl.ds(pl.multiple_of((j - shift) * wide, wide), wide)
        mixed = local[:, here] + reading * reach[:, at]
        value = mixed.astype(BF16).astype(F32) * sgate[:, at]
        gated[:, at] = value
        value = value * value
        return value[:, 0:LANES] + value[:, LANES:]

    def first_pair(i, carry):
        squares[...] += first(2 * i, late, EARLY // 2) + first(2 * i + 1, late, EARLY // 2)
        return carry

    squares[...] = first(0, early, 0) + first(1, early, 0)
    lax.fori_loop(1, 5, first_pair, 0)
    mean = jnp.sum(squares[...], axis=1, keepdims=True) * (1.0 / INNER)
    squares[...] = jnp.broadcast_to(lax.rsqrt(mean + 1e-05), squares.shape)
    eye = (
        lax.broadcasted_iota(jnp.int32, (LANES, LANES), 0) == lax.broadcasted_iota(jnp.int32, (LANES, LANES), 1)
    ).astype(BF16)

    def second(i, carry):
        for k in range(4):
            at = pl.ds(pl.multiple_of((4 * i + k) * LANES, LANES), LANES)
            value = (gated[:, at] * squares[...] * gain[at].reshape(1, LANES)).astype(BF16)
            flat[:, at] = value
            turned[at, :] = dot(eye, value, ((1,), (1,))).astype(BF16)
        return carry

    lax.fori_loop(0, 5, second, 0)
    out = pltpu.make_async_copy(flat, normed, sem)
    out.start()
    y, x, c = [lax.axis_index(a) for a in ("y", "x", "c")]
    far_y = [lax.rem(i - y + 4, 4) for i in range(4)]
    far_x = [lax.rem(i - x + 4, 4) for i in range(4)]

    def deal(zero, other):
        for i in range(4):
            for j in range(4):
                row = 80 * (2 * (4 * i + j))
                zero[far_y[i], j] = turned[row : row + 80, :]
                other[far_x[j], i] = turned[row + 80 : row + 160, :]

    @pl.when(c == 0)
    def _():
        deal(mine, give)

    @pl.when(c == 1)
    def _():
        deal(give, mine)

    out.wait()


def load_kernel(mine, got, c1, c2, c3, *outs):
    del c1, c2, c3
    for k, out in enumerate(outs):
        out[0] = mine[k + 1]
        out[1] = got[k + 1]


def grad_kernel(mine, got, r1, r2, r3, c0, c1, c2, c3, out, flat):
    left = [mine[0].reshape(320, T), got[0].reshape(320, T)]
    right = [c0[0], c0[1]]
    for r, c in ((r1, c1), (r2, c2), (r3, c3)):
        for k in range(2):
            left.append(r[k].reshape(320, T))
            right.append(c[k])
    for n in range(5):
        at = slice(256 * n, 256 * n + 256)
        total = dot(left[0], right[0][:, at])
        for k in range(1, 8):
            total = total + dot(left[k], right[k][:, at])
        for k in range(2):
            row = 20 * (2 * n + k)
            for i in range(16):
                flat[i, row : row + 20, :] = total[20 * i : 20 * i + 20, k * LANES : k * LANES + LANES]
    for i in range(16):
        out[i] = flat[i].astype(BF16)


def sum_kernel(pieces, out, flat):
    total = pieces[0].astype(F32)
    for i in range(1, 16):
        total = total + pieces[i].astype(F32)
    flat[...] = total
    for k in range(10):
        out[:, k * LANES : k * LANES + LANES] = flat[20 * k : 20 * k + 20, :]


def call(kernel, name, out, scratch, limit, flops=0, moved=0, special=0, **kw):
    return pl.pallas_call(
        kernel,
        name=name,
        out_shape=out,
        scratch_shapes=scratch,
        compiler_params=pltpu.CompilerParams(vmem_limit_bytes=limit << 20),
        cost_estimate=pl.CostEstimate(flops=flops, bytes_accessed=moved, transcendentals=special),
        **kw,
    )


def shape(dims, kind=F32):
    return jax.ShapeDtypeStruct(dims, kind)


def shifted(value, by):
    return lax.ppermute(value, "z", [(i, i + by) for i in range(4 - by)])


def around(value, by, first_axis):
    pairs = []
    for y in range(4):
        for x in range(4):
            for c in range(2):
                along_y = (c == 0) == (first_axis == "y")
                to_y, to_x = ((y + by) % 4, x) if along_y else (y, (x + by) % 4)
                pairs.append(((y * 4 + x) * 2 + c, (to_y * 4 + to_x) * 2 + c))
    return lax.ppermute(value, ("y", "x", "c"), pairs)


def place_of(y, x, c, z):
    return ((y * 4 + x) * 2 + c) * 4 + z


PLANES = [[place_of(y, k, 0, z) for k in range(4) for z in range(4)] for y in range(4)] + [
    [place_of(k, x, 1, z) for k in range(4) for z in range(4)] for x in range(4)
]


def swapped(value):
    return lax.ppermute(value, "c", [(0, 1), (1, 0)])


def whole(dims):
    return pl.BlockSpec(dims, lambda i: (0,) * len(dims))


def per_device(conv_input, gate_input, step_input, step_bias, log_rates, skip_gain, conv_weight, conv_bias, norm_gain, doc_ids, cotangent):
    conv = conv_input[0]
    vmem = pl.BlockSpec(memory_space=VMEM)
    anywhere = pl.BlockSpec(memory_space=pl.ANY)
    halo = call(
        edge_kernel,
        "edge",
        shape((8, C_ALL + LANES), BF16),
        [VMEM((16, C_ALL), BF16), VMEM((1, T), jnp.int32), pltpu.SemaphoreType.DMA((2,))],
        63,
        moved=10**5,
        in_specs=[anywhere] * 2,
    )(conv, doc_ids)
    halo = shifted(halo, 1)
    step_in, bias, rates = step_input[0], step_bias[None], log_rates[None]
    cot_other = swapped(cotangent[0])
    act, state, info, top = call(
        front_kernel,
        "front",
        (
            shape((T, C_ALL), BF16),
            shape((N, INNER)),
            shape((16, INNER), BF16),
            shape((16, INNER)),
        ),
        [
            VMEM((2, T + 8, LANES), F32),
            VMEM((T + 8, LANES), F32),
            VMEM((3, T, LANES), F32),
            VMEM((T, INNER), BF16),
            VMEM((T + LANES, LANES), BF16),
        ],
        8,
        flops=10**9,
        moved=4 * 10**6,
        special=10**6,
    )(conv, step_in, bias, rates, conv_weight, conv_bias, doc_ids)
    act, msg = call(
        fix_kernel,
        "fix",
        (shape((T, C_ALL), BF16), shape((MSG, INNER), BF16)),
        [],
        8,
        moved=2 * 10**6,
        grid=(1,),
        in_specs=[
            whole((8, C_ALL + LANES)),
            whole((16, C_ALL)),
            whole((4, C_ALL)),
            whole((C_ALL,)),
            whole((1, T)),
            whole((16, C_ALL)),
            whole((N, INNER)),
            whole((16, INNER)),
            whole((16, INNER)),
        ],
        out_specs=(whole((16, C_ALL)), whole((MSG, INNER))),
        input_output_aliases={5: 0},
    )(halo, conv, conv_weight, conv_bias, doc_ids, act, state, info, top)
    one = shifted(msg, 1)
    two = shifted(msg, 2)
    early, reach, cum, step, scores, fac, cots, sfac = call(
        early_kernel,
        "early",
        (
            shape((T, EARLY * LANES)),
            shape((T, INNER)),
            shape((H, T)),
            shape((H, T)),
            shape((T, T)),
            shape((T, LANES), BF16),
            shape((2, T, D), BF16),
            shape((16, LANES), BF16),
        ),
        [VMEM((T, LANES), BF16)],
        8,
    )(act, step_in, bias, rates, doc_ids, halo, skip_gain[None], cotangent[0], cot_other)
    c1, c2, c3 = [around(cots, k, "y") for k in (1, 2, 3)]
    late, sgate = call(
        late_kernel, "late", (shape((T, INNER - EARLY * LANES)), shape((T, INNER))), [], 8
    )(act, cum, step, scores, fac, gate_input[0], sfac)
    block = (4, 4, 80, T)
    normed, mine, give = call(
        back_kernel,
        "back",
        (shape((T, INNER), BF16), shape(block, BF16), shape(block, BF16)),
        [
            VMEM((T, INNER), F32),
            VMEM((T, LANES), F32),
            VMEM((INNER, T), BF16),
            VMEM((T, INNER), BF16),
            pltpu.SemaphoreType.DMA,
        ],
        12,
        out_specs=(pl.BlockSpec(memory_space=pltpu.HBM), vmem, vmem),
    )(early, late, reach, sgate, act, one, two, norm_gain)
    got = swapped(give)
    sends = call(
        load_kernel,
        "load",
        (shape((2, 4, 80, T), BF16),) * 3,
        [],
        4,
        in_specs=[vmem] * 2 + [anywhere] * 3,
    )(mine, got, c1, c2, c3)
    r1, r2, r3 = [around(v, k + 1, "y") for k, v in enumerate(sends)]
    packed = call(
        grad_kernel,
        "grad",
        shape((16, 200, LANES), BF16),
        [VMEM((16, 200, LANES), F32)],
        10,
        flops=2 * 10**9,
        moved=8 * 10**6,
    )(mine, got, r1, r2, r3, cots, c1, c2, c3)
    pieces = lax.all_to_all(packed, ("y", "x", "c", "z"), 0, 0, axis_index_groups=PLANES)
    grad = call(sum_kernel, "total", shape((20, D)), [VMEM((200, LANES), F32)], 8, moved=10**6)(pieces)
    return (normed[None], grad)


def solution(mesh):
    fine = Mesh(mesh.devices.reshape(4, 4, 2, 4), ("y", "x", "c", "z"))
    dp = ("y", "x", "c")
    in_specs = (
        P(dp, "z", None),
        P(dp, "z", None),
        P(dp, None, "z"),
        P(),
        P(),
        P(),
        P(),
        P(),
        P(),
        P(dp, "z"),
        P(dp, "z", None),
    )
    out_specs = (P(dp, "z", None), P(dp + ("z",), None))
    return jax.shard_map(per_device, mesh=fine, in_specs=in_specs, out_specs=out_specs, check_vma=False)
```

```python
import jax
import jax.numpy as jnp
from jax import lax
from jax.experimental import pallas as pl
from jax.experimental.pallas import tpu as pltpu
from jax.sharding import Mesh
from jax.sharding import PartitionSpec as P

T = 256
H = 40
HD = 64
N = 128
INNER = 2560
C_ALL = 2816
D = 1280
LANES = 128
XCHUNKS = INNER // LANES
MSG = N + 16
F32 = jnp.float32
BF16 = jnp.bfloat16
HIGH = lax.Precision.HIGHEST
VMEM = pltpu.VMEM


def silu(v):
    return 0.5 * v * (1.0 + jnp.tanh(0.5 * v))


def dot(a, b, dims=((1,), (0,)), precision=None):
    return lax.dot_general(a, b, (dims, ((), ())), preferred_element_type=F32, precision=precision)


def split_rows(v):
    hi = v.astype(BF16).astype(F32)
    rest = v - hi
    mid = rest.astype(BF16).astype(F32)
    low = rest - mid
    return jnp.concatenate([hi, mid, low, jnp.zeros((8, v.shape[1]), F32)], 0)


def head_pick(chunk, width):
    rows = lax.broadcasted_iota(jnp.int32, (LANES, width), 0)
    rows = jnp.where(rows >= 2 * H, rows - 2 * H, jnp.where(rows >= H, rows - H, rows))
    real = lax.broadcasted_iota(jnp.int32, (LANES, width), 0) < 3 * H
    lanes = lax.broadcasted_iota(jnp.int32, (LANES, width), 1)
    head = 2 * chunk + jnp.where(lanes >= width // 2, 1, 0)
    return jnp.where(jnp.logical_and(real, rows == head), 1.0, 0.0).astype(BF16)


def column(row, width):
    n = row.shape[1]
    diag = lax.broadcasted_iota(jnp.int32, (n, n), 0) == lax.broadcasted_iota(jnp.int32, (n, n), 1)
    diag = jnp.where(diag, jnp.broadcast_to(row, (n, n)), 0.0).astype(BF16)
    return dot(diag, jnp.ones((n, width), BF16))


def upright(row):
    n = row.shape[1]
    diag = lax.broadcasted_iota(jnp.int32, (n, n), 0) == lax.broadcasted_iota(jnp.int32, (n, n), 1)
    return jnp.sum(jnp.where(diag, jnp.broadcast_to(row, (n, n)), 0.0), axis=1, keepdims=True)


def steps(step_in, bias, rates):
    step = jax.nn.softplus(step_in[...] + upright(bias[...]))
    decay = -jnp.exp(upright(rates[...])) * step
    tri = (
        lax.broadcasted_iota(jnp.int32, (T, T), 0) <= lax.broadcasted_iota(jnp.int32, (T, T), 1)
    ).astype(F32)
    return step, dot(decay, tri, precision=HIGH)


def edge_kernel(conv, docs, out, rows, ids, sems):
    copies = [
        pltpu.make_async_copy(conv.at[pl.ds(T - 16, 16), :], rows, sems.at[0]),
        pltpu.make_async_copy(docs, ids, sems.at[1]),
    ]
    for copy in copies:
        copy.start()
    for copy in copies:
        copy.wait()
    out[:, 0:C_ALL] = rows[8:16, :]
    last = ids[:, LANES:].astype(F32)
    pick = lax.broadcasted_iota(jnp.int32, (8, LANES), 0) + LANES - 8 == lax.broadcasted_iota(jnp.int32, (8, LANES), 1)
    docb = jnp.sum(jnp.where(pick, jnp.broadcast_to(last, (8, LANES)), 0.0), axis=1, keepdims=True)
    out[:, C_ALL:] = jnp.broadcast_to(docb, (8, LANES)).astype(BF16)


def front_kernel(conv, step_in, bias, rates, w, cb, docs, act, state, info, top, win, dwin, masks, xs, fac):
    doc_row = docs[...].astype(F32)
    docb = column(doc_row, LANES)
    dwin[0:8, :] = jnp.zeros((8, LANES), F32)
    dwin[8:, :] = docb
    for k in range(3):
        masks[k] = (dwin[5 + k : 5 + k + T, :] == docb).astype(F32)
    tag = docb[T - 8 :][7:8]
    win[:, 0:8, :] = jnp.zeros((2, 8, LANES), F32)
    xs[0:16, :] = jnp.zeros((16, INNER), BF16)

    def conv_chunk(j, slot):
        at = pl.ds(pl.multiple_of(j * LANES, LANES), LANES)
        win[slot, 8:, :] = conv[:, at].astype(F32)
        taps = w[:, at]
        total = cb[at].reshape(1, LANES) + taps[3:4] * win[slot, 8:, :]
        for k in range(3):
            total = total + (taps[k : k + 1] * win[slot, 5 + k : 5 + k + T, :]) * masks[k]
        out = silu(total).astype(BF16)
        act[:, at] = out
        return at, out

    for slot in range(2):
        conv_chunk(XCHUNKS + slot, slot)
    step, cum = steps(step_in, bias, rates)
    tail = (doc_row == doc_row[:, T - 1 : T]).astype(F32)
    total = cum[:, T - 1 : T]
    factor = step * jnp.exp(total - cum) * tail
    whole = jnp.broadcast_to(jnp.exp(total), (H, LANES))
    fac[...] = split_rows(jnp.concatenate([factor, whole], 1)).T.astype(BF16)

    def value_chunk(j, slot):
        at, out = conv_chunk(j, slot)
        wide = dot(fac[0 : T + 16, :], head_pick(j, LANES))
        xs[16:, at] = (out[16:].astype(F32) * wide[16:T]).astype(BF16)
        top[:, at] = wide[0:16]
        row = lax.broadcasted_iota(jnp.int32, (16, LANES), 0)
        end = wide[T : T + 16]
        hi = end.astype(BF16).astype(F32)
        rows = jnp.where(row == 0, hi, jnp.where(row == 1, end - hi, jnp.where(row == 2, tag, 0.0)))
        info[:, at] = rows.astype(BF16)

    def value_pair(i, carry):
        for slot in range(2):
            value_chunk(2 * i + slot, slot)
        return carry

    lax.fori_loop(0, XCHUNKS // 2, value_pair, 0)
    b_t = act[:, INNER : INNER + N].astype(F32).T.astype(BF16)
    for k in range(5):
        at = slice(512 * k, 512 * k + 512)
        state[:, at] = dot(b_t, xs[:, at])


def fix_kernel(halo, rows, w, cb, docs, old, state, info, top, act, msg):
    own = column(docs[...].astype(F32), LANES)[0:16]
    before = jnp.where(lax.axis_index("z") > 0, halo[:, C_ALL:].astype(F32), -1.0)
    joined = jnp.concatenate([before, own], 0)
    masks = [(joined[5 + k : 21 + k] == own).astype(F32) for k in range(3)]

    def chunk(j):
        at = slice(j * LANES, j * LANES + LANES)
        win = jnp.concatenate([halo[:, at].astype(F32), rows[:, at].astype(F32)], 0)
        total = cb[at].reshape(1, LANES) + w[3:4, at] * win[8:24]
        for k in range(3):
            total = total + (w[k : k + 1, at] * win[5 + k : 21 + k]) * masks[k]
        out = silu(total).astype(BF16)
        act[:, at] = out
        return at, out

    _, b_rows = chunk(XCHUNKS)
    chunk(XCHUNKS + 1)
    b_t = jnp.concatenate([b_rows.astype(F32), jnp.zeros((LANES - 16, LANES), F32)], 0).T.astype(BF16)
    for j in range(XCHUNKS):
        at, out = chunk(j)
        scaled = (out.astype(F32) * top[:, at]).astype(BF16)
        scaled = jnp.concatenate([scaled, jnp.zeros((LANES - 16, LANES), BF16)], 0)
        value = (state[:, at] + dot(b_t, scaled)).astype(BF16)
        msg[0:N, at] = value
        msg[N:, at] = info[:, at]


def pair_chunk(j, act, cum, step, scores, fac, sfac):
    half = T // 2
    at = pl.ds(pl.multiple_of(j * LANES, LANES), LANES)
    vals = act[:, at]
    lanes = lax.broadcasted_iota(jnp.int32, (T, LANES), 1)
    cols = dot(fac[...], head_pick(j, 2 * LANES))
    skip = dot(sfac[...], head_pick(j, LANES))[0:1]
    top = skip * vals[0:half].astype(F32)
    low = skip * vals[half:].astype(F32)
    for k in range(2):
        mine = jnp.where((lanes >= HD) == (k == 1), vals.astype(F32), 0.0).astype(BF16)
        col = cols[:, k * LANES : (k + 1) * LANES]
        row = cum[pl.ds(2 * j + k, 1), :]
        size = step[pl.ds(2 * j + k, 1), :]

        def weights(t, s):
            ts = slice(t * half, t * half + half)
            ss = slice(s * LANES, s * LANES + LANES)
            spread = jnp.minimum(col[ts] - row[:, ss], 0.0)
            return (scores[ts, ss] * jnp.exp(spread) * size[:, ss]).astype(BF16)

        top = top + dot(weights(0, 0), mine[0:half])
        low = low + dot(jnp.concatenate([weights(1, 0), weights(1, 1)], 1), mine)
    return jnp.concatenate([top, low], 0)


def early_kernel(act, step_in, bias, rates, docs, halo, skip, cot, other, reach, cum, step, scores, fac, cots, sfac, efac):
    cots[0] = cot[...]
    cots[1] = other[...]
    sfac[...] = split_rows(jnp.broadcast_to(upright(skip[...]), (H, LANES))).T[0:16].astype(BF16)
    step[...], cum[...] = steps(step_in, bias, rates)
    doc_row = docs[...].astype(F32)
    prev_tag = halo[:, C_ALL : C_ALL + LANES].astype(F32)[7:8, :]
    prev_tag = jnp.where(lax.axis_index("z") > 0, jnp.concatenate([prev_tag, prev_tag], 1), -1.0)
    matched = (doc_row == prev_tag).astype(F32)
    fac[...] = split_rows(cum[...]).T.astype(BF16)
    efac[...] = split_rows(jnp.exp(cum[...]) * matched).T.astype(BF16)
    c_map = act[:, INNER + N :]
    b_map = act[:, INNER : INNER + N]
    doc_col = column(doc_row, LANES)
    for s in range(2):
        at = slice(s * LANES, s * LANES + LANES)
        g = dot(c_map, b_map[at], ((1,), (1,)))
        order = lax.broadcasted_iota(jnp.int32, (T, LANES), 0) >= (
            lax.broadcasted_iota(jnp.int32, (T, LANES), 1) + s * LANES
        )
        same = jnp.logical_and(order, doc_col == doc_row[:, at])
        scores[:, at] = jnp.where(same, g, 0.0)

    def chunk(j, carry):
        at = pl.ds(pl.multiple_of(j * LANES, LANES), LANES)
        reach[:, at] = dot(efac[...], head_pick(j, LANES))
        return carry

    lax.fori_loop(0, XCHUNKS, chunk, 0)


def late_kernel(act, cum, step, scores, fac, gate, sfac, local, sgate):
    def pair(j, carry):
        at = pl.ds(pl.multiple_of(j * LANES, LANES), LANES)
        local[:, at] = pair_chunk(j, act, cum, step, scores, fac, sfac)
        return carry

    lax.fori_loop(0, XCHUNKS, pair, 0)

    def gates(j, carry):
        at = pl.ds(pl.multiple_of(j * 2 * LANES, 2 * LANES), 2 * LANES)
        sgate[:, at] = silu(gate[:, at].astype(F32))
        return carry

    lax.fori_loop(0, XCHUNKS // 2, gates, 0)


def back_kernel(local, reach, sgate, act, one, two, gain, normed, mine, give, gated, squares, turned, flat, sem):
    c_map = act[:, INNER + N :]
    wide = 2 * LANES

    def first(j):
        at = pl.ds(pl.multiple_of(j * wide, wide), wide)
        info = one[N:, at].astype(F32)
        other = two[N:, at].astype(F32)
        linked = (info[2:3] == other[2:3]).astype(F32)
        weight = (info[0:1] + info[1:2]) * linked
        state = one[0:N, at].astype(F32) + weight * two[0:N, at].astype(F32)
        reading = dot(c_map, state.astype(BF16))
        mixed = local[:, at] + reading * reach[:, at]
        value = mixed.astype(BF16).astype(F32) * sgate[:, at]
        gated[:, at] = value
        value = value * value
        return value[:, 0:LANES] + value[:, LANES:]

    def first_pair(i, carry):
        squares[...] += first(2 * i) + first(2 * i + 1)
        return carry

    squares[...] = first(0) + first(1)
    lax.fori_loop(1, 5, first_pair, 0)
    mean = jnp.sum(squares[...], axis=1, keepdims=True) * (1.0 / INNER)
    squares[...] = jnp.broadcast_to(lax.rsqrt(mean + 1e-05), squares.shape)
    eye = (
        lax.broadcasted_iota(jnp.int32, (LANES, LANES), 0) == lax.broadcasted_iota(jnp.int32, (LANES, LANES), 1)
    ).astype(BF16)

    def second(i, carry):
        for k in range(4):
            at = pl.ds(pl.multiple_of((4 * i + k) * LANES, LANES), LANES)
            value = (gated[:, at] * squares[...] * gain[at].reshape(1, LANES)).astype(BF16)
            flat[:, at] = value
            turned[at, :] = dot(eye, value, ((1,), (1,))).astype(BF16)
        return carry

    lax.fori_loop(0, 5, second, 0)
    out = pltpu.make_async_copy(flat, normed, sem)
    out.start()
    y, x, c = [lax.axis_index(a) for a in ("y", "x", "c")]
    far_y = [lax.rem(i - y + 4, 4) for i in range(4)]
    far_x = [lax.rem(i - x + 4, 4) for i in range(4)]

    def deal(zero, other):
        for i in range(4):
            for j in range(4):
                row = 80 * (2 * (4 * i + j))
                zero[far_y[i], j] = turned[row : row + 80, :]
                other[far_x[j], i] = turned[row + 80 : row + 160, :]

    @pl.when(c == 0)
    def _():
        deal(mine, give)

    @pl.when(c == 1)
    def _():
        deal(give, mine)

    out.wait()


def load_kernel(mine, got, c1, c2, c3, *outs):
    del c1, c2, c3
    for k, out in enumerate(outs):
        out[0] = mine[k + 1]
        out[1] = got[k + 1]


def grad_kernel(mine, got, r1, r2, r3, c0, c1, c2, c3, out, flat):
    left = [mine[0].reshape(320, T), got[0].reshape(320, T)]
    right = [c0[0], c0[1]]
    for r, c in ((r1, c1), (r2, c2), (r3, c3)):
        for k in range(2):
            left.append(r[k].reshape(320, T))
            right.append(c[k])
    for n in range(5):
        at = slice(256 * n, 256 * n + 256)
        total = dot(left[0], right[0][:, at])
        for k in range(1, 8):
            total = total + dot(left[k], right[k][:, at])
        for k in range(2):
            row = 20 * (2 * n + k)
            for i in range(16):
                flat[i, row : row + 20, :] = total[20 * i : 20 * i + 20, k * LANES : k * LANES + LANES]
    for i in range(16):
        out[i] = flat[i].astype(BF16)


def sum_kernel(pieces, out, flat):
    total = pieces[0].astype(F32)
    for i in range(1, 16):
        total = total + pieces[i].astype(F32)
    flat[...] = total
    for k in range(10):
        out[:, k * LANES : k * LANES + LANES] = flat[20 * k : 20 * k + 20, :]


def call(kernel, name, out, scratch, limit, flops=0, moved=0, special=0, **kw):
    return pl.pallas_call(
        kernel,
        name=name,
        out_shape=out,
        scratch_shapes=scratch,
        compiler_params=pltpu.CompilerParams(vmem_limit_bytes=limit << 20),
        cost_estimate=pl.CostEstimate(flops=flops, bytes_accessed=moved, transcendentals=special),
        **kw,
    )


def shape(dims, kind=F32):
    return jax.ShapeDtypeStruct(dims, kind)


def shifted(value, by):
    return lax.ppermute(value, "z", [(i, (i + by) % 4) for i in range(4 if by == 1 else 4 - by)])


def around(value, by, first_axis):
    pairs = []
    for y in range(4):
        for x in range(4):
            for c in range(2):
                along_y = (c == 0) == (first_axis == "y")
                to_y, to_x = ((y + by) % 4, x) if along_y else (y, (x + by) % 4)
                pairs.append(((y * 4 + x) * 2 + c, (to_y * 4 + to_x) * 2 + c))
    return lax.ppermute(value, ("y", "x", "c"), pairs)


def place_of(y, x, c, z):
    return ((y * 4 + x) * 2 + c) * 4 + z


PLANES = [[place_of(y, k, 0, z) for k in range(4) for z in range(4)] for y in range(4)] + [
    [place_of(k, x, 1, z) for k in range(4) for z in range(4)] for x in range(4)
]


def swapped(value):
    return lax.ppermute(value, "c", [(0, 1), (1, 0)])


def whole(dims):
    return pl.BlockSpec(dims, lambda i: (0,) * len(dims))


def per_device(conv_input, gate_input, step_input, step_bias, log_rates, skip_gain, conv_weight, conv_bias, norm_gain, doc_ids, cotangent):
    conv = conv_input[0]
    vmem = pl.BlockSpec(memory_space=VMEM)
    anywhere = pl.BlockSpec(memory_space=pl.ANY)
    halo = call(
        edge_kernel,
        "edge",
        shape((8, C_ALL + LANES), BF16),
        [VMEM((16, C_ALL), BF16), VMEM((1, T), jnp.int32), pltpu.SemaphoreType.DMA((2,))],
        63,
        moved=10**5,
        in_specs=[anywhere] * 2,
    )(conv, doc_ids)
    halo = shifted(halo, 1)
    step_in, bias, rates = step_input[0], step_bias[None], log_rates[None]
    cot_other = swapped(cotangent[0])
    act, state, info, top = call(
        front_kernel,
        "front",
        (
            shape((T, C_ALL), BF16),
            shape((N, INNER)),
            shape((16, INNER), BF16),
            shape((16, INNER)),
        ),
        [
            VMEM((2, T + 8, LANES), F32),
            VMEM((T + 8, LANES), F32),
            VMEM((3, T, LANES), F32),
            VMEM((T, INNER), BF16),
            VMEM((T + LANES, LANES), BF16),
        ],
        8,
        flops=10**9,
        moved=4 * 10**6,
        special=10**6,
    )(conv, step_in, bias, rates, conv_weight, conv_bias, doc_ids)
    act, msg = call(
        fix_kernel,
        "fix",
        (shape((T, C_ALL), BF16), shape((MSG, INNER), BF16)),
        [],
        8,
        moved=2 * 10**6,
        grid=(1,),
        in_specs=[
            whole((8, C_ALL + LANES)),
            whole((16, C_ALL)),
            whole((4, C_ALL)),
            whole((C_ALL,)),
            whole((1, T)),
            whole((16, C_ALL)),
            whole((N, INNER)),
            whole((16, INNER)),
            whole((16, INNER)),
        ],
        out_specs=(whole((16, C_ALL)), whole((MSG, INNER))),
        input_output_aliases={5: 0},
    )(halo, conv, conv_weight, conv_bias, doc_ids, act, state, info, top)
    one = shifted(msg, 1)
    two = shifted(msg, 2)
    reach, cum, step, scores, fac, cots, sfac = call(
        early_kernel,
        "early",
        (
            shape((T, INNER)),
            shape((H, T)),
            shape((H, T)),
            shape((T, T)),
            shape((T, LANES), BF16),
            shape((2, T, D), BF16),
            shape((16, LANES), BF16),
        ),
        [VMEM((T, LANES), BF16)],
        8,
    )(act, step_in, bias, rates, doc_ids, halo, skip_gain[None], cotangent[0], cot_other)
    c1, c2, c3 = [around(cots, k, "y") for k in (1, 2, 3)]
    local, sgate = call(
        late_kernel, "late", (shape((T, INNER)), shape((T, INNER))), [], 8
    )(act, cum, step, scores, fac, gate_input[0], sfac)
    block = (4, 4, 80, T)
    normed, mine, give = call(
        back_kernel,
        "back",
        (shape((T, INNER), BF16), shape(block, BF16), shape(block, BF16)),
        [
            VMEM((T, INNER), F32),
            VMEM((T, LANES), F32),
            VMEM((INNER, T), BF16),
            VMEM((T, INNER), BF16),
            pltpu.SemaphoreType.DMA,
        ],
        12,
        out_specs=(pl.BlockSpec(memory_space=pltpu.HBM), vmem, vmem),
    )(local, reach, sgate, act, one, two, norm_gain)
    got = swapped(give)
    sends = call(
        load_kernel,
        "load",
        (shape((2, 4, 80, T), BF16),) * 3,
        [],
        4,
        in_specs=[vmem] * 2 + [anywhere] * 3,
    )(mine, got, c1, c2, c3)
    r1, r2, r3 = [around(v, k + 1, "y") for k, v in enumerate(sends)]
    packed = call(
        grad_kernel,
        "grad",
        shape((16, 200, LANES), BF16),
        [VMEM((16, 200, LANES), F32)],
        10,
        flops=2 * 10**9,
        moved=8 * 10**6,
    )(mine, got, r1, r2, r3, cots, c1, c2, c3)
    pieces = lax.all_to_all(packed, ("y", "x", "c", "z"), 0, 0, axis_index_groups=PLANES)
    grad = call(sum_kernel, "total", shape((20, D)), [VMEM((200, LANES), F32)], 8, moved=10**6)(pieces)
    return (normed[None], grad)


def solution(mesh):
    fine = Mesh(mesh.devices.reshape(4, 4, 2, 4), ("y", "x", "c", "z"))
    dp = ("y", "x", "c")
    in_specs = (
        P(dp, "z", None),
        P(dp, "z", None),
        P(dp, None, "z"),
        P(),
        P(),
        P(),
        P(),
        P(),
        P(),
        P(dp, "z"),
        P(dp, "z", None),
    )
    out_specs = (P(dp, "z", None), P(dp + ("z",), None))
    return jax.shard_map(per_device, mesh=fine, in_specs=in_specs, out_specs=out_specs, check_vma=False)
```

```python
import jax
import jax.numpy as jnp
from jax import lax
from jax.experimental import pallas as pl
from jax.experimental.pallas import tpu as pltpu
from jax.sharding import Mesh
from jax.sharding import PartitionSpec as P

T = 256
H = 40
HD = 64
N = 128
INNER = 2560
C_ALL = 2816
D = 1280
LANES = 128
XCHUNKS = INNER // LANES
MSG = N + 16
F32 = jnp.float32
BF16 = jnp.bfloat16
HIGH = lax.Precision.HIGHEST
VMEM = pltpu.VMEM


def silu(v):
    return 0.5 * v * (1.0 + jnp.tanh(0.5 * v))


def dot(a, b, dims=((1,), (0,)), precision=None):
    return lax.dot_general(a, b, (dims, ((), ())), preferred_element_type=F32, precision=precision)


def split_rows(v):
    hi = v.astype(BF16).astype(F32)
    rest = v - hi
    mid = rest.astype(BF16).astype(F32)
    low = rest - mid
    return jnp.concatenate([hi, mid, low, jnp.zeros((8, v.shape[1]), F32)], 0)


def head_pick(chunk, width):
    rows = lax.broadcasted_iota(jnp.int32, (LANES, width), 0)
    rows = jnp.where(rows >= 2 * H, rows - 2 * H, jnp.where(rows >= H, rows - H, rows))
    real = lax.broadcasted_iota(jnp.int32, (LANES, width), 0) < 3 * H
    lanes = lax.broadcasted_iota(jnp.int32, (LANES, width), 1)
    head = 2 * chunk + jnp.where(lanes >= width // 2, 1, 0)
    return jnp.where(jnp.logical_and(real, rows == head), 1.0, 0.0).astype(BF16)


def column(row, width):
    n = row.shape[1]
    diag = lax.broadcasted_iota(jnp.int32, (n, n), 0) == lax.broadcasted_iota(jnp.int32, (n, n), 1)
    diag = jnp.where(diag, jnp.broadcast_to(row, (n, n)), 0.0).astype(BF16)
    return dot(diag, jnp.ones((n, width), BF16))


def upright(row):
    n = row.shape[1]
    diag = lax.broadcasted_iota(jnp.int32, (n, n), 0) == lax.broadcasted_iota(jnp.int32, (n, n), 1)
    return jnp.sum(jnp.where(diag, jnp.broadcast_to(row, (n, n)), 0.0), axis=1, keepdims=True)


def steps(step_in, bias, rates):
    step = jax.nn.softplus(step_in[...] + upright(bias[...]))
    decay = -jnp.exp(upright(rates[...])) * step
    tri = (
        lax.broadcasted_iota(jnp.int32, (T, T), 0) <= lax.broadcasted_iota(jnp.int32, (T, T), 1)
    ).astype(F32)
    return step, dot(decay, tri, precision=HIGH)


def edge_kernel(conv, docs, out, rows, ids, sems):
    copies = [
        pltpu.make_async_copy(conv.at[pl.ds(T - 16, 16), :], rows, sems.at[0]),
        pltpu.make_async_copy(docs, ids, sems.at[1]),
    ]
    for copy in copies:
        copy.start()
    for copy in copies:
        copy.wait()
    out[:, 0:C_ALL] = rows[8:16, :]
    last = ids[:, LANES:].astype(F32)
    pick = lax.broadcasted_iota(jnp.int32, (8, LANES), 0) + LANES - 8 == lax.broadcasted_iota(jnp.int32, (8, LANES), 1)
    docb = jnp.sum(jnp.where(pick, jnp.broadcast_to(last, (8, LANES)), 0.0), axis=1, keepdims=True)
    out[:, C_ALL:] = jnp.broadcast_to(docb, (8, LANES)).astype(BF16)


def front_kernel(conv, step_in, bias, rates, w, cb, docs, act, state, info, top, win, dwin, masks, xs, fac):
    doc_row = docs[...].astype(F32)
    docb = column(doc_row, LANES)
    dwin[0:8, :] = jnp.zeros((8, LANES), F32)
    dwin[8:, :] = docb
    for k in range(3):
        masks[k] = (dwin[5 + k : 5 + k + T, :] == docb).astype(F32)
    tag = docb[T - 8 :][7:8]
    win[:, 0:8, :] = jnp.zeros((2, 8, LANES), F32)
    xs[0:16, :] = jnp.zeros((16, INNER), BF16)

    def conv_chunk(j, slot):
        at = pl.ds(pl.multiple_of(j * LANES, LANES), LANES)
        win[slot, 8:, :] = conv[:, at].astype(F32)
        taps = w[:, at]
        total = cb[at].reshape(1, LANES) + taps[3:4] * win[slot, 8:, :]
        for k in range(3):
            total = total + (taps[k : k + 1] * win[slot, 5 + k : 5 + k + T, :]) * masks[k]
        out = silu(total).astype(BF16)
        act[:, at] = out
        return at, out

    for slot in range(2):
        conv_chunk(XCHUNKS + slot, slot)
    step, cum = steps(step_in, bias, rates)
    tail = (doc_row == doc_row[:, T - 1 : T]).astype(F32)
    total = cum[:, T - 1 : T]
    factor = step * jnp.exp(total - cum) * tail
    whole = jnp.broadcast_to(jnp.exp(total), (H, LANES))
    fac[...] = split_rows(jnp.concatenate([factor, whole], 1)).T.astype(BF16)

    def value_chunk(j, slot):
        at, out = conv_chunk(j, slot)
        wide = dot(fac[0 : T + 16, :], head_pick(j, LANES))
        xs[16:, at] = (out[16:].astype(F32) * wide[16:T]).astype(BF16)
        top[:, at] = wide[0:16]
        row = lax.broadcasted_iota(jnp.int32, (16, LANES), 0)
        end = wide[T : T + 16]
        hi = end.astype(BF16).astype(F32)
        rows = jnp.where(row == 0, hi, jnp.where(row == 1, end - hi, jnp.where(row == 2, tag, 0.0)))
        info[:, at] = rows.astype(BF16)

    def value_pair(i, carry):
        for slot in range(2):
            value_chunk(2 * i + slot, slot)
        return carry

    lax.fori_loop(0, XCHUNKS // 2, value_pair, 0)
    b_t = act[:, INNER : INNER + N].astype(F32).T.astype(BF16)
    for k in range(5):
        at = slice(512 * k, 512 * k + 512)
        state[:, at] = dot(b_t, xs[:, at])


def fix_kernel(halo, rows, w, cb, docs, old, state, info, top, act, msg):
    own = column(docs[...].astype(F32), LANES)[0:16]
    before = jnp.where(lax.axis_index("z") > 0, halo[:, C_ALL:].astype(F32), -1.0)
    joined = jnp.concatenate([before, own], 0)
    masks = [(joined[5 + k : 21 + k] == own).astype(F32) for k in range(3)]

    def chunk(j):
        at = slice(j * LANES, j * LANES + LANES)
        win = jnp.concatenate([halo[:, at].astype(F32), rows[:, at].astype(F32)], 0)
        total = cb[at].reshape(1, LANES) + w[3:4, at] * win[8:24]
        for k in range(3):
            total = total + (w[k : k + 1, at] * win[5 + k : 21 + k]) * masks[k]
        out = silu(total).astype(BF16)
        act[:, at] = out
        return at, out

    _, b_rows = chunk(XCHUNKS)
    chunk(XCHUNKS + 1)
    b_t = jnp.concatenate([b_rows.astype(F32), jnp.zeros((LANES - 16, LANES), F32)], 0).T.astype(BF16)
    for j in range(XCHUNKS):
        at, out = chunk(j)
        scaled = (out.astype(F32) * top[:, at]).astype(BF16)
        scaled = jnp.concatenate([scaled, jnp.zeros((LANES - 16, LANES), BF16)], 0)
        value = (state[:, at] + dot(b_t, scaled)).astype(BF16)
        msg[0:N, at] = value
        msg[N:, at] = info[:, at]


def pair_chunk(j, act, cum, step, scores, fac, sfac):
    half = T // 2
    at = pl.ds(pl.multiple_of(j * LANES, LANES), LANES)
    vals = act[:, at]
    lanes = lax.broadcasted_iota(jnp.int32, (T, LANES), 1)
    cols = dot(fac[...], head_pick(j, 2 * LANES))
    skip = dot(sfac[...], head_pick(j, LANES))[0:1]
    top = skip * vals[0:half].astype(F32)
    low = skip * vals[half:].astype(F32)
    for k in range(2):
        mine = jnp.where((lanes >= HD) == (k == 1), vals.astype(F32), 0.0).astype(BF16)
        col = cols[:, k * LANES : (k + 1) * LANES]
        row = cum[pl.ds(2 * j + k, 1), :]
        size = step[pl.ds(2 * j + k, 1), :]

        def weights(t, s):
            ts = slice(t * half, t * half + half)
            ss = slice(s * LANES, s * LANES + LANES)
            spread = jnp.minimum(col[ts] - row[:, ss], 0.0)
            return (scores[ts, ss] * jnp.exp(spread) * size[:, ss]).astype(BF16)

        top = top + dot(weights(0, 0), mine[0:half])
        low = low + dot(jnp.concatenate([weights(1, 0), weights(1, 1)], 1), mine)
    return jnp.concatenate([top, low], 0)


def early_kernel(act, step_in, bias, rates, docs, halo, skip, reach, cum, step, scores, fac, sfac, efac):
    sfac[...] = split_rows(jnp.broadcast_to(upright(skip[...]), (H, LANES))).T[0:16].astype(BF16)
    step[...], cum[...] = steps(step_in, bias, rates)
    doc_row = docs[...].astype(F32)
    prev_tag = halo[:, C_ALL : C_ALL + LANES].astype(F32)[7:8, :]
    prev_tag = jnp.where(lax.axis_index("z") > 0, jnp.concatenate([prev_tag, prev_tag], 1), -1.0)
    matched = (doc_row == prev_tag).astype(F32)
    fac[...] = split_rows(cum[...]).T.astype(BF16)
    efac[...] = split_rows(jnp.exp(cum[...]) * matched).T.astype(BF16)
    c_map = act[:, INNER + N :]
    b_map = act[:, INNER : INNER + N]
    doc_col = column(doc_row, LANES)
    for s in range(2):
        at = slice(s * LANES, s * LANES + LANES)
        g = dot(c_map, b_map[at], ((1,), (1,)))
        order = lax.broadcasted_iota(jnp.int32, (T, LANES), 0) >= (
            lax.broadcasted_iota(jnp.int32, (T, LANES), 1) + s * LANES
        )
        same = jnp.logical_and(order, doc_col == doc_row[:, at])
        scores[:, at] = jnp.where(same, g, 0.0)

    def chunk(j, carry):
        at = pl.ds(pl.multiple_of(j * LANES, LANES), LANES)
        reach[:, at] = dot(efac[...], head_pick(j, LANES))
        return carry

    lax.fori_loop(0, XCHUNKS, chunk, 0)


def late_kernel(act, cum, step, scores, fac, gate, sfac, local, sgate):
    def pair(j, carry):
        at = pl.ds(pl.multiple_of(j * LANES, LANES), LANES)
        local[:, at] = pair_chunk(j, act, cum, step, scores, fac, sfac)
        return carry

    lax.fori_loop(0, XCHUNKS, pair, 0)

    def gates(j, carry):
        at = pl.ds(pl.multiple_of(j * 2 * LANES, 2 * LANES), 2 * LANES)
        sgate[:, at] = silu(gate[:, at].astype(F32))
        return carry

    lax.fori_loop(0, XCHUNKS // 2, gates, 0)


def back_kernel(local, reach, sgate, act, one, two, gain, normed, give, m0, m1, m2, m3, gated, squares, turned, flat, sem):
    c_map = act[:, INNER + N :]
    wide = 2 * LANES

    def first(j):
        at = pl.ds(pl.multiple_of(j * wide, wide), wide)
        info = one[N:, at].astype(F32)
        other = two[N:, at].astype(F32)
        linked = (info[2:3] == other[2:3]).astype(F32)
        weight = (info[0:1] + info[1:2]) * linked
        state = one[0:N, at].astype(F32) + weight * two[0:N, at].astype(F32)
        reading = dot(c_map, state.astype(BF16))
        mixed = local[:, at] + reading * reach[:, at]
        value = mixed.astype(BF16).astype(F32) * sgate[:, at]
        gated[:, at] = value
        value = value * value
        return value[:, 0:LANES] + value[:, LANES:]

    def first_pair(i, carry):
        squares[...] += first(2 * i) + first(2 * i + 1)
        return carry

    squares[...] = first(0) + first(1)
    lax.fori_loop(1, 5, first_pair, 0)
    mean = jnp.sum(squares[...], axis=1, keepdims=True) * (1.0 / INNER)
    squares[...] = jnp.broadcast_to(lax.rsqrt(mean + 1e-05), squares.shape)
    eye = (
        lax.broadcasted_iota(jnp.int32, (LANES, LANES), 0) == lax.broadcasted_iota(jnp.int32, (LANES, LANES), 1)
    ).astype(BF16)

    def second(i, carry):
        for k in range(4):
            at = pl.ds(pl.multiple_of((4 * i + k) * LANES, LANES), LANES)
            value = (gated[:, at] * squares[...] * gain[at].reshape(1, LANES)).astype(BF16)
            flat[:, at] = value
            turned[at, :] = dot(eye, value, ((1,), (1,))).astype(BF16)
        return carry

    lax.fori_loop(0, 5, second, 0)
    out = pltpu.make_async_copy(flat, normed, sem)
    out.start()
    y, x, c = [lax.axis_index(a) for a in ("y", "x", "c")]

    def block(core, k, m):
        i = jnp.where(core == 0, lax.rem(y + k, 4), m)
        j = jnp.where(core == 0, m, lax.rem(x + k, 4))
        return turned[pl.ds(pl.multiple_of(80 * (2 * (4 * i + j) + core), 16), 80), :]

    for k, mine in enumerate((m0, m1, m2, m3)):
        for m in range(4):
            give[k, m] = block(1 - c, k, m)
            mine[m] = block(c, k, m)
    out.wait()


def stack_kernel(one, two, after, out):
    del after
    out[0] = one[...]
    out[1] = two[...]


def load_kernel(got, *rest):
    for k, out in enumerate(rest[-3:]):
        out[...] = got[k + 1]


def grad_kernel(m0, got, m1, m2, m3, r1, r2, r3, c0, c1, c2, c3, out, flat):
    left = [m0[...].reshape(320, T), got[0].reshape(320, T)]
    right = [c0[0], c0[1]]
    for m, r, c in ((m1, r1, c1), (m2, r2, c2), (m3, r3, c3)):
        left += [m[...].reshape(320, T), r[...].reshape(320, T)]
        right += [c[0], c[1]]
    for n in range(5):
        at = slice(256 * n, 256 * n + 256)
        total = dot(left[0], right[0][:, at])
        for k in range(1, 8):
            total = total + dot(left[k], right[k][:, at])
        for k in range(2):
            row = 20 * (2 * n + k)
            for i in range(16):
                flat[i, row : row + 20, :] = total[20 * i : 20 * i + 20, k * LANES : k * LANES + LANES]
    for i in range(16):
        out[i] = flat[i].astype(BF16)


def sum_kernel(pieces, out, flat):
    total = pieces[0].astype(F32)
    for i in range(1, 16):
        total = total + pieces[i].astype(F32)
    flat[...] = total
    for k in range(10):
        out[:, k * LANES : k * LANES + LANES] = flat[20 * k : 20 * k + 20, :]


def call(kernel, name, out, scratch, limit, flops=0, moved=0, special=0, **kw):
    return pl.pallas_call(
        kernel,
        name=name,
        out_shape=out,
        scratch_shapes=scratch,
        compiler_params=pltpu.CompilerParams(vmem_limit_bytes=limit << 20),
        cost_estimate=pl.CostEstimate(flops=flops, bytes_accessed=moved, transcendentals=special),
        **kw,
    )


def shape(dims, kind=F32):
    return jax.ShapeDtypeStruct(dims, kind)


def shifted(value, by):
    return lax.ppermute(value, "z", [(i, (i + by) % 4) for i in range(4 if by == 1 else 4 - by)])


def around(value, by, first_axis):
    pairs = []
    for y in range(4):
        for x in range(4):
            for c in range(2):
                along_y = (c == 0) == (first_axis == "y")
                to_y, to_x = ((y + by) % 4, x) if along_y else (y, (x + by) % 4)
                pairs.append(((y * 4 + x) * 2 + c, (to_y * 4 + to_x) * 2 + c))
    return lax.ppermute(value, ("y", "x", "c"), pairs)


def place_of(y, x, c, z):
    return ((y * 4 + x) * 2 + c) * 4 + z


PLANES = [[place_of(y, k, 0, z) for k in range(4) for z in range(4)] for y in range(4)] + [
    [place_of(k, x, 1, z) for k in range(4) for z in range(4)] for x in range(4)
]


def swapped(value):
    return lax.ppermute(value, "c", [(0, 1), (1, 0)])


def whole(dims):
    return pl.BlockSpec(dims, lambda i: (0,) * len(dims))


def per_device(conv_input, gate_input, step_input, step_bias, log_rates, skip_gain, conv_weight, conv_bias, norm_gain, doc_ids, cotangent):
    conv = conv_input[0]
    vmem = pl.BlockSpec(memory_space=VMEM)
    anywhere = pl.BlockSpec(memory_space=pl.ANY)
    halo = call(
        edge_kernel,
        "edge",
        shape((8, C_ALL + LANES), BF16),
        [VMEM((16, C_ALL), BF16), VMEM((1, T), jnp.int32), pltpu.SemaphoreType.DMA((2,))],
        63,
        moved=10**5,
        in_specs=[anywhere] * 2,
    )(conv, doc_ids)
    halo = shifted(halo, 1)
    step_in, bias, rates = step_input[0], step_bias[None], log_rates[None]
    cot_other = swapped(cotangent[0])
    act, state, info, top = call(
        front_kernel,
        "front",
        (
            shape((T, C_ALL), BF16),
            shape((N, INNER)),
            shape((16, INNER), BF16),
            shape((16, INNER)),
        ),
        [
            VMEM((2, T + 8, LANES), F32),
            VMEM((T + 8, LANES), F32),
            VMEM((3, T, LANES), F32),
            VMEM((T, INNER), BF16),
            VMEM((T + LANES, LANES), BF16),
        ],
        8,
        flops=10**9,
        moved=4 * 10**6,
        special=10**6,
    )(conv, step_in, bias, rates, conv_weight, conv_bias, doc_ids)
    act, msg = call(
        fix_kernel,
        "fix",
        (shape((T, C_ALL), BF16), shape((MSG, INNER), BF16)),
        [],
        8,
        moved=2 * 10**6,
        grid=(1,),
        in_specs=[
            whole((8, C_ALL + LANES)),
            whole((16, C_ALL)),
            whole((4, C_ALL)),
            whole((C_ALL,)),
            whole((1, T)),
            whole((16, C_ALL)),
            whole((N, INNER)),
            whole((16, INNER)),
            whole((16, INNER)),
        ],
        out_specs=(whole((16, C_ALL)), whole((MSG, INNER))),
        input_output_aliases={5: 0},
    )(halo, conv, conv_weight, conv_bias, doc_ids, act, state, info, top)
    one = shifted(msg, 1)
    two = shifted(msg, 2)
    reach, cum, step, scores, fac, sfac = call(
        early_kernel,
        "early",
        (
            shape((T, INNER)),
            shape((H, T)),
            shape((H, T)),
            shape((T, T)),
            shape((T, LANES), BF16),
            shape((16, LANES), BF16),
        ),
        [VMEM((T, LANES), BF16)],
        8,
    )(act, step_in, bias, rates, doc_ids, halo, skip_gain[None])
    cots = call(
        stack_kernel, "stack", shape((2, T, D), BF16), [], 4, in_specs=[vmem] * 2 + [anywhere]
    )(cotangent[0], cot_other, act)
    c1, c2, c3 = [around(cots, k, "y") for k in (1, 2, 3)]
    local, sgate = call(
        late_kernel, "late", (shape((T, INNER)), shape((T, INNER))), [], 8
    )(act, cum, step, scores, fac, gate_input[0], sfac)
    block = (4, 4, 80, T)
    normed, give, m0, *mine = call(
        back_kernel,
        "back",
        (shape((T, INNER), BF16), shape(block, BF16)) + (shape(block[1:], BF16),) * 4,
        [
            VMEM((T, INNER), F32),
            VMEM((T, LANES), F32),
            VMEM((INNER, T), BF16),
            VMEM((T, INNER), BF16),
            pltpu.SemaphoreType.DMA,
        ],
        12,
        out_specs=(pl.BlockSpec(memory_space=pltpu.HBM),) + (vmem,) * 5,
    )(local, reach, sgate, act, one, two, norm_gain)
    got = swapped(give)
    mine = [around(v, k + 1, "y") for k, v in enumerate(mine)]
    sends = call(
        load_kernel, "load", (shape(block[1:], BF16),) * 3, [], 4, in_specs=[vmem] + [anywhere] * 3
    )(got, c1, c2, c3)
    got_far = [around(v, k + 1, "y") for k, v in enumerate(sends)]
    packed = call(
        grad_kernel,
        "grad",
        shape((16, 200, LANES), BF16),
        [VMEM((16, 200, LANES), F32)],
        10,
        flops=2 * 10**9,
        moved=8 * 10**6,
    )(m0, got, *mine, *got_far, cots, c1, c2, c3)
    pieces = lax.all_to_all(packed, ("y", "x", "c", "z"), 0, 0, axis_index_groups=PLANES)
    grad = call(sum_kernel, "total", shape((20, D)), [VMEM((200, LANES), F32)], 8, moved=10**6)(pieces)
    return (normed[None], grad)


def solution(mesh):
    fine = Mesh(mesh.devices.reshape(4, 4, 2, 4), ("y", "x", "c", "z"))
    dp = ("y", "x", "c")
    in_specs = (
        P(dp, "z", None),
        P(dp, "z", None),
        P(dp, None, "z"),
        P(),
        P(),
        P(),
        P(),
        P(),
        P(),
        P(dp, "z"),
        P(dp, "z", None),
    )
    out_specs = (P(dp, "z", None), P(dp + ("z",), None))
    return jax.shard_map(per_device, mesh=fine, in_specs=in_specs, out_specs=out_specs, check_vma=False)
```

```python
import jax
import jax.numpy as jnp
from jax import lax
from jax.experimental import pallas as pl
from jax.experimental.pallas import tpu as pltpu
from jax.sharding import Mesh
from jax.sharding import PartitionSpec as P

T = 256
H = 40
HD = 64
N = 128
INNER = 2560
C_ALL = 2816
D = 1280
LANES = 128
XCHUNKS = INNER // LANES
MSG = N + 16
F32 = jnp.float32
BF16 = jnp.bfloat16
HIGH = lax.Precision.HIGHEST
VMEM = pltpu.VMEM


def silu(v):
    return 0.5 * v * (1.0 + jnp.tanh(0.5 * v))


def dot(a, b, dims=((1,), (0,)), precision=None):
    return lax.dot_general(a, b, (dims, ((), ())), preferred_element_type=F32, precision=precision)


def split_rows(v):
    hi = v.astype(BF16).astype(F32)
    rest = v - hi
    mid = rest.astype(BF16).astype(F32)
    low = rest - mid
    return jnp.concatenate([hi, mid, low, jnp.zeros((8, v.shape[1]), F32)], 0)


def head_pick(chunk, width):
    rows = lax.broadcasted_iota(jnp.int32, (LANES, width), 0)
    rows = jnp.where(rows >= 2 * H, rows - 2 * H, jnp.where(rows >= H, rows - H, rows))
    real = lax.broadcasted_iota(jnp.int32, (LANES, width), 0) < 3 * H
    lanes = lax.broadcasted_iota(jnp.int32, (LANES, width), 1)
    head = 2 * chunk + jnp.where(lanes >= width // 2, 1, 0)
    return jnp.where(jnp.logical_and(real, rows == head), 1.0, 0.0).astype(BF16)


def column(row, width):
    n = row.shape[1]
    diag = lax.broadcasted_iota(jnp.int32, (n, n), 0) == lax.broadcasted_iota(jnp.int32, (n, n), 1)
    diag = jnp.where(diag, jnp.broadcast_to(row, (n, n)), 0.0).astype(BF16)
    return dot(diag, jnp.ones((n, width), BF16))


def upright(row):
    n = row.shape[1]
    diag = lax.broadcasted_iota(jnp.int32, (n, n), 0) == lax.broadcasted_iota(jnp.int32, (n, n), 1)
    return jnp.sum(jnp.where(diag, jnp.broadcast_to(row, (n, n)), 0.0), axis=1, keepdims=True)


def steps(step_in, bias, rates):
    step = jax.nn.softplus(step_in[...] + upright(bias[...]))
    decay = -jnp.exp(upright(rates[...])) * step
    tri = (
        lax.broadcasted_iota(jnp.int32, (T, T), 0) <= lax.broadcasted_iota(jnp.int32, (T, T), 1)
    ).astype(F32)
    return step, dot(decay, tri, precision=HIGH)


def edge_kernel(conv, docs, out, rows, ids, sems):
    copies = [
        pltpu.make_async_copy(conv.at[pl.ds(T - 16, 16), :], rows, sems.at[0]),
        pltpu.make_async_copy(docs, ids, sems.at[1]),
    ]
    for copy in copies:
        copy.start()
    for copy in copies:
        copy.wait()
    out[:, 0:C_ALL] = rows[8:16, :]
    last = ids[:, LANES:].astype(F32)
    pick = lax.broadcasted_iota(jnp.int32, (8, LANES), 0) + LANES - 8 == lax.broadcasted_iota(jnp.int32, (8, LANES), 1)
    docb = jnp.sum(jnp.where(pick, jnp.broadcast_to(last, (8, LANES)), 0.0), axis=1, keepdims=True)
    out[:, C_ALL:] = jnp.broadcast_to(docb, (8, LANES)).astype(BF16)


def prep_kernel(step_in, bias, rates, docs, cum_o, step_o, masks, fac, dwin):
    doc_row = docs[...].astype(F32)
    docb = column(doc_row, LANES)
    dwin[0:8, :] = jnp.zeros((8, LANES), F32)
    dwin[8:, :] = docb
    for k in range(3):
        masks[k] = (dwin[5 + k : 5 + k + T, :] == docb).astype(F32)
    step, cum = steps(step_in, bias, rates)
    step_o[...], cum_o[...] = step, cum
    tail = (doc_row == doc_row[:, T - 1 : T]).astype(F32)
    total = cum[:, T - 1 : T]
    factor = step * jnp.exp(total - cum) * tail
    whole = jnp.broadcast_to(jnp.exp(total), (H, LANES))
    fac[...] = split_rows(jnp.concatenate([factor, whole], 1)).T.astype(BF16)


def front_kernel(conv, w, cb, docs, masks, fac, act, state, info, top, win, xs):
    tag = jnp.broadcast_to(docs[:, T - 1 : T].astype(F32), (1, LANES))
    win[:, 0:8, :] = jnp.zeros((2, 8, LANES), F32)
    xs[0:16, :] = jnp.zeros((16, INNER), BF16)

    def conv_chunk(j, slot):
        at = pl.ds(pl.multiple_of(j * LANES, LANES), LANES)
        win[slot, 8:, :] = conv[:, at].astype(F32)
        taps = w[:, at]
        total = cb[at].reshape(1, LANES) + taps[3:4] * win[slot, 8:, :]
        for k in range(3):
            total = total + (taps[k : k + 1] * win[slot, 5 + k : 5 + k + T, :]) * masks[k]
        out = silu(total).astype(BF16)
        act[:, at] = out
        return at, out

    for slot in range(2):
        conv_chunk(XCHUNKS + slot, slot)

    def value_chunk(j, slot):
        at, out = conv_chunk(j, slot)
        wide = dot(fac[0 : T + 16, :], head_pick(j, LANES))
        xs[16:, at] = (out[16:].astype(F32) * wide[16:T]).astype(BF16)
        top[:, at] = wide[0:16]
        row = lax.broadcasted_iota(jnp.int32, (16, LANES), 0)
        end = wide[T : T + 16]
        hi = end.astype(BF16).astype(F32)
        rows = jnp.where(row == 0, hi, jnp.where(row == 1, end - hi, jnp.where(row == 2, tag, 0.0)))
        info[:, at] = rows.astype(BF16)

    def value_pair(i, carry):
        for slot in range(2):
            value_chunk(2 * i + slot, slot)
        return carry

    lax.fori_loop(0, XCHUNKS // 2, value_pair, 0)
    b_t = act[:, INNER : INNER + N].astype(F32).T.astype(BF16)
    for k in range(5):
        at = slice(512 * k, 512 * k + 512)
        state[:, at] = dot(b_t, xs[:, at])


def fix_kernel(halo, rows, w, cb, docs, old, state, info, top, act, msg):
    own = column(docs[...].astype(F32), LANES)[0:16]
    before = jnp.where(lax.axis_index("z") > 0, halo[:, C_ALL:].astype(F32), -1.0)
    joined = jnp.concatenate([before, own], 0)
    masks = [(joined[5 + k : 21 + k] == own).astype(F32) for k in range(3)]

    def chunk(j):
        at = slice(j * LANES, j * LANES + LANES)
        win = jnp.concatenate([halo[:, at].astype(F32), rows[:, at].astype(F32)], 0)
        total = cb[at].reshape(1, LANES) + w[3:4, at] * win[8:24]
        for k in range(3):
            total = total + (w[k : k + 1, at] * win[5 + k : 21 + k]) * masks[k]
        out = silu(total).astype(BF16)
        act[:, at] = out
        return at, out

    _, b_rows = chunk(XCHUNKS)
    chunk(XCHUNKS + 1)
    b_t = jnp.concatenate([b_rows.astype(F32), jnp.zeros((LANES - 16, LANES), F32)], 0).T.astype(BF16)
    for j in range(XCHUNKS):
        at, out = chunk(j)
        scaled = (out.astype(F32) * top[:, at]).astype(BF16)
        scaled = jnp.concatenate([scaled, jnp.zeros((LANES - 16, LANES), BF16)], 0)
        value = (state[:, at] + dot(b_t, scaled)).astype(BF16)
        msg[0:N, at] = value
        msg[N:, at] = info[:, at]


def pair_chunk(j, act, cum, step, scores, fac, sfac):
    half = T // 2
    at = pl.ds(pl.multiple_of(j * LANES, LANES), LANES)
    vals = act[:, at]
    lanes = lax.broadcasted_iota(jnp.int32, (T, LANES), 1)
    cols = dot(fac[...], head_pick(j, 2 * LANES))
    skip = dot(sfac[...], head_pick(j, LANES))[0:1]
    top = skip * vals[0:half].astype(F32)
    low = skip * vals[half:].astype(F32)
    for k in range(2):
        mine = jnp.where((lanes >= HD) == (k == 1), vals.astype(F32), 0.0).astype(BF16)
        col = cols[:, k * LANES : (k + 1) * LANES]
        row = cum[pl.ds(2 * j + k, 1), :]
        size = step[pl.ds(2 * j + k, 1), :]

        def weights(t, s):
            ts = slice(t * half, t * half + half)
            ss = slice(s * LANES, s * LANES + LANES)
            spread = jnp.minimum(col[ts] - row[:, ss], 0.0)
            return (scores[ts, ss] * jnp.exp(spread) * size[:, ss]).astype(BF16)

        top = top + dot(weights(0, 0), mine[0:half])
        low = low + dot(jnp.concatenate([weights(1, 0), weights(1, 1)], 1), mine)
    return jnp.concatenate([top, low], 0)


def early_kernel(act, cum, docs, halo, skip, reach, scores, fac, sfac, efac):
    sfac[...] = split_rows(jnp.broadcast_to(upright(skip[...]), (H, LANES))).T[0:16].astype(BF16)
    doc_row = docs[...].astype(F32)
    prev_tag = halo[:, C_ALL : C_ALL + LANES].astype(F32)[7:8, :]
    prev_tag = jnp.where(lax.axis_index("z") > 0, jnp.concatenate([prev_tag, prev_tag], 1), -1.0)
    matched = (doc_row == prev_tag).astype(F32)
    fac[...] = split_rows(cum[...]).T.astype(BF16)
    efac[...] = split_rows(jnp.exp(cum[...]) * matched).T.astype(BF16)
    c_map = act[:, INNER + N :]
    b_map = act[:, INNER : INNER + N]
    doc_col = column(doc_row, LANES)
    for s in range(2):
        at = slice(s * LANES, s * LANES + LANES)
        g = dot(c_map, b_map[at], ((1,), (1,)))
        order = lax.broadcasted_iota(jnp.int32, (T, LANES), 0) >= (
            lax.broadcasted_iota(jnp.int32, (T, LANES), 1) + s * LANES
        )
        same = jnp.logical_and(order, doc_col == doc_row[:, at])
        scores[:, at] = jnp.where(same, g, 0.0)

    def chunk(j, carry):
        at = pl.ds(pl.multiple_of(j * LANES, LANES), LANES)
        reach[:, at] = dot(efac[...], head_pick(j, LANES))
        return carry

    lax.fori_loop(0, XCHUNKS, chunk, 0)


def late_kernel(act, cum, step, scores, fac, gate, sfac, local, sgate):
    def pair(j, carry):
        at = pl.ds(pl.multiple_of(j * LANES, LANES), LANES)
        local[:, at] = pair_chunk(j, act, cum, step, scores, fac, sfac)
        return carry

    lax.fori_loop(0, XCHUNKS, pair, 0)

    def gates(j, carry):
        at = pl.ds(pl.multiple_of(j * 2 * LANES, 2 * LANES), 2 * LANES)
        sgate[:, at] = silu(gate[:, at].astype(F32))
        return carry

    lax.fori_loop(0, XCHUNKS // 2, gates, 0)


def back_kernel(local, reach, sgate, act, one, two, gain, normed, give, m0, m1, m2, m3, gated, squares, turned, flat, sem):
    c_map = act[:, INNER + N :]
    wide = 2 * LANES

    def first(j):
        at = pl.ds(pl.multiple_of(j * wide, wide), wide)
        info = one[N:, at].astype(F32)
        other = two[N:, at].astype(F32)
        linked = (info[2:3] == other[2:3]).astype(F32)
        weight = (info[0:1] + info[1:2]) * linked
        state = one[0:N, at].astype(F32) + weight * two[0:N, at].astype(F32)
        reading = dot(c_map, state.astype(BF16))
        mixed = local[:, at] + reading * reach[:, at]
        value = mixed.astype(BF16).astype(F32) * sgate[:, at]
        gated[:, at] = value
        value = value * value
        return value[:, 0:LANES] + value[:, LANES:]

    def first_group(i, carry):
        parts = [first(5 * i + k) for k in range(5)]
        squares[...] += (parts[0] + parts[1]) + (parts[2] + parts[3]) + parts[4]
        return carry

    squares[...] = jnp.zeros_like(squares)
    lax.fori_loop(0, 2, first_group, 0)
    mean = jnp.sum(squares[...], axis=1, keepdims=True) * (1.0 / INNER)
    squares[...] = jnp.broadcast_to(lax.rsqrt(mean + 1e-05), squares.shape)
    eye = (
        lax.broadcasted_iota(jnp.int32, (LANES, LANES), 0) == lax.broadcasted_iota(jnp.int32, (LANES, LANES), 1)
    ).astype(BF16)

    def second(i, carry):
        for k in range(4):
            at = pl.ds(pl.multiple_of((4 * i + k) * LANES, LANES), LANES)
            value = (gated[:, at] * squares[...] * gain[at].reshape(1, LANES)).astype(BF16)
            flat[:, at] = value
            turned[at, :] = dot(eye, value, ((1,), (1,))).astype(BF16)
        return carry

    lax.fori_loop(0, 5, second, 0)
    out = pltpu.make_async_copy(flat, normed, sem)
    out.start()
    y, x, c = [lax.axis_index(a) for a in ("y", "x", "c")]

    def block(core, k, m):
        i = jnp.where(core == 0, lax.rem(y + k, 4), m)
        j = jnp.where(core == 0, m, lax.rem(x + k, 4))
        return turned[pl.ds(pl.multiple_of(80 * (2 * (4 * i + j) + core), 16), 80), :]

    for k, mine in enumerate((m0, m1, m2, m3)):
        for m in range(4):
            give[k, m] = block(1 - c, k, m)
            mine[m] = block(c, k, m)
    out.wait()


def stack_kernel(one, two, after, out):
    del after
    out[0] = one[...]
    out[1] = two[...]


def load_kernel(got, *rest):
    for k, out in enumerate(rest[-3:]):
        out[...] = got[k + 1]


def grad_kernel(m0, got, m1, m2, m3, r1, r2, r3, c0, c1, c2, c3, out, flat):
    left = [m0[...].reshape(320, T), got[0].reshape(320, T)]
    right = [c0[0], c0[1]]
    for m, r, c in ((m1, r1, c1), (m2, r2, c2), (m3, r3, c3)):
        left += [m[...].reshape(320, T), r[...].reshape(320, T)]
        right += [c[0], c[1]]
    for n in range(5):
        at = slice(256 * n, 256 * n + 256)
        total = dot(left[0], right[0][:, at])
        for k in range(1, 8):
            total = total + dot(left[k], right[k][:, at])
        for k in range(2):
            row = 20 * (2 * n + k)
            for i in range(16):
                flat[i, row : row + 20, :] = total[20 * i : 20 * i + 20, k * LANES : k * LANES + LANES]
    for i in range(16):
        out[i] = flat[i].astype(BF16)


def sum_kernel(pieces, out, flat):
    total = pieces[0].astype(F32)
    for i in range(1, 16):
        total = total + pieces[i].astype(F32)
    flat[...] = total
    for k in range(10):
        out[:, k * LANES : k * LANES + LANES] = flat[20 * k : 20 * k + 20, :]


def call(kernel, name, out, scratch, limit, flops=0, moved=0, special=0, **kw):
    return pl.pallas_call(
        kernel,
        name=name,
        out_shape=out,
        scratch_shapes=scratch,
        compiler_params=pltpu.CompilerParams(vmem_limit_bytes=limit << 20),
        cost_estimate=pl.CostEstimate(flops=flops, bytes_accessed=moved, transcendentals=special),
        **kw,
    )


def shape(dims, kind=F32):
    return jax.ShapeDtypeStruct(dims, kind)


def shifted(value, by):
    return lax.ppermute(value, "z", [(i, (i + by) % 4) for i in range(4 if by == 1 else 4 - by)])


def around(value, by, first_axis):
    pairs = []
    for y in range(4):
        for x in range(4):
            for c in range(2):
                along_y = (c == 0) == (first_axis == "y")
                to_y, to_x = ((y + by) % 4, x) if along_y else (y, (x + by) % 4)
                pairs.append(((y * 4 + x) * 2 + c, (to_y * 4 + to_x) * 2 + c))
    return lax.ppermute(value, ("y", "x", "c"), pairs)


def place_of(y, x, c, z):
    return ((y * 4 + x) * 2 + c) * 4 + z


PLANES = [[place_of(y, k, 0, z) for k in range(4) for z in range(4)] for y in range(4)] + [
    [place_of(k, x, 1, z) for k in range(4) for z in range(4)] for x in range(4)
]


def swapped(value):
    return lax.ppermute(value, "c", [(0, 1), (1, 0)])


def whole(dims):
    return pl.BlockSpec(dims, lambda i: (0,) * len(dims))


def per_device(conv_input, gate_input, step_input, step_bias, log_rates, skip_gain, conv_weight, conv_bias, norm_gain, doc_ids, cotangent):
    conv = conv_input[0]
    vmem = pl.BlockSpec(memory_space=VMEM)
    anywhere = pl.BlockSpec(memory_space=pl.ANY)
    halo = call(
        edge_kernel,
        "edge",
        shape((8, C_ALL + LANES), BF16),
        [VMEM((16, C_ALL), BF16), VMEM((1, T), jnp.int32), pltpu.SemaphoreType.DMA((2,))],
        63,
        moved=10**5,
        in_specs=[anywhere] * 2,
    )(conv, doc_ids)
    halo = shifted(halo, 1)
    step_in, bias, rates = step_input[0], step_bias[None], log_rates[None]
    cot_other = swapped(cotangent[0])
    cum, step, masks, spread = call(
        prep_kernel,
        "prep",
        (shape((H, T)), shape((H, T)), shape((3, T, LANES)), shape((T + LANES, LANES), BF16)),
        [VMEM((T + 8, LANES), F32)],
        4,
        flops=10**9,
        moved=10**7,
        special=10**5,
    )(step_in, bias, rates, doc_ids)
    act, state, info, top = call(
        front_kernel,
        "front",
        (shape((T, C_ALL), BF16), shape((N, INNER)), shape((16, INNER), BF16), shape((16, INNER))),
        [VMEM((2, T + 8, LANES), F32), VMEM((T, INNER), BF16)],
        8,
        flops=10**9,
        moved=4 * 10**6,
        special=10**6,
    )(conv, conv_weight, conv_bias, doc_ids, masks, spread)
    act, msg = call(
        fix_kernel,
        "fix",
        (shape((T, C_ALL), BF16), shape((MSG, INNER), BF16)),
        [],
        8,
        moved=2 * 10**6,
        grid=(1,),
        in_specs=[
            whole((8, C_ALL + LANES)),
            whole((16, C_ALL)),
            whole((4, C_ALL)),
            whole((C_ALL,)),
            whole((1, T)),
            whole((16, C_ALL)),
            whole((N, INNER)),
            whole((16, INNER)),
            whole((16, INNER)),
        ],
        out_specs=(whole((16, C_ALL)), whole((MSG, INNER))),
        input_output_aliases={5: 0},
    )(halo, conv, conv_weight, conv_bias, doc_ids, act, state, info, top)
    one = shifted(msg, 1)
    two = shifted(msg, 2)
    reach, scores, fac, sfac = call(
        early_kernel,
        "early",
        (
            shape((T, INNER)),
            shape((T, T)),
            shape((T, LANES), BF16),
            shape((16, LANES), BF16),
        ),
        [VMEM((T, LANES), BF16)],
        8,
    )(act, cum, doc_ids, halo, skip_gain[None])
    cots = call(
        stack_kernel, "stack", shape((2, T, D), BF16), [], 4, in_specs=[vmem] * 2 + [anywhere]
    )(cotangent[0], cot_other, act)
    c1, c2, c3 = [around(cots, k, "y") for k in (1, 2, 3)]
    local, sgate = call(
        late_kernel, "late", (shape((T, INNER)), shape((T, INNER))), [], 8
    )(act, cum, step, scores, fac, gate_input[0], sfac)
    block = (4, 4, 80, T)
    normed, give, m0, *mine = call(
        back_kernel,
        "back",
        (shape((T, INNER), BF16), shape(block, BF16)) + (shape(block[1:], BF16),) * 4,
        [
            VMEM((T, INNER), F32),
            VMEM((T, LANES), F32),
            VMEM((INNER, T), BF16),
            VMEM((T, INNER), BF16),
            pltpu.SemaphoreType.DMA,
        ],
        12,
        out_specs=(pl.BlockSpec(memory_space=pltpu.HBM),) + (vmem,) * 5,
    )(local, reach, sgate, act, one, two, norm_gain)
    got = swapped(give)
    mine = [around(v, k + 1, "y") for k, v in enumerate(mine)]
    sends = call(
        load_kernel, "load", (shape(block[1:], BF16),) * 3, [], 4, in_specs=[vmem] + [anywhere] * 3
    )(got, c1, c2, c3)
    got_far = [around(v, k + 1, "y") for k, v in enumerate(sends)]
    packed = call(
        grad_kernel,
        "grad",
        shape((16, 200, LANES), BF16),
        [VMEM((16, 200, LANES), F32)],
        10,
        flops=2 * 10**9,
        moved=8 * 10**6,
    )(m0, got, *mine, *got_far, cots, c1, c2, c3)
    pieces = lax.all_to_all(packed, ("y", "x", "c", "z"), 0, 0, axis_index_groups=PLANES)
    grad = call(sum_kernel, "total", shape((20, D)), [VMEM((200, LANES), F32)], 8, moved=10**6)(pieces)
    return (normed[None], grad)


def solution(mesh):
    fine = Mesh(mesh.devices.reshape(4, 4, 2, 4), ("y", "x", "c", "z"))
    dp = ("y", "x", "c")
    in_specs = (
        P(dp, "z", None),
        P(dp, "z", None),
        P(dp, None, "z"),
        P(),
        P(),
        P(),
        P(),
        P(),
        P(),
        P(dp, "z"),
        P(dp, "z", None),
    )
    out_specs = (P(dp, "z", None), P(dp + ("z",), None))
    return jax.shard_map(per_device, mesh=fine, in_specs=in_specs, out_specs=out_specs, check_vma=False)
```

```python
import jax
import jax.numpy as jnp
from jax import lax
from jax.experimental import pallas as pl
from jax.experimental.pallas import tpu as pltpu
from jax.sharding import Mesh
from jax.sharding import PartitionSpec as P

T = 256
H = 40
HD = 64
N = 128
INNER = 2560
C_ALL = 2816
D = 1280
LANES = 128
XCHUNKS = INNER // LANES
MSG = N + 16
F32 = jnp.float32
BF16 = jnp.bfloat16
HIGH = lax.Precision.HIGHEST
VMEM = pltpu.VMEM


def silu(v):
    return 0.5 * v * (1.0 + jnp.tanh(0.5 * v))


def dot(a, b, dims=((1,), (0,)), precision=None):
    return lax.dot_general(a, b, (dims, ((), ())), preferred_element_type=F32, precision=precision)


def split_rows(v):
    hi = v.astype(BF16).astype(F32)
    rest = v - hi
    mid = rest.astype(BF16).astype(F32)
    low = rest - mid
    return jnp.concatenate([hi, mid, low, jnp.zeros((8, v.shape[1]), F32)], 0)


def head_pick(chunk, width):
    rows = lax.broadcasted_iota(jnp.int32, (LANES, width), 0)
    rows = jnp.where(rows >= 2 * H, rows - 2 * H, jnp.where(rows >= H, rows - H, rows))
    real = lax.broadcasted_iota(jnp.int32, (LANES, width), 0) < 3 * H
    lanes = lax.broadcasted_iota(jnp.int32, (LANES, width), 1)
    head = 2 * chunk + jnp.where(lanes >= width // 2, 1, 0)
    return jnp.where(jnp.logical_and(real, rows == head), 1.0, 0.0).astype(BF16)


def column(row, width):
    n = row.shape[1]
    diag = lax.broadcasted_iota(jnp.int32, (n, n), 0) == lax.broadcasted_iota(jnp.int32, (n, n), 1)
    diag = jnp.where(diag, jnp.broadcast_to(row, (n, n)), 0.0).astype(BF16)
    return dot(diag, jnp.ones((n, width), BF16))


def upright(row):
    n = row.shape[1]
    diag = lax.broadcasted_iota(jnp.int32, (n, n), 0) == lax.broadcasted_iota(jnp.int32, (n, n), 1)
    return jnp.sum(jnp.where(diag, jnp.broadcast_to(row, (n, n)), 0.0), axis=1, keepdims=True)


def steps(step_in, bias, rates):
    step = jax.nn.softplus(step_in[...] + upright(bias[...]))
    decay = -jnp.exp(upright(rates[...])) * step
    tri = (
        lax.broadcasted_iota(jnp.int32, (T, T), 0) <= lax.broadcasted_iota(jnp.int32, (T, T), 1)
    ).astype(F32)
    return step, dot(decay, tri, precision=HIGH)


def edge_kernel(conv, docs, out, rows, ids, sems):
    copies = [
        pltpu.make_async_copy(conv.at[pl.ds(T - 16, 16), :], rows, sems.at[0]),
        pltpu.make_async_copy(docs, ids, sems.at[1]),
    ]
    for copy in copies:
        copy.start()
    for copy in copies:
        copy.wait()
    out[:, 0:C_ALL] = rows[8:16, :]
    last = ids[:, LANES:].astype(F32)
    pick = lax.broadcasted_iota(jnp.int32, (8, LANES), 0) + LANES - 8 == lax.broadcasted_iota(jnp.int32, (8, LANES), 1)
    docb = jnp.sum(jnp.where(pick, jnp.broadcast_to(last, (8, LANES)), 0.0), axis=1, keepdims=True)
    out[:, C_ALL:] = jnp.broadcast_to(docb, (8, LANES)).astype(BF16)


def prep_kernel(step_in, bias, rates, docs, cum_o, step_o, masks, fac, dwin):
    doc_row = docs[...].astype(F32)
    docb = column(doc_row, LANES)
    dwin[0:8, :] = jnp.zeros((8, LANES), F32)
    dwin[8:, :] = docb
    for k in range(3):
        masks[k] = (dwin[5 + k : 5 + k + T, :] == docb).astype(F32)
    step, cum = steps(step_in, bias, rates)
    step_o[...], cum_o[...] = step, cum
    tail = (doc_row == doc_row[:, T - 1 : T]).astype(F32)
    total = cum[:, T - 1 : T]
    factor = step * jnp.exp(total - cum) * tail
    whole = jnp.broadcast_to(jnp.exp(total), (H, LANES))
    fac[...] = split_rows(jnp.concatenate([factor, whole], 1)).T.astype(BF16)


def front_kernel(conv, w, cb, docs, masks, fac, act, state, info, top, win, xs):
    tag = jnp.broadcast_to(docs[:, T - 1 : T].astype(F32), (1, LANES))
    win[:, 0:8, :] = jnp.zeros((5, 8, LANES), F32)
    xs[0:16, :] = jnp.zeros((16, INNER), BF16)

    def conv_chunk(j, slot):
        at = pl.ds(pl.multiple_of(j * LANES, LANES), LANES)
        win[slot, 8:, :] = conv[:, at].astype(F32)
        taps = w[:, at]
        total = cb[at].reshape(1, LANES) + taps[3:4] * win[slot, 8:, :]
        for k in range(3):
            total = total + (taps[k : k + 1] * win[slot, 5 + k : 5 + k + T, :]) * masks[k]
        out = silu(total).astype(BF16)
        act[:, at] = out
        return at, out

    for slot in range(2):
        conv_chunk(XCHUNKS + slot, slot)

    def value_chunk(j, slot):
        at, out = conv_chunk(j, slot)
        wide = dot(fac[0 : T + 16, :], head_pick(j, LANES))
        xs[16:, at] = (out[16:].astype(F32) * wide[16:T]).astype(BF16)
        top[:, at] = wide[0:16]
        row = lax.broadcasted_iota(jnp.int32, (16, LANES), 0)
        end = wide[T : T + 16]
        hi = end.astype(BF16).astype(F32)
        rows = jnp.where(row == 0, hi, jnp.where(row == 1, end - hi, jnp.where(row == 2, tag, 0.0)))
        info[:, at] = rows.astype(BF16)

    def value_group(i, carry):
        for slot in range(5):
            value_chunk(5 * i + slot, slot)
        return carry

    lax.fori_loop(0, XCHUNKS // 5, value_group, 0)
    b_t = act[:, INNER : INNER + N].astype(F32).T.astype(BF16)
    for k in range(5):
        at = slice(512 * k, 512 * k + 512)
        state[:, at] = dot(b_t, xs[:, at])


def fix_kernel(halo, rows, w, cb, docs, old, state, info, top, act, msg):
    own = column(docs[...].astype(F32), LANES)[0:16]
    before = jnp.where(lax.axis_index("z") > 0, halo[:, C_ALL:].astype(F32), -1.0)
    joined = jnp.concatenate([before, own], 0)
    masks = [(joined[5 + k : 21 + k] == own).astype(F32) for k in range(3)]

    def chunk(j):
        at = slice(j * LANES, j * LANES + LANES)
        win = jnp.concatenate([halo[:, at].astype(F32), rows[:, at].astype(F32)], 0)
        total = cb[at].reshape(1, LANES) + w[3:4, at] * win[8:24]
        for k in range(3):
            total = total + (w[k : k + 1, at] * win[5 + k : 21 + k]) * masks[k]
        out = silu(total).astype(BF16)
        act[:, at] = out
        return at, out

    _, b_rows = chunk(XCHUNKS)
    chunk(XCHUNKS + 1)
    b_t = jnp.concatenate([b_rows.astype(F32), jnp.zeros((LANES - 16, LANES), F32)], 0).T.astype(BF16)
    for j in range(XCHUNKS):
        at, out = chunk(j)
        scaled = (out.astype(F32) * top[:, at]).astype(BF16)
        scaled = jnp.concatenate([scaled, jnp.zeros((LANES - 16, LANES), BF16)], 0)
        value = (state[:, at] + dot(b_t, scaled)).astype(BF16)
        msg[0:N, at] = value
        msg[N:, at] = info[:, at]


def pair_chunk(j, act, cum, step, scores, fac, sfac):
    half = T // 2
    at = pl.ds(pl.multiple_of(j * LANES, LANES), LANES)
    vals = act[:, at]
    lanes = lax.broadcasted_iota(jnp.int32, (T, LANES), 1)
    cols = dot(fac[...], head_pick(j, 2 * LANES))
    skip = dot(sfac[...], head_pick(j, LANES))[0:1]
    top = skip * vals[0:half].astype(F32)
    low = skip * vals[half:].astype(F32)
    for k in range(2):
        mine = jnp.where((lanes >= HD) == (k == 1), vals.astype(F32), 0.0).astype(BF16)
        col = cols[:, k * LANES : (k + 1) * LANES]
        row = cum[pl.ds(2 * j + k, 1), :]
        size = step[pl.ds(2 * j + k, 1), :]

        def weights(t, s):
            ts = slice(t * half, t * half + half)
            ss = slice(s * LANES, s * LANES + LANES)
            spread = jnp.minimum(col[ts] - row[:, ss], 0.0)
            return (scores[ts, ss] * jnp.exp(spread) * size[:, ss]).astype(BF16)

        top = top + dot(weights(0, 0), mine[0:half])
        low = low + dot(jnp.concatenate([weights(1, 0), weights(1, 1)], 1), mine)
    return jnp.concatenate([top, low], 0)


def early_kernel(act, cum, docs, halo, skip, reach, scores, fac, sfac, efac):
    sfac[...] = split_rows(jnp.broadcast_to(upright(skip[...]), (H, LANES))).T[0:16].astype(BF16)
    doc_row = docs[...].astype(F32)
    prev_tag = halo[:, C_ALL : C_ALL + LANES].astype(F32)[7:8, :]
    prev_tag = jnp.where(lax.axis_index("z") > 0, jnp.concatenate([prev_tag, prev_tag], 1), -1.0)
    matched = (doc_row == prev_tag).astype(F32)
    fac[...] = split_rows(cum[...]).T.astype(BF16)
    efac[...] = split_rows(jnp.exp(cum[...]) * matched).T.astype(BF16)
    c_map = act[:, INNER + N :]
    b_map = act[:, INNER : INNER + N]
    doc_col = column(doc_row, LANES)
    for s in range(2):
        at = slice(s * LANES, s * LANES + LANES)
        g = dot(c_map, b_map[at], ((1,), (1,)))
        order = lax.broadcasted_iota(jnp.int32, (T, LANES), 0) >= (
            lax.broadcasted_iota(jnp.int32, (T, LANES), 1) + s * LANES
        )
        same = jnp.logical_and(order, doc_col == doc_row[:, at])
        scores[:, at] = jnp.where(same, g, 0.0)

    def chunk(j, carry):
        at = pl.ds(pl.multiple_of(j * LANES, LANES), LANES)
        reach[:, at] = dot(efac[...], head_pick(j, LANES))
        return carry

    lax.fori_loop(0, XCHUNKS, chunk, 0)


def late_kernel(act, cum, step, scores, fac, gate, sfac, local, sgate):
    def pair(j, carry):
        at = pl.ds(pl.multiple_of(j * LANES, LANES), LANES)
        local[:, at] = pair_chunk(j, act, cum, step, scores, fac, sfac)
        return carry

    lax.fori_loop(0, XCHUNKS, pair, 0)

    def gates(j, carry):
        at = pl.ds(pl.multiple_of(j * 2 * LANES, 2 * LANES), 2 * LANES)
        sgate[:, at] = silu(gate[:, at].astype(F32))
        return carry

    lax.fori_loop(0, XCHUNKS // 2, gates, 0)


def back_kernel(local, reach, sgate, act, one, two, gain, normed, give, m0, m1, m2, m3, gated, squares, turned, flat, sem):
    c_map = act[:, INNER + N :]
    wide = 2 * LANES

    def first(j):
        at = pl.ds(pl.multiple_of(j * wide, wide), wide)
        info = one[N:, at].astype(F32)
        other = two[N:, at].astype(F32)
        linked = (info[2:3] == other[2:3]).astype(F32)
        weight = (info[0:1] + info[1:2]) * linked
        state = one[0:N, at].astype(F32) + weight * two[0:N, at].astype(F32)
        reading = dot(c_map, state.astype(BF16))
        mixed = local[:, at] + reading * reach[:, at]
        value = mixed.astype(BF16).astype(F32) * sgate[:, at]
        gated[:, at] = value
        value = value * value
        return value[:, 0:LANES] + value[:, LANES:]

    def first_group(i, carry):
        parts = [first(5 * i + k) for k in range(5)]
        squares[...] += (parts[0] + parts[1]) + (parts[2] + parts[3]) + parts[4]
        return carry

    squares[...] = jnp.zeros_like(squares)
    lax.fori_loop(0, 2, first_group, 0)
    mean = jnp.sum(squares[...], axis=1, keepdims=True) * (1.0 / INNER)
    squares[...] = jnp.broadcast_to(lax.rsqrt(mean + 1e-05), squares.shape)
    eye = (
        lax.broadcasted_iota(jnp.int32, (LANES, LANES), 0) == lax.broadcasted_iota(jnp.int32, (LANES, LANES), 1)
    ).astype(BF16)

    def second(i, carry):
        for k in range(10):
            at = pl.ds(pl.multiple_of((10 * i + k) * LANES, LANES), LANES)
            value = (gated[:, at] * squares[...] * gain[at].reshape(1, LANES)).astype(BF16)
            flat[:, at] = value
            turned[at, :] = dot(eye, value, ((1,), (1,))).astype(BF16)
        return carry

    lax.fori_loop(0, 2, second, 0)
    out = pltpu.make_async_copy(flat, normed, sem)
    out.start()
    y, x, c = [lax.axis_index(a) for a in ("y", "x", "c")]

    def block(core, k, m):
        i = jnp.where(core == 0, lax.rem(y + k, 4), m)
        j = jnp.where(core == 0, m, lax.rem(x + k, 4))
        return turned[pl.ds(pl.multiple_of(80 * (2 * (4 * i + j) + core), 16), 80), :]

    for k, mine in enumerate((m0, m1, m2, m3)):
        for m in range(4):
            give[k, m] = block(1 - c, k, m)
            mine[m] = block(c, k, m)
    out.wait()


def stack_kernel(one, two, after, out):
    del after
    out[0] = one[...]
    out[1] = two[...]


def load_kernel(got, *rest):
    for k, out in enumerate(rest[-3:]):
        out[...] = got[k + 1]


def grad_kernel(m0, got, m1, m2, m3, r1, r2, r3, c0, c1, c2, c3, out, flat):
    left = [m0[...].reshape(320, T), got[0].reshape(320, T)]
    right = [c0[0], c0[1]]
    for m, r, c in ((m1, r1, c1), (m2, r2, c2), (m3, r3, c3)):
        left += [m[...].reshape(320, T), r[...].reshape(320, T)]
        right += [c[0], c[1]]
    for n in range(5):
        at = slice(256 * n, 256 * n + 256)
        total = dot(left[0], right[0][:, at])
        for k in range(1, 8):
            total = total + dot(left[k], right[k][:, at])
        for k in range(2):
            row = 20 * (2 * n + k)
            for i in range(16):
                flat[i, row : row + 20, :] = total[20 * i : 20 * i + 20, k * LANES : k * LANES + LANES]
    for i in range(16):
        out[i] = flat[i].astype(BF16)


def sum_kernel(pieces, out, flat):
    total = pieces[0].astype(F32)
    for i in range(1, 16):
        total = total + pieces[i].astype(F32)
    flat[...] = total
    for k in range(10):
        out[:, k * LANES : k * LANES + LANES] = flat[20 * k : 20 * k + 20, :]


def call(kernel, name, out, scratch, limit, flops=0, moved=0, special=0, **kw):
    return pl.pallas_call(
        kernel,
        name=name,
        out_shape=out,
        scratch_shapes=scratch,
        compiler_params=pltpu.CompilerParams(vmem_limit_bytes=limit << 20),
        cost_estimate=pl.CostEstimate(flops=flops, bytes_accessed=moved, transcendentals=special),
        **kw,
    )


def shape(dims, kind=F32):
    return jax.ShapeDtypeStruct(dims, kind)


def shifted(value, by):
    return lax.ppermute(value, "z", [(i, (i + by) % 4) for i in range(4 if by == 1 else 4 - by)])


def around(value, by, first_axis):
    pairs = []
    for y in range(4):
        for x in range(4):
            for c in range(2):
                along_y = (c == 0) == (first_axis == "y")
                to_y, to_x = ((y + by) % 4, x) if along_y else (y, (x + by) % 4)
                pairs.append(((y * 4 + x) * 2 + c, (to_y * 4 + to_x) * 2 + c))
    return lax.ppermute(value, ("y", "x", "c"), pairs)


def place_of(y, x, c, z):
    return ((y * 4 + x) * 2 + c) * 4 + z


PLANES = [[place_of(y, k, 0, z) for k in range(4) for z in range(4)] for y in range(4)] + [
    [place_of(k, x, 1, z) for k in range(4) for z in range(4)] for x in range(4)
]


def swapped(value):
    return lax.ppermute(value, "c", [(0, 1), (1, 0)])


def whole(dims):
    return pl.BlockSpec(dims, lambda i: (0,) * len(dims))


def per_device(conv_input, gate_input, step_input, step_bias, log_rates, skip_gain, conv_weight, conv_bias, norm_gain, doc_ids, cotangent):
    conv = conv_input[0]
    vmem = pl.BlockSpec(memory_space=VMEM)
    anywhere = pl.BlockSpec(memory_space=pl.ANY)
    halo = call(
        edge_kernel,
        "edge",
        shape((8, C_ALL + LANES), BF16),
        [VMEM((16, C_ALL), BF16), VMEM((1, T), jnp.int32), pltpu.SemaphoreType.DMA((2,))],
        63,
        moved=10**5,
        in_specs=[anywhere] * 2,
    )(conv, doc_ids)
    halo = shifted(halo, 1)
    step_in, bias, rates = step_input[0], step_bias[None], log_rates[None]
    cot_other = swapped(cotangent[0])
    cum, step, masks, spread = call(
        prep_kernel,
        "prep",
        (shape((H, T)), shape((H, T)), shape((3, T, LANES)), shape((T + LANES, LANES), BF16)),
        [VMEM((T + 8, LANES), F32)],
        4,
        flops=10**9,
        moved=10**7,
        special=10**5,
    )(step_in, bias, rates, doc_ids)
    act, state, info, top = call(
        front_kernel,
        "front",
        (shape((T, C_ALL), BF16), shape((N, INNER)), shape((16, INNER), BF16), shape((16, INNER))),
        [VMEM((5, T + 8, LANES), F32), VMEM((T, INNER), BF16)],
        8,
        flops=10**9,
        moved=4 * 10**6,
        special=10**6,
    )(conv, conv_weight, conv_bias, doc_ids, masks, spread)
    act, msg = call(
        fix_kernel,
        "fix",
        (shape((T, C_ALL), BF16), shape((MSG, INNER), BF16)),
        [],
        8,
        moved=2 * 10**6,
        grid=(1,),
        in_specs=[
            whole((8, C_ALL + LANES)),
            whole((16, C_ALL)),
            whole((4, C_ALL)),
            whole((C_ALL,)),
            whole((1, T)),
            whole((16, C_ALL)),
            whole((N, INNER)),
            whole((16, INNER)),
            whole((16, INNER)),
        ],
        out_specs=(whole((16, C_ALL)), whole((MSG, INNER))),
        input_output_aliases={5: 0},
    )(halo, conv, conv_weight, conv_bias, doc_ids, act, state, info, top)
    one = shifted(msg, 1)
    two = shifted(msg, 2)
    reach, scores, fac, sfac = call(
        early_kernel,
        "early",
        (
            shape((T, INNER)),
            shape((T, T)),
            shape((T, LANES), BF16),
            shape((16, LANES), BF16),
        ),
        [VMEM((T, LANES), BF16)],
        8,
    )(act, cum, doc_ids, halo, skip_gain[None])
    cots = call(
        stack_kernel, "stack", shape((2, T, D), BF16), [], 4, in_specs=[vmem] * 2 + [anywhere]
    )(cotangent[0], cot_other, act)
    c1, c2, c3 = [around(cots, k, "y") for k in (1, 2, 3)]
    local, sgate = call(
        late_kernel, "late", (shape((T, INNER)), shape((T, INNER))), [], 8
    )(act, cum, step, scores, fac, gate_input[0], sfac)
    block = (4, 4, 80, T)
    normed, give, m0, *mine = call(
        back_kernel,
        "back",
        (shape((T, INNER), BF16), shape(block, BF16)) + (shape(block[1:], BF16),) * 4,
        [
            VMEM((T, INNER), F32),
            VMEM((T, LANES), F32),
            VMEM((INNER, T), BF16),
            VMEM((T, INNER), BF16),
            pltpu.SemaphoreType.DMA,
        ],
        12,
        out_specs=(pl.BlockSpec(memory_space=pltpu.HBM),) + (vmem,) * 5,
    )(local, reach, sgate, act, one, two, norm_gain)
    got = swapped(give)
    mine = [around(v, k + 1, "y") for k, v in enumerate(mine)]
    sends = call(
        load_kernel, "load", (shape(block[1:], BF16),) * 3, [], 4, in_specs=[vmem] + [anywhere] * 3
    )(got, c1, c2, c3)
    got_far = [around(v, k + 1, "y") for k, v in enumerate(sends)]
    packed = call(
        grad_kernel,
        "grad",
        shape((16, 200, LANES), BF16),
        [VMEM((16, 200, LANES), F32)],
        10,
        flops=2 * 10**9,
        moved=8 * 10**6,
    )(m0, got, *mine, *got_far, cots, c1, c2, c3)
    pieces = lax.all_to_all(packed, ("y", "x", "c", "z"), 0, 0, axis_index_groups=PLANES)
    grad = call(sum_kernel, "total", shape((20, D)), [VMEM((200, LANES), F32)], 8, moved=10**6)(pieces)
    return (normed[None], grad)


def solution(mesh):
    fine = Mesh(mesh.devices.reshape(4, 4, 2, 4), ("y", "x", "c", "z"))
    dp = ("y", "x", "c")
    in_specs = (
        P(dp, "z", None),
        P(dp, "z", None),
        P(dp, None, "z"),
        P(),
        P(),
        P(),
        P(),
        P(),
        P(),
        P(dp, "z"),
        P(dp, "z", None),
    )
    out_specs = (P(dp, "z", None), P(dp + ("z",), None))
    return jax.shard_map(per_device, mesh=fine, in_specs=in_specs, out_specs=out_specs, check_vma=False)
```

```python
import jax
import jax.numpy as jnp
from jax import lax
from jax.experimental import pallas as pl
from jax.experimental.pallas import tpu as pltpu
from jax.sharding import Mesh
from jax.sharding import PartitionSpec as P

T = 256
H = 40
HD = 64
N = 128
INNER = 2560
C_ALL = 2816
D = 1280
LANES = 128
XCHUNKS = INNER // LANES
MSG = N + 16
F32 = jnp.float32
BF16 = jnp.bfloat16
HIGH = lax.Precision.HIGHEST
VMEM = pltpu.VMEM


def silu(v):
    return 0.5 * v * (1.0 + jnp.tanh(0.5 * v))


def dot(a, b, dims=((1,), (0,)), precision=None):
    return lax.dot_general(a, b, (dims, ((), ())), preferred_element_type=F32, precision=precision)


def split_rows(v):
    hi = v.astype(BF16).astype(F32)
    rest = v - hi
    mid = rest.astype(BF16).astype(F32)
    low = rest - mid
    return jnp.concatenate([hi, mid, low, jnp.zeros((8, v.shape[1]), F32)], 0)


def head_pick(chunk, width):
    rows = lax.broadcasted_iota(jnp.int32, (LANES, width), 0)
    rows = jnp.where(rows >= 2 * H, rows - 2 * H, jnp.where(rows >= H, rows - H, rows))
    real = lax.broadcasted_iota(jnp.int32, (LANES, width), 0) < 3 * H
    lanes = lax.broadcasted_iota(jnp.int32, (LANES, width), 1)
    head = 2 * chunk + jnp.where(lanes >= width // 2, 1, 0)
    return jnp.where(jnp.logical_and(real, rows == head), 1.0, 0.0).astype(BF16)


def column(row, width):
    n = row.shape[1]
    diag = lax.broadcasted_iota(jnp.int32, (n, n), 0) == lax.broadcasted_iota(jnp.int32, (n, n), 1)
    diag = jnp.where(diag, jnp.broadcast_to(row, (n, n)), 0.0).astype(BF16)
    return dot(diag, jnp.ones((n, width), BF16))


def upright(row):
    n = row.shape[1]
    diag = lax.broadcasted_iota(jnp.int32, (n, n), 0) == lax.broadcasted_iota(jnp.int32, (n, n), 1)
    return jnp.sum(jnp.where(diag, jnp.broadcast_to(row, (n, n)), 0.0), axis=1, keepdims=True)


def steps(step_in, bias, rates):
    step = jax.nn.softplus(step_in[...] + upright(bias[...]))
    decay = -jnp.exp(upright(rates[...])) * step
    tri = (
        lax.broadcasted_iota(jnp.int32, (T, T), 0) <= lax.broadcasted_iota(jnp.int32, (T, T), 1)
    ).astype(F32)
    return step, dot(decay, tri, precision=HIGH)


def edge_kernel(conv, docs, out, rows, ids, sems):
    copies = [
        pltpu.make_async_copy(conv.at[pl.ds(T - 16, 16), :], rows, sems.at[0]),
        pltpu.make_async_copy(docs, ids, sems.at[1]),
    ]
    for copy in copies:
        copy.start()
    for copy in copies:
        copy.wait()
    out[:, 0:C_ALL] = rows[8:16, :]
    last = ids[:, LANES:].astype(F32)
    pick = lax.broadcasted_iota(jnp.int32, (8, LANES), 0) + LANES - 8 == lax.broadcasted_iota(jnp.int32, (8, LANES), 1)
    docb = jnp.sum(jnp.where(pick, jnp.broadcast_to(last, (8, LANES)), 0.0), axis=1, keepdims=True)
    out[:, C_ALL:] = jnp.broadcast_to(docb, (8, LANES)).astype(BF16)


def prep_kernel(step_in, bias, rates, docs, cum_o, step_o, masks, fac, dwin):
    doc_row = docs[...].astype(F32)
    docb = column(doc_row, LANES)
    dwin[0:8, :] = jnp.zeros((8, LANES), F32)
    dwin[8:, :] = docb
    for k in range(3):
        masks[k] = (dwin[5 + k : 5 + k + T, :] == docb).astype(F32)
    step, cum = steps(step_in, bias, rates)
    step_o[...], cum_o[...] = step, cum
    tail = (doc_row == doc_row[:, T - 1 : T]).astype(F32)
    total = cum[:, T - 1 : T]
    factor = step * jnp.exp(total - cum) * tail
    whole = jnp.broadcast_to(jnp.exp(total), (H, LANES))
    fac[...] = split_rows(jnp.concatenate([factor, whole], 1)).T.astype(BF16)


def front_kernel(conv, w, cb, docs, masks, fac, act, state, info, top, win, xs):
    tag = jnp.broadcast_to(docs[:, T - 1 : T].astype(F32), (1, LANES))
    win[:, 0:8, :] = jnp.zeros((5, 8, LANES), F32)
    xs[0:16, :] = jnp.zeros((16, INNER), BF16)

    def conv_chunk(j, slot):
        at = pl.ds(pl.multiple_of(j * LANES, LANES), LANES)
        win[slot, 8:, :] = conv[:, at].astype(F32)
        taps = w[:, at]
        total = cb[at].reshape(1, LANES) + taps[3:4] * win[slot, 8:, :]
        for k in range(3):
            total = total + (taps[k : k + 1] * win[slot, 5 + k : 5 + k + T, :]) * masks[k]
        out = silu(total).astype(BF16)
        act[:, at] = out
        return at, out

    for slot in range(2):
        conv_chunk(XCHUNKS + slot, slot)

    def value_chunk(j, slot):
        at, out = conv_chunk(j, slot)
        wide = dot(fac[0 : T + 16, :], head_pick(j, LANES))
        xs[16:, at] = (out[16:].astype(F32) * wide[16:T]).astype(BF16)
        top[:, at] = wide[0:16]
        row = lax.broadcasted_iota(jnp.int32, (16, LANES), 0)
        end = wide[T : T + 16]
        hi = end.astype(BF16).astype(F32)
        rows = jnp.where(row == 0, hi, jnp.where(row == 1, end - hi, jnp.where(row == 2, tag, 0.0)))
        info[:, at] = rows.astype(BF16)

    def value_group(i, carry):
        for slot in range(5):
            value_chunk(5 * i + slot, slot)
        return carry

    lax.fori_loop(0, XCHUNKS // 5, value_group, 0)
    b_t = act[:, INNER : INNER + N].astype(F32).T.astype(BF16)
    for k in range(5):
        at = slice(512 * k, 512 * k + 512)
        state[:, at] = dot(b_t, xs[:, at])


def fix_kernel(halo, rows, w, cb, docs, old, state, info, top, act, msg):
    own = column(docs[...].astype(F32), LANES)[0:16]
    before = jnp.where(lax.axis_index("z") > 0, halo[:, C_ALL:].astype(F32), -1.0)
    joined = jnp.concatenate([before, own], 0)
    masks = [(joined[5 + k : 21 + k] == own).astype(F32) for k in range(3)]

    def chunk(j):
        at = slice(j * LANES, j * LANES + LANES)
        win = jnp.concatenate([halo[:, at].astype(F32), rows[:, at].astype(F32)], 0)
        total = cb[at].reshape(1, LANES) + w[3:4, at] * win[8:24]
        for k in range(3):
            total = total + (w[k : k + 1, at] * win[5 + k : 21 + k]) * masks[k]
        out = silu(total).astype(BF16)
        act[:, at] = out
        return at, out

    _, b_rows = chunk(XCHUNKS)
    chunk(XCHUNKS + 1)
    b_t = jnp.concatenate([b_rows.astype(F32), jnp.zeros((LANES - 16, LANES), F32)], 0).T.astype(BF16)
    for j in range(XCHUNKS):
        at, out = chunk(j)
        scaled = (out.astype(F32) * top[:, at]).astype(BF16)
        scaled = jnp.concatenate([scaled, jnp.zeros((LANES - 16, LANES), BF16)], 0)
        value = (state[:, at] + dot(b_t, scaled)).astype(BF16)
        msg[0:N, at] = value
        msg[N:, at] = info[:, at]


def pair_chunk(j, act, cum, step, scores, fac, sfac):
    half = T // 2
    at = pl.ds(pl.multiple_of(j * LANES, LANES), LANES)
    vals = act[:, at]
    lanes = lax.broadcasted_iota(jnp.int32, (T, LANES), 1)
    cols = dot(fac[...], head_pick(j, 2 * LANES))
    skip = dot(sfac[...], head_pick(j, LANES))[0:1]
    top = skip * vals[0:half].astype(F32)
    low = skip * vals[half:].astype(F32)
    for k in range(2):
        mine = jnp.where((lanes >= HD) == (k == 1), vals.astype(F32), 0.0).astype(BF16)
        col = cols[:, k * LANES : (k + 1) * LANES]
        row = cum[pl.ds(2 * j + k, 1), :]
        size = step[pl.ds(2 * j + k, 1), :]

        def weights(t, s):
            ts = slice(t * half, t * half + half)
            ss = slice(s * LANES, s * LANES + LANES)
            spread = jnp.minimum(col[ts] - row[:, ss], 0.0)
            return (scores[ts, ss] * jnp.exp(spread) * size[:, ss]).astype(BF16)

        top = top + dot(weights(0, 0), mine[0:half])
        low = low + dot(jnp.concatenate([weights(1, 0), weights(1, 1)], 1), mine)
    return jnp.concatenate([top, low], 0)


def early_kernel(act, cum, docs, halo, skip, reach, scores, fac, sfac, efac):
    sfac[...] = split_rows(jnp.broadcast_to(upright(skip[...]), (H, LANES))).T[0:16].astype(BF16)
    doc_row = docs[...].astype(F32)
    prev_tag = halo[:, C_ALL : C_ALL + LANES].astype(F32)[7:8, :]
    prev_tag = jnp.where(lax.axis_index("z") > 0, jnp.concatenate([prev_tag, prev_tag], 1), -1.0)
    matched = (doc_row == prev_tag).astype(F32)
    fac[...] = split_rows(cum[...]).T.astype(BF16)
    efac[...] = split_rows(jnp.exp(cum[...]) * matched).T.astype(BF16)
    c_map = act[:, INNER + N :]
    b_map = act[:, INNER : INNER + N]
    doc_col = column(doc_row, LANES)
    for s in range(2):
        at = slice(s * LANES, s * LANES + LANES)
        g = dot(c_map, b_map[at], ((1,), (1,)))
        order = lax.broadcasted_iota(jnp.int32, (T, LANES), 0) >= (
            lax.broadcasted_iota(jnp.int32, (T, LANES), 1) + s * LANES
        )
        same = jnp.logical_and(order, doc_col == doc_row[:, at])
        scores[:, at] = jnp.where(same, g, 0.0)

    def chunk(j, carry):
        at = pl.ds(pl.multiple_of(j * LANES, LANES), LANES)
        reach[:, at] = dot(efac[...], head_pick(j, LANES))
        return carry

    lax.fori_loop(0, XCHUNKS, chunk, 0)


def late_kernel(act, cum, step, scores, fac, gate, sfac, local, sgate):
    def pair(j, carry):
        at = pl.ds(pl.multiple_of(j * LANES, LANES), LANES)
        local[:, at] = pair_chunk(j, act, cum, step, scores, fac, sfac)
        return carry

    lax.fori_loop(0, XCHUNKS, pair, 0)

    def gates(j, carry):
        at = pl.ds(pl.multiple_of(j * 2 * LANES, 2 * LANES), 2 * LANES)
        sgate[:, at] = silu(gate[:, at].astype(F32))
        return carry

    lax.fori_loop(0, XCHUNKS // 2, gates, 0)


def back_kernel(local, reach, sgate, act, one, two, gain, normed, give, m0, m1, m2, m3, gated, squares, turned, flat, sem):
    c_map = act[:, INNER + N :]
    wide = 2 * LANES

    def first(j):
        at = pl.ds(pl.multiple_of(j * wide, wide), wide)
        info = one[N:, at].astype(F32)
        other = two[N:, at].astype(F32)
        linked = (info[2:3] == other[2:3]).astype(F32)
        weight = (info[0:1] + info[1:2]) * linked
        state = one[0:N, at].astype(F32) + weight * two[0:N, at].astype(F32)
        reading = dot(c_map, state.astype(BF16))
        mixed = local[:, at] + reading * reach[:, at]
        value = mixed.astype(BF16).astype(F32) * sgate[:, at]
        gated[:, at] = value
        value = value * value
        return value[:, 0:LANES] + value[:, LANES:]

    def first_group(i, carry):
        parts = first(10 * i)
        for k in range(1, 10):
            parts = parts + first(10 * i + k)
        squares[...] += parts
        return carry

    squares[...] = jnp.zeros_like(squares)
    lax.fori_loop(0, 1, first_group, 0)
    mean = jnp.sum(squares[...], axis=1, keepdims=True) * (1.0 / INNER)
    squares[...] = jnp.broadcast_to(lax.rsqrt(mean + 1e-05), squares.shape)
    eye = (
        lax.broadcasted_iota(jnp.int32, (LANES, LANES), 0) == lax.broadcasted_iota(jnp.int32, (LANES, LANES), 1)
    ).astype(BF16)

    def second(i, carry):
        for k in range(10):
            at = pl.ds(pl.multiple_of((10 * i + k) * LANES, LANES), LANES)
            value = (gated[:, at] * squares[...] * gain[at].reshape(1, LANES)).astype(BF16)
            flat[:, at] = value
            turned[at, :] = dot(eye, value, ((1,), (1,))).astype(BF16)
        return carry

    lax.fori_loop(0, 2, second, 0)
    out = pltpu.make_async_copy(flat, normed, sem)
    out.start()
    y, x, c = [lax.axis_index(a) for a in ("y", "x", "c")]

    def block(core, k, m):
        i = jnp.where(core == 0, lax.rem(y + k, 4), m)
        j = jnp.where(core == 0, m, lax.rem(x + k, 4))
        return turned[pl.ds(pl.multiple_of(80 * (2 * (4 * i + j) + core), 16), 80), :]

    for k, mine in enumerate((m0, m1, m2, m3)):
        for m in range(4):
            give[k, m] = block(1 - c, k, m)
            mine[m] = block(c, k, m)
    out.wait()


def stack_kernel(one, two, after, out):
    del after
    out[0] = one[...]
    out[1] = two[...]


def load_kernel(got, *rest):
    for k, out in enumerate(rest[-3:]):
        out[...] = got[k + 1]


def grad_kernel(m0, got, m1, m2, m3, r1, r2, r3, c0, c1, c2, c3, out, flat):
    left = [m0[...].reshape(320, T), got[0].reshape(320, T)]
    right = [c0[0], c0[1]]
    for m, r, c in ((m1, r1, c1), (m2, r2, c2), (m3, r3, c3)):
        left += [m[...].reshape(320, T), r[...].reshape(320, T)]
        right += [c[0], c[1]]
    for n in range(5):
        at = slice(256 * n, 256 * n + 256)
        total = dot(left[0], right[0][:, at])
        for k in range(1, 8):
            total = total + dot(left[k], right[k][:, at])
        for k in range(2):
            row = 20 * (2 * n + k)
            for i in range(16):
                flat[i, row : row + 20, :] = total[20 * i : 20 * i + 20, k * LANES : k * LANES + LANES]
    for i in range(16):
        out[i] = flat[i].astype(BF16)


def sum_kernel(pieces, out, flat):
    total = pieces[0].astype(F32)
    for i in range(1, 16):
        total = total + pieces[i].astype(F32)
    flat[...] = total
    for k in range(10):
        out[:, k * LANES : k * LANES + LANES] = flat[20 * k : 20 * k + 20, :]


def call(kernel, name, out, scratch, limit, flops=0, moved=0, special=0, **kw):
    return pl.pallas_call(
        kernel,
        name=name,
        out_shape=out,
        scratch_shapes=scratch,
        compiler_params=pltpu.CompilerParams(vmem_limit_bytes=limit << 20),
        cost_estimate=pl.CostEstimate(flops=flops, bytes_accessed=moved, transcendentals=special),
        **kw,
    )


def shape(dims, kind=F32):
    return jax.ShapeDtypeStruct(dims, kind)


def shifted(value, by):
    return lax.ppermute(value, "z", [(i, (i + by) % 4) for i in range(4 if by == 1 else 4 - by)])


def around(value, by, first_axis):
    pairs = []
    for y in range(4):
        for x in range(4):
            for c in range(2):
                along_y = (c == 0) == (first_axis == "y")
                to_y, to_x = ((y + by) % 4, x) if along_y else (y, (x + by) % 4)
                pairs.append(((y * 4 + x) * 2 + c, (to_y * 4 + to_x) * 2 + c))
    return lax.ppermute(value, ("y", "x", "c"), pairs)


def place_of(y, x, c, z):
    return ((y * 4 + x) * 2 + c) * 4 + z


PLANES = [[place_of(y, k, 0, z) for k in range(4) for z in range(4)] for y in range(4)] + [
    [place_of(k, x, 1, z) for k in range(4) for z in range(4)] for x in range(4)
]


def swapped(value):
    return lax.ppermute(value, "c", [(0, 1), (1, 0)])


def whole(dims):
    return pl.BlockSpec(dims, lambda i: (0,) * len(dims))


def per_device(conv_input, gate_input, step_input, step_bias, log_rates, skip_gain, conv_weight, conv_bias, norm_gain, doc_ids, cotangent):
    conv = conv_input[0]
    vmem = pl.BlockSpec(memory_space=VMEM)
    anywhere = pl.BlockSpec(memory_space=pl.ANY)
    halo = call(
        edge_kernel,
        "edge",
        shape((8, C_ALL + LANES), BF16),
        [VMEM((16, C_ALL), BF16), VMEM((1, T), jnp.int32), pltpu.SemaphoreType.DMA((2,))],
        63,
        moved=10**5,
        in_specs=[anywhere] * 2,
    )(conv, doc_ids)
    halo = shifted(halo, 1)
    step_in, bias, rates = step_input[0], step_bias[None], log_rates[None]
    cot_other = swapped(cotangent[0])
    cum, step, masks, spread = call(
        prep_kernel,
        "prep",
        (shape((H, T)), shape((H, T)), shape((3, T, LANES)), shape((T + LANES, LANES), BF16)),
        [VMEM((T + 8, LANES), F32)],
        4,
        flops=10**9,
        moved=10**7,
        special=10**5,
    )(step_in, bias, rates, doc_ids)
    act, state, info, top = call(
        front_kernel,
        "front",
        (shape((T, C_ALL), BF16), shape((N, INNER)), shape((16, INNER), BF16), shape((16, INNER))),
        [VMEM((5, T + 8, LANES), F32), VMEM((T, INNER), BF16)],
        8,
        flops=10**9,
        moved=4 * 10**6,
        special=10**6,
    )(conv, conv_weight, conv_bias, doc_ids, masks, spread)
    act, msg = call(
        fix_kernel,
        "fix",
        (shape((T, C_ALL), BF16), shape((MSG, INNER), BF16)),
        [],
        8,
        moved=2 * 10**6,
        grid=(1,),
        in_specs=[
            whole((8, C_ALL + LANES)),
            whole((16, C_ALL)),
            whole((4, C_ALL)),
            whole((C_ALL,)),
            whole((1, T)),
            whole((16, C_ALL)),
            whole((N, INNER)),
            whole((16, INNER)),
            whole((16, INNER)),
        ],
        out_specs=(whole((16, C_ALL)), whole((MSG, INNER))),
        input_output_aliases={5: 0},
    )(halo, conv, conv_weight, conv_bias, doc_ids, act, state, info, top)
    one = shifted(msg, 1)
    two = shifted(msg, 2)
    reach, scores, fac, sfac = call(
        early_kernel,
        "early",
        (
            shape((T, INNER)),
            shape((T, T)),
            shape((T, LANES), BF16),
            shape((16, LANES), BF16),
        ),
        [VMEM((T, LANES), BF16)],
        8,
    )(act, cum, doc_ids, halo, skip_gain[None])
    cots = call(
        stack_kernel, "stack", shape((2, T, D), BF16), [], 4, in_specs=[vmem] * 2 + [anywhere]
    )(cotangent[0], cot_other, act)
    c1, c2, c3 = [around(cots, k, "y") for k in (1, 2, 3)]
    local, sgate = call(
        late_kernel, "late", (shape((T, INNER)), shape((T, INNER))), [], 8
    )(act, cum, step, scores, fac, gate_input[0], sfac)
    block = (4, 4, 80, T)
    normed, give, m0, *mine = call(
        back_kernel,
        "back",
        (shape((T, INNER), BF16), shape(block, BF16)) + (shape(block[1:], BF16),) * 4,
        [
            VMEM((T, INNER), F32),
            VMEM((T, LANES), F32),
            VMEM((INNER, T), BF16),
            VMEM((T, INNER), BF16),
            pltpu.SemaphoreType.DMA,
        ],
        12,
        out_specs=(pl.BlockSpec(memory_space=pltpu.HBM),) + (vmem,) * 5,
    )(local, reach, sgate, act, one, two, norm_gain)
    got = swapped(give)
    mine = [around(v, k + 1, "y") for k, v in enumerate(mine)]
    sends = call(
        load_kernel, "load", (shape(block[1:], BF16),) * 3, [], 4, in_specs=[vmem] + [anywhere] * 3
    )(got, c1, c2, c3)
    got_far = [around(v, k + 1, "y") for k, v in enumerate(sends)]
    packed = call(
        grad_kernel,
        "grad",
        shape((16, 200, LANES), BF16),
        [VMEM((16, 200, LANES), F32)],
        10,
        flops=2 * 10**9,
        moved=8 * 10**6,
    )(m0, got, *mine, *got_far, cots, c1, c2, c3)
    pieces = lax.all_to_all(packed, ("y", "x", "c", "z"), 0, 0, axis_index_groups=PLANES)
    grad = call(sum_kernel, "total", shape((20, D)), [VMEM((200, LANES), F32)], 8, moved=10**6)(pieces)
    return (normed[None], grad)


def solution(mesh):
    fine = Mesh(mesh.devices.reshape(4, 4, 2, 4), ("y", "x", "c", "z"))
    dp = ("y", "x", "c")
    in_specs = (
        P(dp, "z", None),
        P(dp, "z", None),
        P(dp, None, "z"),
        P(),
        P(),
        P(),
        P(),
        P(),
        P(),
        P(dp, "z"),
        P(dp, "z", None),
    )
    out_specs = (P(dp, "z", None), P(dp + ("z",), None))
    return jax.shard_map(per_device, mesh=fine, in_specs=in_specs, out_specs=out_specs, check_vma=False)
```

```python
import jax
import jax.numpy as jnp
from jax import lax
from jax.experimental import pallas as pl
from jax.experimental.pallas import tpu as pltpu
from jax.sharding import Mesh
from jax.sharding import PartitionSpec as P

T = 256
H = 40
HD = 64
N = 128
INNER = 2560
C_ALL = 2816
D = 1280
LANES = 128
XCHUNKS = INNER // LANES
MSG = N + 16
F32 = jnp.float32
BF16 = jnp.bfloat16
HIGH = lax.Precision.HIGHEST
VMEM = pltpu.VMEM


def silu(v):
    return 0.5 * v * (1.0 + jnp.tanh(0.5 * v))


def dot(a, b, dims=((1,), (0,)), precision=None):
    return lax.dot_general(a, b, (dims, ((), ())), preferred_element_type=F32, precision=precision)


def split_rows(v):
    hi = v.astype(BF16).astype(F32)
    rest = v - hi
    mid = rest.astype(BF16).astype(F32)
    low = rest - mid
    return jnp.concatenate([hi, mid, low, jnp.zeros((8, v.shape[1]), F32)], 0)


def head_pick(chunk, width):
    rows = lax.broadcasted_iota(jnp.int32, (LANES, width), 0)
    rows = jnp.where(rows >= 2 * H, rows - 2 * H, jnp.where(rows >= H, rows - H, rows))
    real = lax.broadcasted_iota(jnp.int32, (LANES, width), 0) < 3 * H
    lanes = lax.broadcasted_iota(jnp.int32, (LANES, width), 1)
    head = 2 * chunk + jnp.where(lanes >= width // 2, 1, 0)
    return jnp.where(jnp.logical_and(real, rows == head), 1.0, 0.0).astype(BF16)


def column(row, width):
    n = row.shape[1]
    diag = lax.broadcasted_iota(jnp.int32, (n, n), 0) == lax.broadcasted_iota(jnp.int32, (n, n), 1)
    diag = jnp.where(diag, jnp.broadcast_to(row, (n, n)), 0.0).astype(BF16)
    return dot(diag, jnp.ones((n, width), BF16))


def upright(row):
    n = row.shape[1]
    diag = lax.broadcasted_iota(jnp.int32, (n, n), 0) == lax.broadcasted_iota(jnp.int32, (n, n), 1)
    return jnp.sum(jnp.where(diag, jnp.broadcast_to(row, (n, n)), 0.0), axis=1, keepdims=True)


def steps(step_in, bias, rates):
    step = jax.nn.softplus(step_in[...] + upright(bias[...]))
    decay = -jnp.exp(upright(rates[...])) * step
    tri = (
        lax.broadcasted_iota(jnp.int32, (T, T), 0) <= lax.broadcasted_iota(jnp.int32, (T, T), 1)
    ).astype(F32)
    return step, dot(decay, tri, precision=HIGH)


def edge_kernel(conv, docs, out, rows, ids, sems):
    copies = [
        pltpu.make_async_copy(conv.at[pl.ds(T - 16, 16), :], rows, sems.at[0]),
        pltpu.make_async_copy(docs, ids, sems.at[1]),
    ]
    for copy in copies:
        copy.start()
    for copy in copies:
        copy.wait()
    out[:, 0:C_ALL] = rows[8:16, :]
    last = ids[:, LANES:].astype(F32)
    pick = lax.broadcasted_iota(jnp.int32, (8, LANES), 0) + LANES - 8 == lax.broadcasted_iota(jnp.int32, (8, LANES), 1)
    docb = jnp.sum(jnp.where(pick, jnp.broadcast_to(last, (8, LANES)), 0.0), axis=1, keepdims=True)
    out[:, C_ALL:] = jnp.broadcast_to(docb, (8, LANES)).astype(BF16)


def prep_kernel(step_in, bias, rates, docs, cum_o, step_o, masks, fac, dwin):
    doc_row = docs[...].astype(F32)
    docb = column(doc_row, LANES)
    dwin[0:8, :] = jnp.zeros((8, LANES), F32)
    dwin[8:, :] = docb
    for k in range(3):
        masks[k] = (dwin[5 + k : 5 + k + T, :] == docb).astype(F32)
    step, cum = steps(step_in, bias, rates)
    step_o[...], cum_o[...] = step, cum
    tail = (doc_row == doc_row[:, T - 1 : T]).astype(F32)
    total = cum[:, T - 1 : T]
    factor = step * jnp.exp(total - cum) * tail
    whole = jnp.broadcast_to(jnp.exp(total), (H, LANES))
    fac[...] = split_rows(jnp.concatenate([factor, whole], 1)).T.astype(BF16)


def front_kernel(conv, w, cb, docs, masks, fac, act, state, info, top, win, xs):
    tag = jnp.broadcast_to(docs[:, T - 1 : T].astype(F32), (1, LANES))
    win[:, 0:8, :] = jnp.zeros((5, 8, LANES), F32)
    xs[0:16, :] = jnp.zeros((16, INNER), BF16)

    def conv_chunk(j, slot):
        at = pl.ds(pl.multiple_of(j * LANES, LANES), LANES)
        win[slot, 8:, :] = conv[:, at].astype(F32)
        taps = w[:, at]
        total = cb[at].reshape(1, LANES) + taps[3:4] * win[slot, 8:, :]
        for k in range(3):
            total = total + (taps[k : k + 1] * win[slot, 5 + k : 5 + k + T, :]) * masks[k]
        out = silu(total).astype(BF16)
        act[:, at] = out
        return at, out

    for slot in range(2):
        conv_chunk(XCHUNKS + slot, slot)

    def value_chunk(j, slot):
        at, out = conv_chunk(j, slot)
        wide = dot(fac[0 : T + 16, :], head_pick(j, LANES))
        xs[16:, at] = (out[16:].astype(F32) * wide[16:T]).astype(BF16)
        top[:, at] = wide[0:16]
        row = lax.broadcasted_iota(jnp.int32, (16, LANES), 0)
        end = wide[T : T + 16]
        hi = end.astype(BF16).astype(F32)
        rows = jnp.where(row == 0, hi, jnp.where(row == 1, end - hi, jnp.where(row == 2, tag, 0.0)))
        info[:, at] = rows.astype(BF16)

    def value_group(i, carry):
        for slot in range(5):
            value_chunk(5 * i + slot, slot)
        return carry

    lax.fori_loop(0, XCHUNKS // 5, value_group, 0)
    b_t = act[:, INNER : INNER + N].astype(F32).T.astype(BF16)
    for k in range(5):
        at = slice(512 * k, 512 * k + 512)
        state[:, at] = dot(b_t, xs[:, at])


def fix_kernel(halo, rows, w, cb, docs, old, state, info, top, act, msg):
    own = column(docs[...].astype(F32), LANES)[0:16]
    before = jnp.where(lax.axis_index("z") > 0, halo[:, C_ALL:].astype(F32), -1.0)
    joined = jnp.concatenate([before, own], 0)
    masks = [(joined[5 + k : 21 + k] == own).astype(F32) for k in range(3)]

    def chunk(j):
        at = slice(j * LANES, j * LANES + LANES)
        win = jnp.concatenate([halo[:, at].astype(F32), rows[:, at].astype(F32)], 0)
        total = cb[at].reshape(1, LANES) + w[3:4, at] * win[8:24]
        for k in range(3):
            total = total + (w[k : k + 1, at] * win[5 + k : 21 + k]) * masks[k]
        out = silu(total).astype(BF16)
        act[:, at] = out
        return at, out

    _, b_rows = chunk(XCHUNKS)
    chunk(XCHUNKS + 1)
    b_t = jnp.concatenate([b_rows.astype(F32), jnp.zeros((LANES - 16, LANES), F32)], 0).T.astype(BF16)
    for j in range(XCHUNKS):
        at, out = chunk(j)
        scaled = (out.astype(F32) * top[:, at]).astype(BF16)
        scaled = jnp.concatenate([scaled, jnp.zeros((LANES - 16, LANES), BF16)], 0)
        value = (state[:, at] + dot(b_t, scaled)).astype(BF16)
        msg[0:N, at] = value
        msg[N:, at] = info[:, at]


def pair_chunk(j, act, cum, step, scores, fac, sfac):
    half = T // 2
    at = pl.ds(pl.multiple_of(j * LANES, LANES), LANES)
    vals = act[:, at]
    lanes = lax.broadcasted_iota(jnp.int32, (T, LANES), 1)
    cols = dot(fac[...], head_pick(j, 2 * LANES))
    skip = dot(sfac[...], head_pick(j, LANES))[0:1]
    top = skip * vals[0:half].astype(F32)
    low = skip * vals[half:].astype(F32)
    for k in range(2):
        mine = jnp.where((lanes >= HD) == (k == 1), vals.astype(F32), 0.0).astype(BF16)
        col = cols[:, k * LANES : (k + 1) * LANES]
        row = cum[pl.ds(2 * j + k, 1), :]
        size = step[pl.ds(2 * j + k, 1), :]

        def weights(t, s):
            ts = slice(t * half, t * half + half)
            ss = slice(s * LANES, s * LANES + LANES)
            spread = jnp.minimum(col[ts] - row[:, ss], 0.0)
            return (scores[ts, ss] * jnp.exp(spread) * size[:, ss]).astype(BF16)

        top = top + dot(weights(0, 0), mine[0:half])
        low = low + dot(jnp.concatenate([weights(1, 0), weights(1, 1)], 1), mine)
    return jnp.concatenate([top, low], 0)


def early_kernel(act, cum, docs, halo, skip, reach, scores, fac, sfac, efac):
    sfac[...] = split_rows(jnp.broadcast_to(upright(skip[...]), (H, LANES))).T[0:16].astype(BF16)
    doc_row = docs[...].astype(F32)
    prev_tag = halo[:, C_ALL : C_ALL + LANES].astype(F32)[7:8, :]
    prev_tag = jnp.where(lax.axis_index("z") > 0, jnp.concatenate([prev_tag, prev_tag], 1), -1.0)
    matched = (doc_row == prev_tag).astype(F32)
    fac[...] = split_rows(cum[...]).T.astype(BF16)
    efac[...] = split_rows(jnp.exp(cum[...]) * matched).T.astype(BF16)
    c_map = act[:, INNER + N :]
    b_map = act[:, INNER : INNER + N]
    doc_col = column(doc_row, LANES)
    for s in range(2):
        at = slice(s * LANES, s * LANES + LANES)
        g = dot(c_map, b_map[at], ((1,), (1,)))
        order = lax.broadcasted_iota(jnp.int32, (T, LANES), 0) >= (
            lax.broadcasted_iota(jnp.int32, (T, LANES), 1) + s * LANES
        )
        same = jnp.logical_and(order, doc_col == doc_row[:, at])
        scores[:, at] = jnp.where(same, g, 0.0)

    def chunk(j, carry):
        at = pl.ds(pl.multiple_of(j * LANES, LANES), LANES)
        reach[:, at] = dot(efac[...], head_pick(j, LANES))
        return carry

    lax.fori_loop(0, XCHUNKS, chunk, 0)


def late_kernel(act, cum, step, scores, fac, gate, sfac, local, sgate):
    def pair(j, carry):
        at = pl.ds(pl.multiple_of(j * LANES, LANES), LANES)
        local[:, at] = pair_chunk(j, act, cum, step, scores, fac, sfac)
        return carry

    lax.fori_loop(0, XCHUNKS, pair, 0)

    def gates(j, carry):
        at = pl.ds(pl.multiple_of(j * 2 * LANES, 2 * LANES), 2 * LANES)
        sgate[:, at] = silu(gate[:, at].astype(F32))
        return carry

    lax.fori_loop(0, XCHUNKS // 2, gates, 0)


def back_kernel(local, reach, sgate, act, one, two, gain, normed, give, m0, m1, m2, m3, gated, squares, turned, flat, sem):
    c_map = act[:, INNER + N :]
    wide = 2 * LANES

    def first(j):
        at = pl.ds(pl.multiple_of(j * wide, wide), wide)
        info = one[N:, at].astype(F32)
        other = two[N:, at].astype(F32)
        linked = (info[2:3] == other[2:3]).astype(F32)
        weight = (info[0:1] + info[1:2]) * linked
        state = one[0:N, at].astype(F32) + weight * two[0:N, at].astype(F32)
        reading = dot(c_map, state.astype(BF16))
        mixed = local[:, at] + reading * reach[:, at]
        value = mixed.astype(BF16).astype(F32) * sgate[:, at]
        gated[:, at] = value
        value = value * value
        return value[:, 0:LANES] + value[:, LANES:]

    def first_group(i, carry):
        parts = first(10 * i)
        for k in range(1, 10):
            parts = parts + first(10 * i + k)
        squares[...] += parts
        return carry

    squares[...] = jnp.zeros_like(squares)
    lax.fori_loop(0, 1, first_group, 0)
    mean = jnp.sum(squares[...], axis=1, keepdims=True) * (1.0 / INNER)
    squares[...] = jnp.broadcast_to(lax.rsqrt(mean + 1e-05), squares.shape)
    eye = (
        lax.broadcasted_iota(jnp.int32, (LANES, LANES), 0) == lax.broadcasted_iota(jnp.int32, (LANES, LANES), 1)
    ).astype(BF16)

    def second(i, carry):
        for k in range(20):
            at = pl.ds(pl.multiple_of((20 * i + k) * LANES, LANES), LANES)
            value = (gated[:, at] * squares[...] * gain[at].reshape(1, LANES)).astype(BF16)
            flat[:, at] = value
            turned[at, :] = dot(eye, value, ((1,), (1,))).astype(BF16)
        return carry

    lax.fori_loop(0, 1, second, 0)
    out = pltpu.make_async_copy(flat, normed, sem)
    out.start()
    y, x, c = [lax.axis_index(a) for a in ("y", "x", "c")]

    def block(core, k, m):
        i = jnp.where(core == 0, lax.rem(y + k, 4), m)
        j = jnp.where(core == 0, m, lax.rem(x + k, 4))
        return turned[pl.ds(pl.multiple_of(80 * (2 * (4 * i + j) + core), 16), 80), :]

    for k, mine in enumerate((m0, m1, m2, m3)):
        for m in range(4):
            give[k, m] = block(1 - c, k, m)
            mine[m] = block(c, k, m)
    out.wait()


def stack_kernel(one, two, after, out):
    del after
    out[0] = one[...]
    out[1] = two[...]


def load_kernel(got, *rest):
    for k, out in enumerate(rest[-3:]):
        out[...] = got[k + 1]


def grad_kernel(m0, got, m1, m2, m3, r1, r2, r3, c0, c1, c2, c3, out, flat):
    left = [m0[...].reshape(320, T), got[0].reshape(320, T)]
    right = [c0[0], c0[1]]
    for m, r, c in ((m1, r1, c1), (m2, r2, c2), (m3, r3, c3)):
        left += [m[...].reshape(320, T), r[...].reshape(320, T)]
        right += [c[0], c[1]]
    for n in range(5):
        at = slice(256 * n, 256 * n + 256)
        total = dot(left[0], right[0][:, at])
        for k in range(1, 8):
            total = total + dot(left[k], right[k][:, at])
        for k in range(2):
            row = 20 * (2 * n + k)
            for i in range(16):
                flat[i, row : row + 20, :] = total[20 * i : 20 * i + 20, k * LANES : k * LANES + LANES]
    for i in range(16):
        out[i] = flat[i].astype(BF16)


def sum_kernel(pieces, out, flat):
    total = pieces[0].astype(F32)
    for i in range(1, 16):
        total = total + pieces[i].astype(F32)
    flat[...] = total
    for k in range(10):
        out[:, k * LANES : k * LANES + LANES] = flat[20 * k : 20 * k + 20, :]


def call(kernel, name, out, scratch, limit, flops=0, moved=0, special=0, **kw):
    return pl.pallas_call(
        kernel,
        name=name,
        out_shape=out,
        scratch_shapes=scratch,
        compiler_params=pltpu.CompilerParams(vmem_limit_bytes=limit << 20),
        cost_estimate=pl.CostEstimate(flops=flops, bytes_accessed=moved, transcendentals=special),
        **kw,
    )


def shape(dims, kind=F32):
    return jax.ShapeDtypeStruct(dims, kind)


def shifted(value, by):
    return lax.ppermute(value, "z", [(i, (i + by) % 4) for i in range(4 if by == 1 else 4 - by)])


def around(value, by, first_axis):
    pairs = []
    for y in range(4):
        for x in range(4):
            for c in range(2):
                along_y = (c == 0) == (first_axis == "y")
                to_y, to_x = ((y + by) % 4, x) if along_y else (y, (x + by) % 4)
                pairs.append(((y * 4 + x) * 2 + c, (to_y * 4 + to_x) * 2 + c))
    return lax.ppermute(value, ("y", "x", "c"), pairs)


def place_of(y, x, c, z):
    return ((y * 4 + x) * 2 + c) * 4 + z


PLANES = [[place_of(y, k, 0, z) for k in range(4) for z in range(4)] for y in range(4)] + [
    [place_of(k, x, 1, z) for k in range(4) for z in range(4)] for x in range(4)
]


def swapped(value):
    return lax.ppermute(value, "c", [(0, 1), (1, 0)])


def whole(dims):
    return pl.BlockSpec(dims, lambda i: (0,) * len(dims))


def per_device(conv_input, gate_input, step_input, step_bias, log_rates, skip_gain, conv_weight, conv_bias, norm_gain, doc_ids, cotangent):
    conv = conv_input[0]
    vmem = pl.BlockSpec(memory_space=VMEM)
    anywhere = pl.BlockSpec(memory_space=pl.ANY)
    halo = call(
        edge_kernel,
        "edge",
        shape((8, C_ALL + LANES), BF16),
        [VMEM((16, C_ALL), BF16), VMEM((1, T), jnp.int32), pltpu.SemaphoreType.DMA((2,))],
        63,
        moved=10**5,
        in_specs=[anywhere] * 2,
    )(conv, doc_ids)
    halo = shifted(halo, 1)
    step_in, bias, rates = step_input[0], step_bias[None], log_rates[None]
    cot_other = swapped(cotangent[0])
    cum, step, masks, spread = call(
        prep_kernel,
        "prep",
        (shape((H, T)), shape((H, T)), shape((3, T, LANES)), shape((T + LANES, LANES), BF16)),
        [VMEM((T + 8, LANES), F32)],
        4,
        flops=10**9,
        moved=10**7,
        special=10**5,
    )(step_in, bias, rates, doc_ids)
    act, state, info, top = call(
        front_kernel,
        "front",
        (shape((T, C_ALL), BF16), shape((N, INNER)), shape((16, INNER), BF16), shape((16, INNER))),
        [VMEM((5, T + 8, LANES), F32), VMEM((T, INNER), BF16)],
        8,
        flops=10**9,
        moved=4 * 10**6,
        special=10**6,
    )(conv, conv_weight, conv_bias, doc_ids, masks, spread)
    act, msg = call(
        fix_kernel,
        "fix",
        (shape((T, C_ALL), BF16), shape((MSG, INNER), BF16)),
        [],
        8,
        moved=2 * 10**6,
        grid=(1,),
        in_specs=[
            whole((8, C_ALL + LANES)),
            whole((16, C_ALL)),
            whole((4, C_ALL)),
            whole((C_ALL,)),
            whole((1, T)),
            whole((16, C_ALL)),
            whole((N, INNER)),
            whole((16, INNER)),
            whole((16, INNER)),
        ],
        out_specs=(whole((16, C_ALL)), whole((MSG, INNER))),
        input_output_aliases={5: 0},
    )(halo, conv, conv_weight, conv_bias, doc_ids, act, state, info, top)
    one = shifted(msg, 1)
    two = shifted(msg, 2)
    reach, scores, fac, sfac = call(
        early_kernel,
        "early",
        (
            shape((T, INNER)),
            shape((T, T)),
            shape((T, LANES), BF16),
            shape((16, LANES), BF16),
        ),
        [VMEM((T, LANES), BF16)],
        8,
    )(act, cum, doc_ids, halo, skip_gain[None])
    cots = call(
        stack_kernel, "stack", shape((2, T, D), BF16), [], 4, in_specs=[vmem] * 2 + [anywhere]
    )(cotangent[0], cot_other, act)
    c1, c2, c3 = [around(cots, k, "y") for k in (1, 2, 3)]
    local, sgate = call(
        late_kernel, "late", (shape((T, INNER)), shape((T, INNER))), [], 8
    )(act, cum, step, scores, fac, gate_input[0], sfac)
    block = (4, 4, 80, T)
    normed, give, m0, *mine = call(
        back_kernel,
        "back",
        (shape((T, INNER), BF16), shape(block, BF16)) + (shape(block[1:], BF16),) * 4,
        [
            VMEM((T, INNER), F32),
            VMEM((T, LANES), F32),
            VMEM((INNER, T), BF16),
            VMEM((T, INNER), BF16),
            pltpu.SemaphoreType.DMA,
        ],
        12,
        out_specs=(pl.BlockSpec(memory_space=pltpu.HBM),) + (vmem,) * 5,
    )(local, reach, sgate, act, one, two, norm_gain)
    got = swapped(give)
    mine = [around(v, k + 1, "y") for k, v in enumerate(mine)]
    sends = call(
        load_kernel, "load", (shape(block[1:], BF16),) * 3, [], 4, in_specs=[vmem] + [anywhere] * 3
    )(got, c1, c2, c3)
    got_far = [around(v, k + 1, "y") for k, v in enumerate(sends)]
    packed = call(
        grad_kernel,
        "grad",
        shape((16, 200, LANES), BF16),
        [VMEM((16, 200, LANES), F32)],
        10,
        flops=2 * 10**9,
        moved=8 * 10**6,
    )(m0, got, *mine, *got_far, cots, c1, c2, c3)
    pieces = lax.all_to_all(packed, ("y", "x", "c", "z"), 0, 0, axis_index_groups=PLANES)
    grad = call(sum_kernel, "total", shape((20, D)), [VMEM((200, LANES), F32)], 8, moved=10**6)(pieces)
    return (normed[None], grad)


def solution(mesh):
    fine = Mesh(mesh.devices.reshape(4, 4, 2, 4), ("y", "x", "c", "z"))
    dp = ("y", "x", "c")
    in_specs = (
        P(dp, "z", None),
        P(dp, "z", None),
        P(dp, None, "z"),
        P(),
        P(),
        P(),
        P(),
        P(),
        P(),
        P(dp, "z"),
        P(dp, "z", None),
    )
    out_specs = (P(dp, "z", None), P(dp + ("z",), None))
    return jax.shard_map(per_device, mesh=fine, in_specs=in_specs, out_specs=out_specs, check_vma=False)
```
